32 devices in a mesh: sky: 4 (over z), tm: 8 (over y, x, core).
Axes of the slice: x: 2, y: 2, z: 4, core: 2. Of those that a mesh axis runs over, the one named last changes fastest.
Arguments:
- tiles: float32 [512, 128, 256], P(('sky', 'tm')), may hold values from -0.375 to 0.375
- tile_seg: int32 [512], P(('sky', 'tm')), may hold values from 0 to 127, as said below
- tile_count: int32 [512], P(('sky', 'tm')), may hold values from 32 to 128
- src_index: int32 [512, 128], P(('sky', 'tm')), may hold values from 0 to 32767, as said below
- src_coef: float32 [5, 512, 128], P(None, ('sky', 'tm')), may hold values from -6 to 6
- obs_weight: float32 [512, 128], P(('sky', 'tm')), may hold values from 0.2 to 5
- att_dir: float32 [128, 256], P('tm'), may hold values from -6 to 6
- src_dir: float32 [5, 131072], P(None, ('sky', 'tm')), may hold values from -6 to 6
Outputs:
- projected: float32 [512, 128], P(('sky', 'tm'))
- att_normal: float32 [128, 256], P('tm')
- src_normal: float32 [5, 131072], P(None, ('sky', 'tm'))
- curvature: float32 [], replicated
The draws below stay inside these ranges and needn't reach their ends.
Inputs may be any that keep to these rules, and one draw needn't show every extreme that they name: `tile_seg`: within each aligned block of 16 tiles, at most 4 tiles name segments s with s // 16 equal to any one value; every block reaches 4 for some value. `src_index`: within each aligned block of 16 tiles, at most 512 observations name sources i with i // 4096 equal to any one value; every block reaches 512 for some value.
All inputs are finite; a program needn't handle non-finite values.
Results may differ from the reference program's by a relative error of at most 0.00011.
Values sent between devices are 32-bit elements; how exact they have to be, the bound alone decides.
No kernel may reach another device: no remote copies, remote signals or barrier semaphores. Data moves between devices by JAX's collectives and lax.ppermute only.
A program may use at most 192 MiB of HBM per device.

```python
import math
import jax
import jax.numpy as jnp
from jax import lax

ROWS = 128
COLS = 256
PARAMS = 5
TILES_DEV = 16
SEG_DEV = 16
SRC_DEV = 4096
TILES = 512
SEGMENTS = 128
SRC_G = 32768
SOURCES = 131072
CAP_T = 4
CAP_S = 512
N_SKY = 4
N_TM = 8


def owner_block(key, full, count, n_owner, cap):
    rest = count - cap
    slots = jax.random.permutation(key, (n_owner - 1) * cap)[:rest]
    other = (slots // cap).astype(jnp.int32)
    other = other + (other >= full).astype(jnp.int32)
    owners = jnp.concatenate([jnp.full((cap,), full, dtype=jnp.int32), other])
    order = jax.random.permutation(jax.random.fold_in(key, 7), count)
    return owners[order]


def block_owners(key, salt, count, cap):
    blocks = N_SKY * N_TM
    block_ids = jnp.arange(blocks, dtype=jnp.int32)

    def one_block(block):
        sky = block // N_TM
        full = jax.random.randint(jax.random.fold_in(jax.random.fold_in(key, salt + 1), sky), (), 0, N_TM).astype(jnp.int32)
        inner = jax.random.fold_in(jax.random.fold_in(key, salt), block)
        return owner_block(inner, full, count, N_TM, cap)
    return jax.vmap(one_block)(block_ids)


def draw_tile_seg(key, part):
    owners = block_owners(key, 100, TILES_DEV, CAP_T)
    first = jax.random.randint(jax.random.fold_in(key, 200), owners.shape, 0, SEG_DEV)
    second = jax.random.randint(jax.random.fold_in(key, 201), owners.shape, 0, SEG_DEV)
    local = jnp.minimum(first, second).astype(jnp.int32)
    return (owners * SEG_DEV + local).reshape(TILES).astype(jnp.int32)


def draw_src_index(key, part):
    owners = block_owners(key, 300, TILES_DEV * ROWS, CAP_S)
    local = jax.random.randint(jax.random.fold_in(key, 400), owners.shape, 0, SRC_DEV).astype(jnp.int32)
    return (owners * SRC_DEV + local).reshape(TILES, ROWS).astype(jnp.int32)


def plant(result, stream_key, least, top_value):
    longest = result.shape.index(max(result.shape))
    spots = []
    for shift in (0, 1):
        where = [jax.random.randint(jax.random.fold_in(stream_key, axis), (), 0, length) for axis, length in enumerate(result.shape)]
        where[longest] = (where[longest] + shift) % result.shape[longest]
        spots.append(tuple(where))
    return result.at[spots[0]].set(least).at[spots[1]].set(top_value)


def steps_of(own_key, extent, pieces, low, top_value):
    gain, own = 1.0, jax.random.fold_in(own_key, 6)
    for dim, parts in pieces:
        draws = jnp.exp(jax.random.uniform(jax.random.fold_in(own, dim), (parts,), jnp.float32, low / len(pieces), top_value / len(pieces)))
        gain = gain * jnp.repeat(draws, extent[dim] // parts).reshape([-1 if axis == dim else 1 for axis in range(len(extent))])
    return gain


def gaussian(key, dims, width, bound, split=(), kind=jnp.bfloat16):
    factor_of = steps_of(key, dims, split, -0.22, 0.18) if split else 1.0
    entries = jax.random.normal(key, dims, jnp.float32) * width * factor_of
    return jnp.minimum(jnp.maximum(entries, -bound), bound).astype(kind)


def setup_inputs(seed: int = 0) -> dict:
    splits = jax.random.split(jax.random.key(seed), 9)
    tiles = gaussian(splits[0], (TILES, ROWS, COLS), COLS ** -0.5, 0.375, ((0, 32),), jnp.float32)
    tile_seg = draw_tile_seg(jax.random.fold_in(splits[8], 71), 0)
    tile_count = plant(jax.random.randint(splits[2], (TILES,), ROWS // 4, ROWS + 1), jax.random.fold_in(splits[2], 1), ROWS // 4, ROWS).astype(jnp.int32)
    src_index = draw_src_index(jax.random.fold_in(splits[8], 71), 0)
    src_coef = gaussian(splits[4], (PARAMS, TILES, ROWS), 1.0, 6.0, ((1, 32),), jnp.float32)
    obs_weight = jnp.clip(jnp.exp(math.log(5.0) - 3.218876 * jax.random.uniform(splits[5], (TILES, ROWS), jnp.float32) ** steps_of(splits[5], (TILES, ROWS), ((0, 32),), -0.2, 0.2)), 0.2, 5.0)
    att_dir = gaussian(splits[6], (SEGMENTS, COLS), 1.0, 6.0, ((0, 8),), jnp.float32)
    src_dir = gaussian(splits[7], (PARAMS, SOURCES), 1.0, 6.0, ((1, 32),), jnp.float32)
    return dict(tiles=tiles, tile_seg=tile_seg, tile_count=tile_count, src_index=src_index, src_coef=src_coef, obs_weight=obs_weight, att_dir=att_dir, src_dir=src_dir)


def reference(tiles, tile_seg, tile_count, src_index, src_coef, obs_weight, att_dir, src_dir):
    row_ids = jnp.arange(ROWS, dtype=jnp.int32)
    live_rows = row_ids[None, :] < tile_count[:, None]
    seg_rows = att_dir[tile_seg]
    att_part = jnp.einsum('tjc,tc->tj', tiles, seg_rows, precision=lax.Precision.HIGHEST)
    sky_group = (jnp.arange(TILES, dtype=jnp.int32) // (TILES_DEV * N_TM)).astype(jnp.int32)
    src_column = sky_group[:, None] * SRC_G + src_index
    picked = src_dir[:, src_column]
    projected = jnp.where(live_rows, att_part + jnp.sum(src_coef * picked, axis=0), jnp.zeros_like(att_part))
    weighted = obs_weight * projected
    curvature = jnp.sum(projected * weighted)
    tile_grad = jnp.einsum('tjc,tj->tc', tiles, weighted, precision=lax.Precision.HIGHEST)
    att_normal = jax.ops.segment_sum(tile_grad, tile_seg, num_segments=SEGMENTS)
    terms = (src_coef * weighted[None]).reshape(PARAMS, -1).T
    src_normal = jax.ops.segment_sum(terms, src_column.reshape(-1), num_segments=SOURCES).T
    return (projected, att_normal, src_normal, curvature)
```

```python
import functools

import jax
import jax.numpy as jnp
from jax import lax
from jax.experimental import pallas as pl
from jax.experimental.pallas import tpu as pltpu
from jax.sharding import PartitionSpec as P

LANES = 128
SLOTS = 8
WIDE = 256
NT = (((1,), (1,)), ((), ()))
F32 = jnp.float32
BF16 = jnp.bfloat16
VMEM = pl.BlockSpec(memory_space=pltpu.VMEM)
SMEM = pl.BlockSpec(memory_space=pltpu.SMEM)
PARAMS = pltpu.CompilerParams(vmem_limit_bytes=16 * 1024 * 1024)


def halves(x):
    high = x.astype(BF16)
    return high, (x - high.astype(F32)).astype(BF16)


def rows_of(values, shape):
    ids = lax.broadcasted_iota(jnp.int32, shape, 0)
    out = jnp.zeros(shape, jnp.int32)
    for t, value in enumerate(values):
        out = jnp.where(ids == t, value, out)
    return out


def project_kernel(seg, count, table, tiles, index, coef, weight, projected, sent):
    params, tile_total, width = coef.shape
    cols = tiles.shape[2]
    owners, _, span = table.shape
    seg_rows = span // cols
    blocks = span // LANES
    ids = index[...]
    lane = lax.rem(ids, LANES)
    block = lax.div(ids, LANES)

    def take(owner, picked):
        picked = list(picked)
        for b in range(blocks):
            hit = block == owner * blocks + b
            for k in range(params):
                row = table[owner, k : k + 1, b * LANES : (b + 1) * LANES]
                found = jnp.take_along_axis(jnp.broadcast_to(row, ids.shape), lane, axis=1)
                picked[k] = jnp.where(hit, found, picked[k])
        return tuple(picked)

    picked = lax.fori_loop(0, owners, take, tuple(jnp.zeros(ids.shape, F32) for _ in range(params)))
    row_ids = lax.broadcasted_iota(jnp.int32, ids.shape, 0)
    total = jnp.zeros(ids.shape, F32)
    for t in range(tile_total):
        s = seg[t]
        start = pl.multiple_of(lax.rem(s, seg_rows) * cols, cols)
        direction = table[lax.div(s, seg_rows), params : params + 1, pl.ds(start, cols)]
        product = tiles[t] * direction
        folded = product[:, :LANES]
        for c in range(1, cols // LANES):
            folded = folded + product[:, c * LANES : (c + 1) * LANES]
        ones = jnp.where(row_ids == t, 1.0, 0.0).astype(BF16)
        for part in halves(folded):
            total = total + lax.dot_general(ones, part, NT, preferred_element_type=F32)
    for k in range(params):
        total = total + coef[k] * picked[k]
    live = lax.broadcasted_iota(jnp.int32, ids.shape, 1) < rows_of(
        [count[t] for t in range(tile_total)], ids.shape
    )
    value = jnp.where(live, total, 0.0)
    weighted = weight[...] * value
    projected[...] = value
    for k in range(params):
        sent[pl.ds(k, tile_total, stride=SLOTS), :] = coef[k] * weighted
    sent[pl.ds(params, tile_total, stride=SLOTS), :] = ids.astype(F32)
    names = rows_of([seg[t] for t in range(tile_total)], ids.shape)
    sent[pl.ds(params + 1, tile_total, stride=SLOTS), :] = names.astype(F32)
    sent[pl.ds(params + 2, tile_total, stride=SLOTS), :] = value * weighted
    columns = weighted.T
    base = tile_total * SLOTS
    for t in range(tile_total):
        grad = jnp.sum(tiles[t] * columns[:, t : t + 1], axis=0, keepdims=True)
        for c in range(cols // LANES):
            sent[pl.ds(base + c * tile_total + t, 1), :] = grad[:, c * LANES : (c + 1) * LANES]


def attitude_kernel(me, got, part, *, params, tile_total, seg_rows, folds):
    owners = got.shape[0]
    lane = lax.broadcasted_iota(jnp.int32, (tile_total, LANES), 1)
    first = me[0] * seg_rows
    base = tile_total * SLOTS
    group = LANES // tile_total
    sums = [jnp.zeros((seg_rows, LANES), F32) for _ in range(folds)]
    curve = jnp.zeros((tile_total, LANES), F32)
    for g in range(0, owners, group):
        members = range(g, min(g + group, owners))
        hits = []
        for d in members:
            name = got[d, pl.ds(params + 1, tile_total, stride=SLOTS), :].astype(jnp.int32)
            hits.append(jnp.where(name - first == lane, 1.0, 0.0))
            curve = curve + got[d, pl.ds(params + 2, tile_total, stride=SLOTS), :]
        pick = jnp.concatenate(hits, axis=0).T[:seg_rows].astype(BF16)
        for c in range(folds):
            grads = jnp.concatenate(
                [got[d, pl.ds(base + c * tile_total, tile_total), :] for d in members], axis=0
            )
            for piece in halves(grads):
                sums[c] = sums[c] + jnp.dot(pick, piece, preferred_element_type=F32)
    for c in range(folds):
        part[pl.ds(c * seg_rows, seg_rows), :] = sums[c]
    whole = jnp.sum(jnp.sum(curve, axis=0, keepdims=True), axis=1, keepdims=True)
    part[pl.ds(folds * seg_rows, 8), :] = jnp.broadcast_to(whole, (8, LANES))


def source_kernel(me, got, out, left, right, acc, *, params, tile_total):
    owners = got.shape[0]
    span = out.shape[1]
    high_total = span // WIDE
    depth = params * high_total
    high_ids = lax.broadcasted_iota(jnp.int32, (high_total, LANES), 0)
    low_ids = lax.broadcasted_iota(jnp.int32, (WIDE, LANES), 0)
    acc[...] = jnp.zeros_like(acc)

    def add(d, carry):
        for t in range(tile_total):
            at = slice(t * LANES, (t + 1) * LANES)
            tile = got[d, t * SLOTS : (t + 1) * SLOTS, :]
            local = tile[params : params + 1].astype(jnp.int32) - me[0] * span
            high = lax.shift_right_arithmetic(local, 8)
            low = lax.bitwise_and(local, WIDE - 1)
            right[:, at] = jnp.where(low_ids == low, 1.0, 0.0).astype(BF16)
            hit = high_ids == high
            for k in range(params):
                for p, piece in enumerate(halves(tile[k : k + 1])):
                    row = p * depth + k * high_total
                    left[row : row + high_total, at] = jnp.where(hit, piece.astype(F32), 0.0).astype(BF16)
        acc[...] += lax.dot_general(left[...], right[...], NT, preferred_element_type=F32)
        return carry

    lax.fori_loop(0, owners, add, 0)
    for k in range(params):
        for h in range(high_total):
            row = k * high_total + h
            out[k : k + 1, h * WIDE : (h + 1) * WIDE] = acc[row : row + 1, :] + acc[depth + row : depth + row + 1, :]


def finish_kernel(*refs, seg_rows, folds):
    *parts, normal, curvature = refs
    total = parts[0][...]
    for part in parts[1:]:
        total = total + part[...]
    for c in range(folds):
        normal[:, c * LANES : (c + 1) * LANES] = total[c * seg_rows : (c + 1) * seg_rows]
    curvature[0, 0] = total[folds * seg_rows, 0]


def per_device(tiles, tile_seg, tile_count, src_index, src_coef, obs_weight, att_dir, src_dir, *, sky):
    tile_total, row_count, cols = tiles.shape
    params, span = src_dir.shape
    seg_rows = att_dir.shape[0]
    folds = cols // LANES
    me = lax.axis_index("tm").astype(jnp.int32).reshape(1)
    directions = jnp.concatenate([src_dir, att_dir.reshape(-1, span)], axis=0)
    table = lax.all_gather(directions, "tm", axis=0, tiled=False)
    projected, sent = pl.pallas_call(
        project_kernel,
        out_shape=(
            jax.ShapeDtypeStruct((tile_total, row_count), F32),
            jax.ShapeDtypeStruct((tile_total * (SLOTS + folds), LANES), F32),
        ),
        in_specs=[SMEM, SMEM] + [VMEM] * 5,
        out_specs=(VMEM, VMEM),
        compiler_params=PARAMS,
        name="project",
    )(tile_seg, tile_count, table, tiles, src_index, src_coef, obs_weight)
    got = lax.all_gather(sent, "tm", axis=0, tiled=False)
    part = pl.pallas_call(
        functools.partial(
            attitude_kernel, params=params, tile_total=tile_total, seg_rows=seg_rows, folds=folds
        ),
        out_shape=jax.ShapeDtypeStruct((folds * seg_rows + 8, LANES), F32),
        in_specs=[SMEM, VMEM],
        out_specs=VMEM,
        compiler_params=PARAMS,
        name="attitude",
    )(me, got)
    others = [
        lax.ppermute(part, "sky", [(i, (i + k) % sky) for i in range(sky)]) for k in range(1, sky)
    ]
    depth = params * (span // WIDE)
    src_normal = pl.pallas_call(
        functools.partial(source_kernel, params=params, tile_total=tile_total),
        out_shape=jax.ShapeDtypeStruct((params, span), F32),
        in_specs=[SMEM, VMEM],
        out_specs=VMEM,
        scratch_shapes=[
            pltpu.VMEM((2 * depth, tile_total * LANES), BF16),
            pltpu.VMEM((WIDE, tile_total * LANES), BF16),
            pltpu.VMEM((2 * depth, WIDE), F32),
        ],
        compiler_params=PARAMS,
        cost_estimate=pl.CostEstimate(flops=2_000_000_000, bytes_accessed=1_000_000, transcendentals=0),
        name="source",
    )(me, got)
    att_normal, curvature = pl.pallas_call(
        functools.partial(finish_kernel, seg_rows=seg_rows, folds=folds),
        out_shape=(
            jax.ShapeDtypeStruct((seg_rows, cols), F32),
            jax.ShapeDtypeStruct((1, 1), F32),
        ),
        in_specs=[VMEM] * sky,
        out_specs=(VMEM, SMEM),
        compiler_params=PARAMS,
        name="finish",
    )(part, *others)
    return projected, att_normal, src_normal, curvature.reshape(())


def solution(mesh):
    placed = (
        P(("sky", "tm"), None, None),
        P(("sky", "tm")),
        P(("sky", "tm")),
        P(("sky", "tm"), None),
        P(None, ("sky", "tm"), None),
        P(("sky", "tm"), None),
        P("tm", None),
        P(None, ("sky", "tm")),
    )
    return jax.shard_map(
        functools.partial(per_device, sky=mesh.shape["sky"]),
        mesh=mesh,
        in_specs=placed,
        out_specs=(P(("sky", "tm"), None), P("tm", None), P(None, ("sky", "tm")), P()),
        check_vma=False,
    )
```

```python
import functools

import jax
import jax.numpy as jnp
from jax import lax
from jax.experimental import pallas as pl
from jax.experimental.pallas import tpu as pltpu
from jax.sharding import PartitionSpec as P

LANES = 128
SLOTS = 8
WIDE = 256
NT = (((1,), (1,)), ((), ()))
F32 = jnp.float32
BF16 = jnp.bfloat16
VMEM = pl.BlockSpec(memory_space=pltpu.VMEM)
HBM = pl.BlockSpec(memory_space=pltpu.HBM)
SMEM = pl.BlockSpec(memory_space=pltpu.SMEM)
PARAMS = pltpu.CompilerParams(vmem_limit_bytes=16 * 1024 * 1024)


def in_hbm(x):
    return pltpu.with_memory_space_constraint(x, pltpu.HBM)


def halves(x):
    high = x.astype(BF16)
    return high, (x - high.astype(F32)).astype(BF16)


def rows_of(values, shape):
    ids = lax.broadcasted_iota(jnp.int32, shape, 0)
    out = jnp.zeros(shape, jnp.int32)
    for t, value in enumerate(values):
        out = jnp.where(ids == t, value, out)
    return out


def pack_kernel(source, attitude, index, coef, weight, directions, index_out, coef_out, weight_out, held, sems):
    params, span = source.shape
    seg_rows, cols = attitude.shape
    copies = [
        pltpu.make_async_copy(source, held, sems.at[0]),
        pltpu.make_async_copy(index, index_out, sems.at[2]),
        pltpu.make_async_copy(coef, coef_out, sems.at[3]),
        pltpu.make_async_copy(weight, weight_out, sems.at[4]),
    ]
    base = params * (span // LANES)
    for c in range(cols // LANES):
        copies.append(
            pltpu.make_async_copy(
                attitude.at[:, pl.ds(c * LANES, LANES)],
                directions.at[pl.ds(base + c * seg_rows, seg_rows), :],
                sems.at[5 + c],
            )
        )
    for copy in copies:
        copy.start()
    copies[0].wait()
    for b in range(span // LANES):
        directions[b * params : (b + 1) * params, :] = held[:, b * LANES : (b + 1) * LANES]
    for copy in copies[1:]:
        copy.wait()


def project_kernel(seg_in, count_in, tiles_in, table, index, coef, weight, projected, sent, seg, count, tiles, sems, *, seg_rows):
    params, tile_total, width = coef.shape
    cols = tiles.shape[2]
    folds = cols // LANES
    owners = table.shape[0]
    base = table.shape[1] - folds * seg_rows
    blocks = base // params
    copies = [
        pltpu.make_async_copy(seg_in, seg, sems.at[0]),
        pltpu.make_async_copy(count_in, count, sems.at[1]),
        pltpu.make_async_copy(tiles_in, tiles, sems.at[2]),
    ]
    for copy in copies:
        copy.start()
    ids = index[...]
    lane = lax.rem(ids, LANES)
    block = lax.div(ids, LANES)

    def take(owner, picked):
        picked = list(picked)
        for b in range(blocks):
            hit = block == owner * blocks + b
            for k in range(params):
                row = table[owner, pl.ds(b * params + k, 1), :]
                found = jnp.take_along_axis(jnp.broadcast_to(row, ids.shape), lane, axis=1)
                picked[k] = jnp.where(hit, found, picked[k])
        return tuple(picked)

    picked = lax.fori_loop(0, owners, take, tuple(jnp.zeros(ids.shape, F32) for _ in range(params)))
    for copy in copies:
        copy.wait()
    row_ids = lax.broadcasted_iota(jnp.int32, ids.shape, 0)
    total = jnp.zeros(ids.shape, F32)
    for t in range(tile_total):
        s = seg[t]
        owner, local = lax.div(s, seg_rows), lax.rem(s, seg_rows)
        folded = None
        for c in range(folds):
            direction = table[owner, pl.ds(base + c * seg_rows + local, 1), :]
            product = tiles[t, :, c * LANES : (c + 1) * LANES] * direction
            folded = product if folded is None else folded + product
        ones = jnp.where(row_ids == t, 1.0, 0.0).astype(BF16)
        for part in halves(folded):
            total = total + lax.dot_general(ones, part, NT, preferred_element_type=F32)
    for k in range(params):
        total = total + coef[k] * picked[k]
    live = lax.broadcasted_iota(jnp.int32, ids.shape, 1) < rows_of(
        [count[t] for t in range(tile_total)], ids.shape
    )
    value = jnp.where(live, total, 0.0)
    weighted = weight[...] * value
    projected[...] = value
    for k in range(params):
        sent[pl.ds(k, tile_total, stride=SLOTS), :] = coef[k] * weighted
    sent[pl.ds(params, tile_total, stride=SLOTS), :] = ids.astype(F32)
    names = rows_of([seg[t] for t in range(tile_total)], ids.shape)
    sent[pl.ds(params + 1, tile_total, stride=SLOTS), :] = names.astype(F32)
    sent[pl.ds(params + 2, tile_total, stride=SLOTS), :] = value * weighted
    columns = weighted.T
    base = tile_total * SLOTS
    for t in range(tile_total):
        grad = jnp.sum(tiles[t] * columns[:, t : t + 1], axis=0, keepdims=True)
        for c in range(folds):
            sent[pl.ds(base + c * tile_total + t, 1), :] = grad[:, c * LANES : (c + 1) * LANES]


def attitude_kernel(me, got, part, *, params, tile_total, seg_rows, folds):
    owners = got.shape[0]
    lane = lax.broadcasted_iota(jnp.int32, (tile_total, LANES), 1)
    first = me[0] * seg_rows
    base = tile_total * SLOTS
    group = LANES // tile_total
    sums = [jnp.zeros((seg_rows, LANES), F32) for _ in range(folds)]
    curve = jnp.zeros((tile_total, LANES), F32)
    for g in range(0, owners, group):
        members = range(g, min(g + group, owners))
        hits = []
        for d in members:
            name = got[d, pl.ds(params + 1, tile_total, stride=SLOTS), :].astype(jnp.int32)
            hits.append(jnp.where(name - first == lane, 1.0, 0.0))
            curve = curve + got[d, pl.ds(params + 2, tile_total, stride=SLOTS), :]
        pick = jnp.concatenate(hits, axis=0).T[:seg_rows].astype(BF16)
        for c in range(folds):
            grads = jnp.concatenate(
                [got[d, pl.ds(base + c * tile_total, tile_total), :] for d in members], axis=0
            )
            for piece in halves(grads):
                sums[c] = sums[c] + jnp.dot(pick, piece, preferred_element_type=F32)
    for c in range(folds):
        part[pl.ds(c * seg_rows, seg_rows), :] = sums[c]
    whole = jnp.sum(jnp.sum(curve, axis=0, keepdims=True), axis=1, keepdims=True)
    part[pl.ds(folds * seg_rows, 8), :] = jnp.broadcast_to(whole, (8, LANES))


def source_kernel(me, got, out, left, right, acc, *, params, tile_total):
    owners = got.shape[0]
    span = out.shape[1]
    high_total = span // WIDE
    depth = params * high_total
    high_ids = lax.broadcasted_iota(jnp.int32, (high_total, LANES), 0)
    low_ids = lax.broadcasted_iota(jnp.int32, (WIDE, LANES), 0)
    acc[...] = jnp.zeros_like(acc)

    def add(d, carry):
        for t in range(tile_total):
            at = slice(t * LANES, (t + 1) * LANES)
            tile = got[d, t * SLOTS : (t + 1) * SLOTS, :]
            local = tile[params : params + 1].astype(jnp.int32) - me[0] * span
            high = lax.shift_right_arithmetic(local, 8)
            low = lax.bitwise_and(local, WIDE - 1)
            right[:, at] = jnp.where(low_ids == low, 1.0, 0.0).astype(BF16)
            hit = high_ids == high
            for k in range(params):
                for p, piece in enumerate(halves(tile[k : k + 1])):
                    row = p * depth + k * high_total
                    left[row : row + high_total, at] = jnp.where(hit, piece.astype(F32), 0.0).astype(BF16)
        acc[...] += lax.dot_general(left[...], right[...], NT, preferred_element_type=F32)
        return carry

    lax.fori_loop(0, owners, add, 0)
    for k in range(params):
        for h in range(high_total):
            row = k * high_total + h
            out[k : k + 1, h * WIDE : (h + 1) * WIDE] = acc[row : row + 1, :] + acc[depth + row : depth + row + 1, :]


def finish_kernel(*refs, seg_rows, folds):
    *parts, normal, curvature = refs
    total = parts[0][...]
    for part in parts[1:]:
        total = total + part[...]
    for c in range(folds):
        normal[:, c * LANES : (c + 1) * LANES] = total[c * seg_rows : (c + 1) * seg_rows]
    curvature[0, 0] = total[folds * seg_rows, 0]


def per_device(tiles, tile_seg, tile_count, src_index, src_coef, obs_weight, att_dir, src_dir, *, sky):
    tile_total, row_count, cols = tiles.shape
    params, span = src_dir.shape
    seg_rows = att_dir.shape[0]
    folds = cols // LANES
    me = lax.axis_index("tm").astype(jnp.int32).reshape(1)
    directions, index, coef, weight = pl.pallas_call(
        pack_kernel,
        out_shape=(
            jax.ShapeDtypeStruct((params * (span // LANES) + folds * seg_rows, LANES), F32),
            jax.ShapeDtypeStruct(src_index.shape, src_index.dtype),
            jax.ShapeDtypeStruct(src_coef.shape, F32),
            jax.ShapeDtypeStruct(obs_weight.shape, F32),
        ),
        in_specs=[HBM] * 5,
        out_specs=(VMEM,) * 4,
        scratch_shapes=[pltpu.VMEM((params, span), F32), pltpu.SemaphoreType.DMA((5 + folds,))],
        compiler_params=PARAMS,
        name="pack",
    )(*map(in_hbm, (src_dir, att_dir, src_index, src_coef, obs_weight)))
    table = lax.all_gather(directions, "tm", axis=0, tiled=False)
    projected, sent = pl.pallas_call(
        functools.partial(project_kernel, seg_rows=seg_rows),
        out_shape=(
            jax.ShapeDtypeStruct((tile_total, row_count), F32),
            jax.ShapeDtypeStruct((tile_total * (SLOTS + folds), LANES), F32),
        ),
        in_specs=[HBM] * 3 + [VMEM] * 4,
        out_specs=(VMEM, VMEM),
        scratch_shapes=[
            pltpu.SMEM(tile_seg.shape, jnp.int32),
            pltpu.SMEM(tile_count.shape, jnp.int32),
            pltpu.VMEM(tiles.shape, F32),
            pltpu.SemaphoreType.DMA((3,)),
        ],
        compiler_params=PARAMS,
        name="project",
    )(*map(in_hbm, (tile_seg, tile_count, tiles)), table, index, coef, weight)
    got = lax.all_gather(sent, "tm", axis=0, tiled=False)
    part = pl.pallas_call(
        functools.partial(
            attitude_kernel, params=params, tile_total=tile_total, seg_rows=seg_rows, folds=folds
        ),
        out_shape=jax.ShapeDtypeStruct((folds * seg_rows + 8, LANES), F32),
        in_specs=[SMEM, VMEM],
        out_specs=VMEM,
        compiler_params=PARAMS,
        name="attitude",
    )(me, got)
    others = [
        lax.ppermute(part, "sky", [(i, (i + k) % sky) for i in range(sky)]) for k in range(1, sky)
    ]
    depth = params * (span // WIDE)
    src_normal = pl.pallas_call(
        functools.partial(source_kernel, params=params, tile_total=tile_total),
        out_shape=jax.ShapeDtypeStruct((params, span), F32),
        in_specs=[SMEM, VMEM],
        out_specs=VMEM,
        scratch_shapes=[
            pltpu.VMEM((2 * depth, tile_total * LANES), BF16),
            pltpu.VMEM((WIDE, tile_total * LANES), BF16),
            pltpu.VMEM((2 * depth, WIDE), F32),
        ],
        compiler_params=PARAMS,
        cost_estimate=pl.CostEstimate(flops=2_000_000_000, bytes_accessed=1_000_000, transcendentals=0),
        name="source",
    )(me, got)
    att_normal, curvature = pl.pallas_call(
        functools.partial(finish_kernel, seg_rows=seg_rows, folds=folds),
        out_shape=(
            jax.ShapeDtypeStruct((seg_rows, cols), F32),
            jax.ShapeDtypeStruct((1, 1), F32),
        ),
        in_specs=[VMEM] * sky,
        out_specs=(VMEM, SMEM),
        compiler_params=PARAMS,
        name="finish",
    )(part, *others)
    return projected, att_normal, src_normal, curvature.reshape(())


def solution(mesh):
    placed = (
        P(("sky", "tm"), None, None),
        P(("sky", "tm")),
        P(("sky", "tm")),
        P(("sky", "tm"), None),
        P(None, ("sky", "tm"), None),
        P(("sky", "tm"), None),
        P("tm", None),
        P(None, ("sky", "tm")),
    )
    return jax.shard_map(
        functools.partial(per_device, sky=mesh.shape["sky"]),
        mesh=mesh,
        in_specs=placed,
        out_specs=(P(("sky", "tm"), None), P("tm", None), P(None, ("sky", "tm")), P()),
        check_vma=False,
    )
```

```python
import functools

import jax
import jax.numpy as jnp
from jax import lax
from jax.experimental import pallas as pl
from jax.experimental.pallas import tpu as pltpu
from jax.sharding import PartitionSpec as P

LANES = 128
SLOTS = 8
WIDE = 256
NT = (((1,), (1,)), ((), ()))
F32 = jnp.float32
BF16 = jnp.bfloat16
VMEM = pl.BlockSpec(memory_space=pltpu.VMEM)
HBM = pl.BlockSpec(memory_space=pltpu.HBM)
SMEM = pl.BlockSpec(memory_space=pltpu.SMEM)
PARAMS = pltpu.CompilerParams(vmem_limit_bytes=16 * 1024 * 1024)


def in_hbm(x):
    return pltpu.with_memory_space_constraint(x, pltpu.HBM)


def halves(x):
    high = x.astype(BF16)
    return high, (x - high.astype(F32)).astype(BF16)


def rows_of(values, shape):
    ids = lax.broadcasted_iota(jnp.int32, shape, 0)
    out = jnp.zeros(shape, jnp.int32)
    for t, value in enumerate(values):
        out = jnp.where(ids == t, value, out)
    return out


def pack_kernel(source, attitude, index, coef, weight, directions, index_out, coef_out, weight_out, held, sems):
    params, span = source.shape
    seg_rows, cols = attitude.shape
    copies = [
        pltpu.make_async_copy(source, held, sems.at[0]),
        pltpu.make_async_copy(index, index_out, sems.at[2]),
        pltpu.make_async_copy(coef, coef_out, sems.at[3]),
        pltpu.make_async_copy(weight, weight_out, sems.at[4]),
    ]
    base = params * (span // LANES)
    for c in range(cols // LANES):
        copies.append(
            pltpu.make_async_copy(
                attitude.at[:, pl.ds(c * LANES, LANES)],
                directions.at[pl.ds(base + c * seg_rows, seg_rows), :],
                sems.at[5 + c],
            )
        )
    for copy in copies:
        copy.start()
    copies[0].wait()
    for b in range(span // LANES):
        directions[b * params : (b + 1) * params, :] = held[:, b * LANES : (b + 1) * LANES]
    for copy in copies[1:]:
        copy.wait()


def gather(owner, table, ids, picked, params):
    blocks = (table.shape[0] // (params * 8)) * 8
    lane = lax.rem(ids, LANES)
    block = lax.div(ids, LANES) - owner * blocks

    def step(i, picked):
        picked = list(picked)
        for j in range(8):
            hit = block == i * 8 + j
            for k in range(params):
                row = table[pl.ds((i * 8 + j) * params + k, 1), :]
                found = jnp.take_along_axis(jnp.broadcast_to(row, ids.shape), lane, axis=1)
                picked[k] = jnp.where(hit, found, picked[k])
        return tuple(picked)

    return lax.fori_loop(0, blocks // 8, step, tuple(picked))


def pass_kernel(*refs, count):
    for q in range(count):
        refs[-1][q] = refs[q][...]


def pick_kernel(*refs, params, offsets, first):
    me, index, *refs = refs
    ids = index[...]
    rows = ids.shape[0]
    tables, refs = refs[: len(offsets)], refs[len(offsets) :]
    if first:
        tiles_in, out, tiles, sem = refs
        copy = pltpu.make_async_copy(tiles_in, tiles, sem)
        copy.start()
        picked = [jnp.zeros(ids.shape, F32) for _ in range(params)]
    else:
        before, out = refs
        picked = [before[k * rows : (k + 1) * rows, :] for k in range(params)]
    for offset, table in zip(offsets, tables):
        picked = gather(lax.bitwise_xor(me[0], offset), table, ids, picked, params)
    for k in range(params):
        out[k * rows : (k + 1) * rows, :] = picked[k]
    if first:
        copy.wait()


def project_kernel(*refs, seg_rows, offsets, late):
    me, seg_in, count_in, tiles, before, index, coef, weight, *refs = refs
    tables, refs = refs[: len(offsets)], refs[len(offsets) :]
    projected, sent, seg, count, lines, sems = refs
    params, tile_total, width = coef.shape
    folds = tiles.shape[2] // LANES
    base = tables[0].shape[0] - folds * seg_rows
    copies = [
        pltpu.make_async_copy(seg_in, seg, sems.at[0]),
        pltpu.make_async_copy(count_in, count, sems.at[1]),
    ]
    for copy in copies:
        copy.start()
    ids = index[...]
    picked = [before[k * tile_total : (k + 1) * tile_total, :] for k in range(params)]
    for offset, table in zip(offsets, tables):
        lines[offset] = table[base:, :]
        if offset in late:
            picked = gather(lax.bitwise_xor(me[0], offset), table, ids, picked, params)
    for copy in copies:
        copy.wait()
    row_ids = lax.broadcasted_iota(jnp.int32, ids.shape, 0)
    total = jnp.zeros(ids.shape, F32)
    for t in range(tile_total):
        s = seg[t]
        place, local = lax.bitwise_xor(lax.div(s, seg_rows), me[0]), lax.rem(s, seg_rows)
        folded = None
        for c in range(folds):
            direction = lines[place, pl.ds(c * seg_rows + local, 1), :]
            product = tiles[t, :, c * LANES : (c + 1) * LANES] * direction
            folded = product if folded is None else folded + product
        ones = jnp.where(row_ids == t, 1.0, 0.0).astype(BF16)
        for part in halves(folded):
            total = total + lax.dot_general(ones, part, NT, preferred_element_type=F32)
    for k in range(params):
        total = total + coef[k] * picked[k]
    live = lax.broadcasted_iota(jnp.int32, ids.shape, 1) < rows_of(
        [count[t] for t in range(tile_total)], ids.shape
    )
    value = jnp.where(live, total, 0.0)
    weighted = weight[...] * value
    projected[...] = value
    for k in range(params):
        sent[pl.ds(k, tile_total, stride=SLOTS), :] = coef[k] * weighted
    sent[pl.ds(params, tile_total, stride=SLOTS), :] = ids.astype(F32)
    names = rows_of([seg[t] for t in range(tile_total)], ids.shape)
    sent[pl.ds(params + 1, tile_total, stride=SLOTS), :] = names.astype(F32)
    sent[pl.ds(params + 2, tile_total, stride=SLOTS), :] = value * weighted
    columns = weighted.T
    base = tile_total * SLOTS
    for t in range(tile_total):
        grad = jnp.sum(tiles[t] * columns[:, t : t + 1], axis=0, keepdims=True)
        for c in range(folds):
            sent[pl.ds(base + c * tile_total + t, 1), :] = grad[:, c * LANES : (c + 1) * LANES]


def attitude_kernel(*refs, params, tile_total, seg_rows, folds):
    me, *blocks, _, mine, other, packed = refs
    core = lax.rem(me[0], 2)
    lane = lax.broadcasted_iota(jnp.int32, (tile_total, LANES), 1)
    first = (me[0] - core) * seg_rows
    base = tile_total * SLOTS
    group = LANES // tile_total
    sums = [jnp.zeros((2 * seg_rows, LANES), F32) for _ in range(folds)]
    curve = jnp.zeros((tile_total, LANES), F32)
    for g in range(0, len(blocks), group):
        members = blocks[g : g + group]
        hits = []
        for got in members:
            name = got[pl.ds(params + 1, tile_total, stride=SLOTS), :].astype(jnp.int32)
            hits.append(jnp.where(name - first == lane, 1.0, 0.0))
            curve = curve + got[pl.ds(params + 2, tile_total, stride=SLOTS), :]
        pick = jnp.concatenate(hits, axis=0).T[: 2 * seg_rows].astype(BF16)
        for c in range(folds):
            grads = jnp.concatenate(
                [got[pl.ds(base + c * tile_total, tile_total), :] for got in members], axis=0
            )
            for piece in halves(grads):
                sums[c] = sums[c] + jnp.dot(pick, piece, preferred_element_type=F32)
    even = core == 0
    for c in range(folds):
        low, high = sums[c][:seg_rows], sums[c][seg_rows:]
        mine[pl.ds(c * seg_rows, seg_rows), :] = jnp.where(even, low, high)
        other[pl.ds(c * seg_rows, seg_rows), :] = jnp.where(even, high, low)
    whole = jnp.sum(jnp.sum(curve, axis=0, keepdims=True), axis=1, keepdims=True)
    whole = jnp.broadcast_to(whole, (8, LANES))
    mine[pl.ds(folds * seg_rows, 8), :] = whole
    other[pl.ds(folds * seg_rows, 8), :] = whole
    for q, got in enumerate(blocks):
        packed[q] = got[:base, :]


def join_kernel(mine, other, _, part):
    part[...] = mine[...] + other[...]


def source_kernel(*refs, params, tile_total, span, singles, starts, ends, carries, many_range):
    me, *refs = refs
    if ends:
        *refs, token, left, right = refs
        token[...] = jnp.zeros_like(token)
        refs += [left, right]
    left, right = refs[-2:]
    refs = refs[:-2]
    if carries:
        refs[-1][...] = refs[-3][...]
        refs = refs[:-3] + refs[-2:-1]
    target = refs.pop()
    if not starts:
        acc = refs.pop(0)
    high_total = span // WIDE
    depth = params * high_total
    high_ids = lax.broadcasted_iota(jnp.int32, (high_total, LANES), 0).astype(BF16)
    low_ids = lax.broadcasted_iota(jnp.int32, (WIDE, LANES), 0).astype(BF16)
    one, zero = jnp.ones((), BF16), jnp.zeros((), BF16)

    def product(tiles_of):
        for t in range(tile_total):
            at = slice(t * LANES, (t + 1) * LANES)
            tile = tiles_of(t)
            local = tile[params : params + 1].astype(jnp.int32) - me[0] * span
            high = lax.shift_right_arithmetic(local, 8)
            high = jnp.where((high >= 0) & (high < high_total), high, high_total).astype(F32)
            low = lax.bitwise_and(local, WIDE - 1).astype(F32)
            low = jnp.broadcast_to(low, (WIDE, LANES)).astype(BF16)
            right[:, at] = jnp.where(low_ids == low, one, zero)
            hit = high_ids == jnp.broadcast_to(high, (high_total, LANES)).astype(BF16)
            for k in range(params):
                for p, piece in enumerate(halves(jnp.broadcast_to(tile[k : k + 1], (high_total, LANES)))):
                    row = p * depth + k * high_total
                    left[row : row + high_total, at] = jnp.where(hit, piece, zero)
        return lax.dot_general(left[...], right[...], NT, preferred_element_type=F32)

    total = jnp.zeros((2 * depth, WIDE), F32) if starts else acc[...]
    for got in refs[:singles]:
        total = total + product(lambda t: got[t * SLOTS : (t + 1) * SLOTS, :])
    if many_range:
        many = refs[singles]

        def step(d, total):
            return total + product(lambda t: many[d, t * SLOTS : (t + 1) * SLOTS, :])

        total = lax.fori_loop(*many_range, step, total)
    if ends:
        for k in range(params):
            for h in range(high_total):
                row = k * high_total + h
                target[k : k + 1, h * WIDE : (h + 1) * WIDE] = (
                    total[row : row + 1, :] + total[depth + row : depth + row + 1, :]
                )
    else:
        target[...] = total


def finish_kernel(*refs, seg_rows, folds):
    *parts, _, normal, curvature = refs
    total = parts[0][...]
    for part in parts[1:]:
        total = total + part[...]
    for c in range(folds):
        normal[:, c * LANES : (c + 1) * LANES] = total[c * seg_rows : (c + 1) * seg_rows]
    curvature[0, 0] = total[folds * seg_rows, 0]


def cost(microseconds):
    return pl.CostEstimate(flops=int(microseconds * 1e9), bytes_accessed=1, transcendentals=0)


def swapped(x, axis, size, offset):
    return lax.ppermute(x, axis, [(i, i ^ offset) for i in range(size)])


def per_device(tiles, tile_seg, tile_count, src_index, src_coef, obs_weight, att_dir, src_dir, *, sky, tm):
    tile_total, row_count, cols = tiles.shape
    params, span = src_dir.shape
    seg_rows = att_dir.shape[0]
    folds = cols // LANES
    across = range(2, tm, 2)
    me = lax.axis_index("tm").astype(jnp.int32).reshape(1)

    directions, index, coef, weight = pl.pallas_call(
        pack_kernel,
        out_shape=(
            jax.ShapeDtypeStruct((params * (span // LANES) + folds * seg_rows, LANES), F32),
            jax.ShapeDtypeStruct(src_index.shape, src_index.dtype),
            jax.ShapeDtypeStruct(src_coef.shape, F32),
            jax.ShapeDtypeStruct(obs_weight.shape, F32),
        ),
        in_specs=[HBM] * 5,
        out_specs=(VMEM,) * 4,
        scratch_shapes=[pltpu.VMEM((params, span), F32), pltpu.SemaphoreType.DMA((5 + folds,))],
        compiler_params=PARAMS,
        name="pack",
    )(*map(in_hbm, (src_dir, att_dir, src_index, src_coef, obs_weight)))

    far = list(across[1:])
    tables = {0: directions}
    for offset in across:
        tables[offset] = swapped(directions, "tm", tm, offset)
    tables[1] = swapped(directions, "tm", tm, 1)

    picked_shape = jax.ShapeDtypeStruct((params * tile_total, row_count), F32)

    def pick(offsets, before):
        return pl.pallas_call(
            functools.partial(pick_kernel, params=params, offsets=offsets, first=False),
            out_shape=picked_shape,
            in_specs=[SMEM] + [VMEM] * (len(offsets) + 2),
            out_specs=VMEM,
            compiler_params=PARAMS,
            cost_estimate=cost(0.4 * len(offsets)),
            name="pick",
        )(me, index, *[tables[o] for o in offsets], before)

    early = [0]
    picked, tiles_held = pl.pallas_call(
        functools.partial(pick_kernel, params=params, offsets=early, first=True),
        out_shape=(picked_shape, jax.ShapeDtypeStruct(tiles.shape, F32)),
        in_specs=[SMEM] + [VMEM] * (len(early) + 1) + [HBM],
        out_specs=(VMEM, VMEM),
        scratch_shapes=[pltpu.SemaphoreType.DMA],
        compiler_params=PARAMS,
        cost_estimate=cost(1.6),
        name="pick",
    )(me, index, *[tables[o] for o in early], in_hbm(tiles))

    def passed(offsets, after):
        return pl.pallas_call(
            functools.partial(pass_kernel, count=len(offsets)),
            out_shape=jax.ShapeDtypeStruct((len(offsets), *directions.shape), F32),
            in_specs=[VMEM] * (len(offsets) + 1),
            out_specs=VMEM,
            compiler_params=PARAMS,
            name="pass",
        )(*[tables[o] for o in offsets], after)

    first_pair = swapped(passed([2], picked), "tm", tm, 1)
    tables[3] = first_pair[0]
    picked = pick([1, 2], picked)
    others = swapped(passed(far, picked), "tm", tm, 1)
    for q, offset in enumerate(far):
        tables[offset + 1] = others[q]
    picked = pick([3, *far], picked)
    late = [o + 1 for o in across[1:]]
    offsets = sorted(tables)
    projected, sent = pl.pallas_call(
        functools.partial(project_kernel, seg_rows=seg_rows, offsets=offsets, late=late),
        out_shape=(
            jax.ShapeDtypeStruct((tile_total, row_count), F32),
            jax.ShapeDtypeStruct((tile_total * (SLOTS + folds), LANES), F32),
        ),
        in_specs=[SMEM] + [HBM] * 2 + [VMEM] * (5 + tm),
        out_specs=(VMEM, VMEM),
        scratch_shapes=[
            pltpu.SMEM(tile_seg.shape, jnp.int32),
            pltpu.SMEM(tile_count.shape, jnp.int32),
            pltpu.VMEM((tm, folds * seg_rows, LANES), F32),
            pltpu.SemaphoreType.DMA((2,)),
        ],
        compiler_params=PARAMS,
        name="project",
    )(
        me,
        *map(in_hbm, (tile_seg, tile_count)),
        tiles_held,
        picked,
        index,
        coef,
        weight,
        *[tables[o] for o in offsets],
    )

    blocks = [swapped(sent, "tm", tm, offset) for offset in across]
    part_shape = jax.ShapeDtypeStruct((folds * seg_rows + 8, LANES), F32)
    depth = params * (span // WIDE)
    sum_shape = jax.ShapeDtypeStruct((2 * depth, WIDE), F32)

    def source(before, singles, many=None, many_range=(), carried=None, after=None, out=sum_shape):
        operands = [x for x in (before, *singles, many, after, carried) if x is not None]
        ends = out is not sum_shape
        copied = () if carried is None else (jax.ShapeDtypeStruct(carried.shape, F32),)
        if ends:
            copied = (jax.ShapeDtypeStruct((8, LANES), F32),)
        return pl.pallas_call(
            functools.partial(
                source_kernel,
                params=params,
                tile_total=tile_total,
                span=span,
                singles=len(singles),
                starts=before is None,
                ends=ends,
                many_range=many_range,
                carries=carried is not None,
            ),
            out_shape=(out, *copied),
            in_specs=[SMEM] + [VMEM] * len(operands),
            out_specs=(VMEM,) * (1 + len(copied)),
            scratch_shapes=[
                pltpu.VMEM((2 * depth, tile_total * LANES), BF16),
                pltpu.VMEM((WIDE, tile_total * LANES), BF16),
            ],
            compiler_params=PARAMS,
            cost_estimate=cost(0.8 * (len(singles) + (len(range(*many_range)) if many_range else 0))),
            name="source",
        )(me, *operands)

    def join(one, two, after):
        return pl.pallas_call(
            join_kernel,
            out_shape=part_shape,
            in_specs=[VMEM] * 3,
            out_specs=VMEM,
            compiler_params=PARAMS,
            name="join",
        )(one, two, after)

    sums, projected = source(None, [sent], carried=projected)
    (sums,) = source(sums, blocks[:1])
    mine, other, packed = pl.pallas_call(
        functools.partial(
            attitude_kernel, params=params, tile_total=tile_total, seg_rows=seg_rows, folds=folds
        ),
        out_shape=(
            part_shape,
            part_shape,
            jax.ShapeDtypeStruct((tm // 2, tile_total * SLOTS, LANES), F32),
        ),
        in_specs=[SMEM] + [VMEM] * (tm // 2 + 1),
        out_specs=(VMEM,) * 3,
        compiler_params=PARAMS,
        name="attitude",
    )(me, sent, *blocks, sums)
    other = swapped(other, "tm", tm, 1)
    packed = swapped(packed, "tm", tm, 1)
    (sums,) = source(sums, blocks[1:2])
    part = join(mine, other, sums)
    half = tm // 4
    ranges = [(0, half), (half, tm // 2)]
    singles = blocks[2:]
    step = 1
    while step < sky:
        moved = swapped(part, "sky", sky, step)
        step *= 2
        if step < sky:
            if ranges[1:]:
                (sums,) = source(sums, singles, packed, ranges.pop(0), after=None)
                singles = []
            part = join(part, moved, sums)
    src_normal, token = source(
        sums, singles, packed, (ranges[0][0], tm // 2), after=part, out=jax.ShapeDtypeStruct((params, span), F32)
    )
    att_normal, curvature = pl.pallas_call(
        functools.partial(finish_kernel, seg_rows=seg_rows, folds=folds),
        out_shape=(
            jax.ShapeDtypeStruct((seg_rows, cols), F32),
            jax.ShapeDtypeStruct((1, 1), F32),
        ),
        in_specs=[VMEM] * 3,
        out_specs=(VMEM, SMEM),
        compiler_params=PARAMS,
        name="finish",
    )(part, moved, token)
    return projected, att_normal, src_normal, curvature.reshape(())


def solution(mesh):
    placed = (
        P(("sky", "tm"), None, None),
        P(("sky", "tm")),
        P(("sky", "tm")),
        P(("sky", "tm"), None),
        P(None, ("sky", "tm"), None),
        P(("sky", "tm"), None),
        P("tm", None),
        P(None, ("sky", "tm")),
    )
    return jax.shard_map(
        functools.partial(per_device, sky=mesh.shape["sky"], tm=mesh.shape["tm"]),
        mesh=mesh,
        in_specs=placed,
        out_specs=(P(("sky", "tm"), None), P("tm", None), P(None, ("sky", "tm")), P()),
        check_vma=False,
    )
```

```python
import functools

import jax
import jax.numpy as jnp
from jax import lax
from jax.experimental import pallas as pl
from jax.experimental.pallas import tpu as pltpu
from jax.sharding import PartitionSpec as P

LANES = 128
SLOTS = 8
WIDE = 256
NT = (((1,), (1,)), ((), ()))
F32 = jnp.float32
BF16 = jnp.bfloat16
VMEM = pl.BlockSpec(memory_space=pltpu.VMEM)
HBM = pl.BlockSpec(memory_space=pltpu.HBM)
SMEM = pl.BlockSpec(memory_space=pltpu.SMEM)
PARAMS = pltpu.CompilerParams(vmem_limit_bytes=16 * 1024 * 1024)


def in_hbm(x):
    return pltpu.with_memory_space_constraint(x, pltpu.HBM)


def halves(x):
    high = x.astype(BF16)
    return high, (x - high.astype(F32)).astype(BF16)


def rows_of(values, shape):
    ids = lax.broadcasted_iota(jnp.int32, shape, 0)
    out = jnp.zeros(shape, jnp.int32)
    for t, value in enumerate(values):
        out = jnp.where(ids == t, value, out)
    return out


def pack_kernel(source, attitude, index, coef, weight, directions, index_out, coef_out, weight_out, held, sems):
    params, span = source.shape
    seg_rows, cols = attitude.shape
    copies = [
        pltpu.make_async_copy(source, held, sems.at[0]),
        pltpu.make_async_copy(index, index_out, sems.at[2]),
        pltpu.make_async_copy(coef, coef_out, sems.at[3]),
        pltpu.make_async_copy(weight, weight_out, sems.at[4]),
    ]
    base = params * (span // LANES)
    for c in range(cols // LANES):
        copies.append(
            pltpu.make_async_copy(
                attitude.at[:, pl.ds(c * LANES, LANES)],
                directions.at[pl.ds(base + c * seg_rows, seg_rows), :],
                sems.at[5 + c],
            )
        )
    for copy in copies:
        copy.start()
    copies[0].wait()
    for b in range(span // LANES):
        directions[b * params : (b + 1) * params, :] = held[:, b * LANES : (b + 1) * LANES]
    for copy in copies[1:]:
        copy.wait()


def gather(owner, table, ids, picked, params):
    blocks = (table.shape[0] // (params * 8)) * 8
    lane = lax.rem(ids, LANES)
    block = lax.div(ids, LANES) - owner * blocks

    picked = list(picked)
    for b in range(blocks):
        hit = block == b
        for k in range(params):
            row = table[b * params + k : b * params + k + 1, :]
            found = jnp.take_along_axis(jnp.broadcast_to(row, ids.shape), lane, axis=1)
            picked[k] = jnp.where(hit, found, picked[k])
    return picked


def pass_kernel(*refs, count):
    for q in range(count):
        refs[-1][q] = refs[q][...]


def pick_kernel(*refs, params, offsets, first):
    me, index, *refs = refs
    ids = index[...]
    rows = ids.shape[0]
    tables, refs = refs[: len(offsets)], refs[len(offsets) :]
    if first:
        tiles_in, out, tiles, sem = refs
        copy = pltpu.make_async_copy(tiles_in, tiles, sem)
        copy.start()
        picked = [jnp.zeros(ids.shape, F32) for _ in range(params)]
    else:
        before, out = refs
        picked = [before[k * rows : (k + 1) * rows, :] for k in range(params)]
    for offset, table in zip(offsets, tables):
        picked = gather(lax.bitwise_xor(me[0], offset), table, ids, picked, params)
    for k in range(params):
        out[k * rows : (k + 1) * rows, :] = picked[k]
    if first:
        copy.wait()


def project_kernel(*refs, seg_rows, offsets, late):
    me, seg_in, count_in, tiles, before, index, coef, weight, *refs = refs
    tables, refs = refs[: len(offsets)], refs[len(offsets) :]
    projected, sent, seg, count, lines, sems = refs
    params, tile_total, width = coef.shape
    folds = tiles.shape[2] // LANES
    base = tables[0].shape[0] - folds * seg_rows
    copies = [
        pltpu.make_async_copy(seg_in, seg, sems.at[0]),
        pltpu.make_async_copy(count_in, count, sems.at[1]),
    ]
    for copy in copies:
        copy.start()
    ids = index[...]
    picked = [before[k * tile_total : (k + 1) * tile_total, :] for k in range(params)]
    for offset, table in zip(offsets, tables):
        lines[offset] = table[base:, :]
        if offset in late:
            picked = gather(lax.bitwise_xor(me[0], offset), table, ids, picked, params)
    for copy in copies:
        copy.wait()
    row_ids = lax.broadcasted_iota(jnp.int32, ids.shape, 0)
    total = jnp.zeros(ids.shape, F32)
    for t in range(tile_total):
        s = seg[t]
        place, local = lax.bitwise_xor(lax.div(s, seg_rows), me[0]), lax.rem(s, seg_rows)
        folded = None
        for c in range(folds):
            direction = lines[place, pl.ds(c * seg_rows + local, 1), :]
            product = tiles[t, :, c * LANES : (c + 1) * LANES] * direction
            folded = product if folded is None else folded + product
        total = jnp.where(row_ids == t, jnp.sum(folded.T, axis=0, keepdims=True), total)
    for k in range(params):
        total = total + coef[k] * picked[k]
    live = lax.broadcasted_iota(jnp.int32, ids.shape, 1) < rows_of(
        [count[t] for t in range(tile_total)], ids.shape
    )
    value = jnp.where(live, total, 0.0)
    weighted = weight[...] * value
    projected[...] = value
    for k in range(params):
        sent[pl.ds(k, tile_total, stride=SLOTS), :] = coef[k] * weighted
    sent[pl.ds(params, tile_total, stride=SLOTS), :] = ids.astype(F32)
    names = rows_of([seg[t] for t in range(tile_total)], ids.shape)
    sent[pl.ds(params + 1, tile_total, stride=SLOTS), :] = names.astype(F32)
    sent[pl.ds(params + 2, tile_total, stride=SLOTS), :] = value * weighted
    columns = weighted.T
    base = tile_total * SLOTS
    for t in range(tile_total):
        grad = jnp.sum(tiles[t] * columns[:, t : t + 1], axis=0, keepdims=True)
        for c in range(folds):
            sent[pl.ds(base + c * tile_total + t, 1), :] = grad[:, c * LANES : (c + 1) * LANES]


def attitude_kernel(*refs, params, tile_total, seg_rows, folds):
    me, *blocks, _, mine, other, packed = refs
    core = lax.rem(me[0], 2)
    lane = lax.broadcasted_iota(jnp.int32, (tile_total, LANES), 1)
    first = (me[0] - core) * seg_rows
    base = tile_total * SLOTS
    group = LANES // tile_total
    sums = [jnp.zeros((2 * seg_rows, LANES), F32) for _ in range(folds)]
    curve = jnp.zeros((tile_total, LANES), F32)
    for g in range(0, len(blocks), group):
        members = blocks[g : g + group]
        hits = []
        for got in members:
            name = got[pl.ds(params + 1, tile_total, stride=SLOTS), :].astype(jnp.int32)
            hits.append(jnp.where(name - first == lane, 1.0, 0.0))
            curve = curve + got[pl.ds(params + 2, tile_total, stride=SLOTS), :]
        pick = jnp.concatenate(hits, axis=0).T[: 2 * seg_rows].astype(BF16)
        for c in range(folds):
            grads = jnp.concatenate(
                [got[pl.ds(base + c * tile_total, tile_total), :] for got in members], axis=0
            )
            for piece in halves(grads):
                sums[c] = sums[c] + jnp.dot(pick, piece, preferred_element_type=F32)
    even = core == 0
    for c in range(folds):
        low, high = sums[c][:seg_rows], sums[c][seg_rows:]
        mine[pl.ds(c * seg_rows, seg_rows), :] = jnp.where(even, low, high)
        other[pl.ds(c * seg_rows, seg_rows), :] = jnp.where(even, high, low)
    whole = jnp.sum(jnp.sum(curve, axis=0, keepdims=True), axis=1, keepdims=True)
    whole = jnp.broadcast_to(whole, (8, LANES))
    mine[pl.ds(folds * seg_rows, 8), :] = whole
    other[pl.ds(folds * seg_rows, 8), :] = whole
    for q, got in enumerate(blocks):
        packed[q] = got[:base, :]


def join_kernel(mine, other, _, part):
    part[...] = mine[...] + other[...]


def source_kernel(*refs, params, tile_total, span, singles, starts, ends, carries, many_range):
    me, *refs = refs
    if ends:
        *refs, token, left, right = refs
        token[...] = jnp.zeros_like(token)
        refs += [left, right]
    left, right = refs[-2:]
    refs = refs[:-2]
    if carries:
        refs[-1][...] = refs[-3][...]
        refs = refs[:-3] + refs[-2:-1]
    target = refs.pop()
    if not starts:
        acc = refs.pop(0)
    high_total = span // WIDE
    depth = params * high_total
    high_ids = lax.broadcasted_iota(jnp.int32, (high_total, LANES), 0).astype(BF16)
    low_ids = lax.broadcasted_iota(jnp.int32, (WIDE, LANES), 0).astype(BF16)
    one, zero = jnp.ones((), BF16), jnp.zeros((), BF16)

    def product(tiles_of):
        for t in range(tile_total):
            at = slice(t * LANES, (t + 1) * LANES)
            tile = tiles_of(t)
            local = tile[params : params + 1].astype(jnp.int32) - me[0] * span
            high = lax.shift_right_arithmetic(local, 8)
            high = jnp.where((high >= 0) & (high < high_total), high, high_total).astype(F32)
            low = lax.bitwise_and(local, WIDE - 1).astype(F32)
            low = jnp.broadcast_to(low, (WIDE, LANES)).astype(BF16)
            right[:, at] = jnp.where(low_ids == low, one, zero)
            hit = high_ids == jnp.broadcast_to(high, (high_total, LANES)).astype(BF16)
            for k in range(params):
                for p, piece in enumerate(halves(jnp.broadcast_to(tile[k : k + 1], (high_total, LANES)))):
                    row = p * depth + k * high_total
                    left[row : row + high_total, at] = jnp.where(hit, piece, zero)
        return lax.dot_general(left[...], right[...], NT, preferred_element_type=F32)

    total = jnp.zeros((2 * depth, WIDE), F32) if starts else acc[...]
    for got in refs[:singles]:
        total = total + product(lambda t: got[t * SLOTS : (t + 1) * SLOTS, :])
    if many_range:
        many = refs[singles]

        def step(d, total):
            return total + product(lambda t: many[d, t * SLOTS : (t + 1) * SLOTS, :])

        total = lax.fori_loop(*many_range, step, total)
    if ends:
        for k in range(params):
            for h in range(high_total):
                row = k * high_total + h
                target[k : k + 1, h * WIDE : (h + 1) * WIDE] = (
                    total[row : row + 1, :] + total[depth + row : depth + row + 1, :]
                )
    else:
        target[...] = total


def finish_kernel(*refs, seg_rows, folds):
    *parts, _, normal, curvature = refs
    total = parts[0][...]
    for part in parts[1:]:
        total = total + part[...]
    for c in range(folds):
        normal[:, c * LANES : (c + 1) * LANES] = total[c * seg_rows : (c + 1) * seg_rows]
    curvature[0, 0] = total[folds * seg_rows, 0]


def cost(microseconds):
    return pl.CostEstimate(flops=int(microseconds * 1e9), bytes_accessed=1, transcendentals=0)


def swapped(x, axis, size, offset):
    return lax.ppermute(x, axis, [(i, i ^ offset) for i in range(size)])


def per_device(tiles, tile_seg, tile_count, src_index, src_coef, obs_weight, att_dir, src_dir, *, sky, tm):
    tile_total, row_count, cols = tiles.shape
    params, span = src_dir.shape
    seg_rows = att_dir.shape[0]
    folds = cols // LANES
    across = range(2, tm, 2)
    me = lax.axis_index("tm").astype(jnp.int32).reshape(1)

    directions, index, coef, weight = pl.pallas_call(
        pack_kernel,
        out_shape=(
            jax.ShapeDtypeStruct((params * (span // LANES) + folds * seg_rows, LANES), F32),
            jax.ShapeDtypeStruct(src_index.shape, src_index.dtype),
            jax.ShapeDtypeStruct(src_coef.shape, F32),
            jax.ShapeDtypeStruct(obs_weight.shape, F32),
        ),
        in_specs=[HBM] * 5,
        out_specs=(VMEM,) * 4,
        scratch_shapes=[pltpu.VMEM((params, span), F32), pltpu.SemaphoreType.DMA((5 + folds,))],
        compiler_params=PARAMS,
        name="pack",
    )(*map(in_hbm, (src_dir, att_dir, src_index, src_coef, obs_weight)))

    far = list(across[1:])
    tables = {0: directions}
    for offset in across:
        tables[offset] = swapped(directions, "tm", tm, offset)
    tables[1] = swapped(directions, "tm", tm, 1)

    picked_shape = jax.ShapeDtypeStruct((params * tile_total, row_count), F32)

    def pick(offsets, before):
        return pl.pallas_call(
            functools.partial(pick_kernel, params=params, offsets=offsets, first=False),
            out_shape=picked_shape,
            in_specs=[SMEM] + [VMEM] * (len(offsets) + 2),
            out_specs=VMEM,
            compiler_params=PARAMS,
            cost_estimate=cost(0.4 * len(offsets)),
            name="pick",
        )(me, index, *[tables[o] for o in offsets], before)

    early = [0]
    picked, tiles_held = pl.pallas_call(
        functools.partial(pick_kernel, params=params, offsets=early, first=True),
        out_shape=(picked_shape, jax.ShapeDtypeStruct(tiles.shape, F32)),
        in_specs=[SMEM] + [VMEM] * (len(early) + 1) + [HBM],
        out_specs=(VMEM, VMEM),
        scratch_shapes=[pltpu.SemaphoreType.DMA],
        compiler_params=PARAMS,
        cost_estimate=cost(1.6),
        name="pick",
    )(me, index, *[tables[o] for o in early], in_hbm(tiles))

    def passed(offsets, after):
        return pl.pallas_call(
            functools.partial(pass_kernel, count=len(offsets)),
            out_shape=jax.ShapeDtypeStruct((len(offsets), *directions.shape), F32),
            in_specs=[VMEM] * (len(offsets) + 1),
            out_specs=VMEM,
            compiler_params=PARAMS,
            name="pass",
        )(*[tables[o] for o in offsets], after)

    first_pair = swapped(passed([2], picked), "tm", tm, 1)
    tables[3] = first_pair[0]
    picked = pick([1, 2], picked)
    others = swapped(passed(far, picked), "tm", tm, 1)
    for q, offset in enumerate(far):
        tables[offset + 1] = others[q]
    picked = pick([3, *far], picked)
    late = [o + 1 for o in across[1:]]
    offsets = sorted(tables)
    projected, sent = pl.pallas_call(
        functools.partial(project_kernel, seg_rows=seg_rows, offsets=offsets, late=late),
        out_shape=(
            jax.ShapeDtypeStruct((tile_total, row_count), F32),
            jax.ShapeDtypeStruct((tile_total * (SLOTS + folds), LANES), F32),
        ),
        in_specs=[SMEM] + [HBM] * 2 + [VMEM] * (5 + tm),
        out_specs=(VMEM, VMEM),
        scratch_shapes=[
            pltpu.SMEM(tile_seg.shape, jnp.int32),
            pltpu.SMEM(tile_count.shape, jnp.int32),
            pltpu.VMEM((tm, folds * seg_rows, LANES), F32),
            pltpu.SemaphoreType.DMA((2,)),
        ],
        compiler_params=PARAMS,
        name="project",
    )(
        me,
        *map(in_hbm, (tile_seg, tile_count)),
        tiles_held,
        picked,
        index,
        coef,
        weight,
        *[tables[o] for o in offsets],
    )

    blocks = [swapped(sent, "tm", tm, offset) for offset in across]
    part_shape = jax.ShapeDtypeStruct((folds * seg_rows + 8, LANES), F32)
    depth = params * (span // WIDE)
    sum_shape = jax.ShapeDtypeStruct((2 * depth, WIDE), F32)

    def source(before, singles, many=None, many_range=(), carried=None, after=None, out=sum_shape):
        operands = [x for x in (before, *singles, many, after, carried) if x is not None]
        ends = out is not sum_shape
        copied = () if carried is None else (jax.ShapeDtypeStruct(carried.shape, F32),)
        if ends:
            copied = (jax.ShapeDtypeStruct((8, LANES), F32),)
        return pl.pallas_call(
            functools.partial(
                source_kernel,
                params=params,
                tile_total=tile_total,
                span=span,
                singles=len(singles),
                starts=before is None,
                ends=ends,
                many_range=many_range,
                carries=carried is not None,
            ),
            out_shape=(out, *copied),
            in_specs=[SMEM] + [VMEM] * len(operands),
            out_specs=(VMEM,) * (1 + len(copied)),
            scratch_shapes=[
                pltpu.VMEM((2 * depth, tile_total * LANES), BF16),
                pltpu.VMEM((WIDE, tile_total * LANES), BF16),
            ],
            compiler_params=PARAMS,
            cost_estimate=cost(0.8 * (len(singles) + (len(range(*many_range)) if many_range else 0))),
            name="source",
        )(me, *operands)

    def join(one, two, after):
        return pl.pallas_call(
            join_kernel,
            out_shape=part_shape,
            in_specs=[VMEM] * 3,
            out_specs=VMEM,
            compiler_params=PARAMS,
            name="join",
        )(one, two, after)

    sums, projected = source(None, [sent], carried=projected)
    (sums,) = source(sums, blocks[:1])
    mine, other, packed = pl.pallas_call(
        functools.partial(
            attitude_kernel, params=params, tile_total=tile_total, seg_rows=seg_rows, folds=folds
        ),
        out_shape=(
            part_shape,
            part_shape,
            jax.ShapeDtypeStruct((tm // 2, tile_total * SLOTS, LANES), F32),
        ),
        in_specs=[SMEM] + [VMEM] * (tm // 2 + 1),
        out_specs=(VMEM,) * 3,
        compiler_params=PARAMS,
        name="attitude",
    )(me, sent, *blocks, sums)
    other = swapped(other, "tm", tm, 1)
    packed = swapped(packed, "tm", tm, 1)
    (sums,) = source(sums, blocks[1:2])
    part = join(mine, other, sums)
    half = tm // 4
    ranges = [(0, half), (half, tm // 2)]
    singles = blocks[2:]
    step = 1
    while step < sky:
        moved = swapped(part, "sky", sky, step)
        step *= 2
        if step < sky:
            if ranges[1:]:
                (sums,) = source(sums, singles, packed, ranges.pop(0), after=None)
                singles = []
            part = join(part, moved, sums)
    src_normal, token = source(
        sums, singles, packed, (ranges[0][0], tm // 2), after=part, out=jax.ShapeDtypeStruct((params, span), F32)
    )
    att_normal, curvature = pl.pallas_call(
        functools.partial(finish_kernel, seg_rows=seg_rows, folds=folds),
        out_shape=(
            jax.ShapeDtypeStruct((seg_rows, cols), F32),
            jax.ShapeDtypeStruct((1, 1), F32),
        ),
        in_specs=[VMEM] * 3,
        out_specs=(VMEM, SMEM),
        compiler_params=PARAMS,
        name="finish",
    )(part, moved, token)
    return projected, att_normal, src_normal, curvature.reshape(())


def solution(mesh):
    placed = (
        P(("sky", "tm"), None, None),
        P(("sky", "tm")),
        P(("sky", "tm")),
        P(("sky", "tm"), None),
        P(None, ("sky", "tm"), None),
        P(("sky", "tm"), None),
        P("tm", None),
        P(None, ("sky", "tm")),
    )
    return jax.shard_map(
        functools.partial(per_device, sky=mesh.shape["sky"], tm=mesh.shape["tm"]),
        mesh=mesh,
        in_specs=placed,
        out_specs=(P(("sky", "tm"), None), P("tm", None), P(None, ("sky", "tm")), P()),
        check_vma=False,
    )
```

```python
import functools

import jax
import jax.numpy as jnp
from jax import lax
from jax.experimental import pallas as pl
from jax.experimental.pallas import tpu as pltpu
from jax.sharding import PartitionSpec as P

LANES = 128
CAP_TILES = 4
WIDE = 256
NT = (((1,), (1,)), ((), ()))
F32 = jnp.float32
BF16 = jnp.bfloat16
VMEM = pl.BlockSpec(memory_space=pltpu.VMEM)
HBM = pl.BlockSpec(memory_space=pltpu.HBM)
SMEM = pl.BlockSpec(memory_space=pltpu.SMEM)
PARAMS = pltpu.CompilerParams(vmem_limit_bytes=16 * 1024 * 1024)


def up8(rows):
    return (rows + 7) // 8 * 8


def in_hbm(x):
    return pltpu.with_memory_space_constraint(x, pltpu.HBM)


def halves(x):
    high = x.astype(BF16)
    return high, (x - high.astype(F32)).astype(BF16)


def rows_of(values, shape):
    ids = lax.broadcasted_iota(jnp.int32, shape, 0)
    out = jnp.zeros(shape, jnp.int32)
    for t, value in enumerate(values):
        out = jnp.where(ids == t, value, out)
    return out


def pack_kernel(source, attitude, index, coef, weight, directions, index_out, coef_out, weight_out, held, sems):
    params, span = source.shape
    seg_rows, cols = attitude.shape
    copies = [
        pltpu.make_async_copy(source, held, sems.at[0]),
        pltpu.make_async_copy(index, index_out, sems.at[2]),
        pltpu.make_async_copy(coef, coef_out, sems.at[3]),
        pltpu.make_async_copy(weight, weight_out, sems.at[4]),
    ]
    base = params * (span // LANES)
    for c in range(cols // LANES):
        copies.append(
            pltpu.make_async_copy(
                attitude.at[:, pl.ds(c * LANES, LANES)],
                directions.at[pl.ds(base + c * seg_rows, seg_rows), :],
                sems.at[5 + c],
            )
        )
    for copy in copies:
        copy.start()
    copies[0].wait()
    for b in range(span // LANES):
        directions[b * params : (b + 1) * params, :] = held[:, b * LANES : (b + 1) * LANES]
    for copy in copies[1:]:
        copy.wait()


def gather(owner, table, ids, picked, params):
    blocks = (table.shape[0] // (params * 8)) * 8
    lane = lax.rem(ids, LANES)
    block = lax.div(ids, LANES) - owner * blocks

    picked = list(picked)
    for b in range(blocks):
        hit = block == b
        for k in range(params):
            row = table[b * params + k : b * params + k + 1, :]
            found = jnp.take_along_axis(jnp.broadcast_to(row, ids.shape), lane, axis=1)
            picked[k] = jnp.where(hit, found, picked[k])
    return picked


def pass_kernel(*refs, count):
    for q in range(count):
        refs[-1][q] = refs[q][...]


def pick_kernel(*refs, params, offsets, first):
    me, index, *refs = refs
    ids = index[...]
    rows = ids.shape[0]
    tables, refs = refs[: len(offsets)], refs[len(offsets) :]
    if first:
        tiles_in, out, tiles, sem = refs
        copy = pltpu.make_async_copy(tiles_in, tiles, sem)
        copy.start()
        picked = [jnp.zeros(ids.shape, F32) for _ in range(params)]
    else:
        before, out = refs
        picked = [before[k * rows : (k + 1) * rows, :] for k in range(params)]
    for offset, table in zip(offsets, tables):
        picked = gather(lax.bitwise_xor(me[0], offset), table, ids, picked, params)
    for k in range(params):
        out[k * rows : (k + 1) * rows, :] = picked[k]
    if first:
        copy.wait()


def order_kernel(index, coef, _, tile_at, lane_at, coef_out, source_out, left, right, *, owners, span, cap):
    params, tile_total, _ = coef.shape
    slots = tile_at.shape[0]
    ids = index[...]
    owner = lax.div(ids, span)
    mask = jnp.concatenate([jnp.where(owner == o, 1.0, 0.0) for o in range(owners)], axis=0)
    rows = mask.shape[0]
    half = mask.astype(BF16)
    row_ids = lax.broadcasted_iota(jnp.int32, (LANES, LANES), 0)
    col_ids = lax.broadcasted_iota(jnp.int32, (LANES, LANES), 1)
    upper = jnp.where(row_ids < col_ids, 1.0, 0.0).astype(BF16)
    inside = jnp.dot(half, upper, preferred_element_type=F32)
    counts = jnp.dot(half, jnp.ones((LANES, LANES), BF16), preferred_element_type=F32)
    one = lax.broadcasted_iota(jnp.int32, (rows, rows), 0)
    two = lax.broadcasted_iota(jnp.int32, (rows, rows), 1)
    earlier = (lax.div(one, tile_total) == lax.div(two, tile_total)) & (two < one)
    earlier = jnp.where(earlier, 1.0, 0.0).astype(BF16)
    rank = inside + jnp.dot(earlier, counts.astype(BF16), preferred_element_type=F32)
    rank = mask * rank
    total = rank[:tile_total]
    for o in range(1, owners):
        total = total + rank[o * tile_total : (o + 1) * tile_total]
    slot = owner * cap + total.astype(jnp.int32)
    high = lax.div(slot, LANES).astype(F32)
    low = lax.rem(slot, LANES).astype(F32)
    high_ids = lax.broadcasted_iota(jnp.int32, (slots, LANES), 0).astype(BF16)
    low_ids = lax.broadcasted_iota(jnp.int32, (LANES, LANES), 0).astype(BF16)
    lanes = lax.broadcasted_iota(jnp.int32, (slots, LANES), 1).astype(BF16)
    unit, zero = jnp.ones((), BF16), jnp.zeros((), BF16)
    for t in range(tile_total):
        at = slice(t * LANES, (t + 1) * LANES)
        hit = high_ids == jnp.broadcast_to(high[t : t + 1], (slots, LANES)).astype(BF16)
        left[:slots, at] = jnp.where(hit, jnp.full((), t + 1, BF16), zero)
        left[slots:, at] = jnp.where(hit, lanes, zero)
        right[:, at] = jnp.where(
            low_ids == jnp.broadcast_to(low[t : t + 1], (LANES, LANES)).astype(BF16), unit, zero
        )
    place = lax.dot_general(left[...], right[...], NT, preferred_element_type=F32).astype(jnp.int32)
    tile, lane = place[:slots] - 1, place[slots:]
    tile_at[...] = tile
    lane_at[...] = lane
    ordered = [jnp.zeros((slots, LANES), F32) for _ in range(params)] + [jnp.full((slots, LANES), -1.0, F32)]
    for t in range(tile_total):
        hit = tile == t
        for k in range(params + 1):
            row = coef[k, t : t + 1, :] if k < params else ids[t : t + 1].astype(F32)
            found = jnp.take_along_axis(jnp.broadcast_to(row, (slots, LANES)), lane, axis=1)
            ordered[k] = jnp.where(hit, found, ordered[k])
    for k in range(params):
        coef_out[k] = ordered[k]
    source_out[...] = ordered[params]


def project_kernel(*refs, seg_rows, offsets, late):
    me, seg_in, count_in, tiles, before, index, coef, weight, tile_at, lane_at, coef_at, source_at, *refs = refs
    tables, refs = refs[: len(offsets)], refs[len(offsets) :]
    projected, sent, seg, count, used, lines, sems = refs
    params, tile_total, width = coef.shape
    folds = tiles.shape[2] // LANES
    base = tables[0].shape[0] - folds * seg_rows
    copies = [
        pltpu.make_async_copy(seg_in, seg, sems.at[0]),
        pltpu.make_async_copy(count_in, count, sems.at[1]),
    ]
    for copy in copies:
        copy.start()
    ids = index[...]
    picked = [before[k * tile_total : (k + 1) * tile_total, :] for k in range(params)]
    for offset, table in zip(offsets, tables):
        lines[offset] = table[base:, :]
        if offset in late:
            picked = gather(lax.bitwise_xor(me[0], offset), table, ids, picked, params)
    for copy in copies:
        copy.wait()
    row_ids = lax.broadcasted_iota(jnp.int32, ids.shape, 0)
    total = jnp.zeros(ids.shape, F32)
    for t in range(tile_total):
        s = seg[t]
        place, local = lax.bitwise_xor(lax.div(s, seg_rows), me[0]), lax.rem(s, seg_rows)
        folded = None
        for c in range(folds):
            direction = lines[place, pl.ds(c * seg_rows + local, 1), :]
            product = tiles[t, :, c * LANES : (c + 1) * LANES] * direction
            folded = product if folded is None else folded + product
        total = jnp.where(row_ids == t, jnp.sum(folded.T, axis=0, keepdims=True), total)
    for k in range(params):
        total = total + coef[k] * picked[k]
    live = lax.broadcasted_iota(jnp.int32, ids.shape, 1) < rows_of(
        [count[t] for t in range(tile_total)], ids.shape
    )
    value = jnp.where(live, total, 0.0)
    weighted = weight[...] * value
    projected[...] = value
    owners = len(offsets)
    slots = tile_at.shape[0]
    depth = sent.shape[0] // owners
    share = slots // owners
    tile, lane = tile_at[...], lane_at[...]
    ordered = jnp.zeros(tile.shape, F32)
    for t in range(tile_total):
        row = jnp.broadcast_to(weighted[t : t + 1], tile.shape)
        ordered = jnp.where(tile == t, jnp.take_along_axis(row, lane, axis=1), ordered)
    grads_from = up8((params + 1) * share)
    names_from = grads_from + folds * CAP_TILES
    curve = jnp.sum(value * weighted, axis=0, keepdims=True)
    for o in range(owners):
        used[o] = 0
        sent[pl.ds(o * depth + grads_from, folds * CAP_TILES), :] = jnp.zeros((folds * CAP_TILES, LANES), F32)
        sent[pl.ds(o * depth + names_from, CAP_TILES), :] = jnp.full((CAP_TILES, LANES), -1.0, F32)
        sent[pl.ds(o * depth + names_from + CAP_TILES, 1), :] = curve
    for k in range(params + 1):
        values = coef_at[k] * ordered if k < params else source_at[...]
        for o in range(owners):
            sent[pl.ds(o * depth + k * share, share), :] = values[o * share : (o + 1) * share]
    columns = weighted.T
    for t in range(tile_total):
        s = seg[t]
        owner = lax.div(s, seg_rows)
        place = used[owner]
        used[owner] = place + 1
        start = owner * depth + place
        grad = jnp.sum(tiles[t] * columns[:, t : t + 1], axis=0, keepdims=True)
        for c in range(folds):
            sent[pl.ds(start + grads_from + c * CAP_TILES, 1), :] = grad[:, c * LANES : (c + 1) * LANES]
        sent[pl.ds(start + names_from, 1), :] = jnp.full((1, LANES), s, jnp.int32).astype(F32)


def attitude_kernel(me, got, part, *, owners, grads_from, seg_rows, folds):
    depth = got.shape[0] // owners
    names_from = grads_from + folds * CAP_TILES
    lane = lax.broadcasted_iota(jnp.int32, (owners, LANES), 1)
    first = me[0] * seg_rows
    hits, grads = [], [[] for _ in range(folds)]
    for r in range(CAP_TILES):
        name = got[pl.ds(names_from + r, owners, stride=depth), :].astype(jnp.int32)
        hits.append(jnp.where(name - first == lane, 1.0, 0.0))
        for c in range(folds):
            grads[c].append(got[pl.ds(grads_from + c * CAP_TILES + r, owners, stride=depth), :])
    pick = jnp.concatenate(hits, axis=0).T[:seg_rows].astype(BF16)
    for c in range(folds):
        total = jnp.zeros((seg_rows, LANES), F32)
        for piece in halves(jnp.concatenate(grads[c], axis=0)):
            total = total + jnp.dot(pick, piece, preferred_element_type=F32)
        part[pl.ds(c * seg_rows, seg_rows), :] = total
    curve = got[pl.ds(names_from + CAP_TILES, owners, stride=depth), :]
    whole = jnp.sum(jnp.sum(curve, axis=0, keepdims=True), axis=1, keepdims=True)
    part[pl.ds(folds * seg_rows, 8), :] = jnp.broadcast_to(whole, (8, LANES))


def join_kernel(mine, other, _, part):
    part[...] = mine[...] + other[...]


def source_kernel(me, got, held, out, kept, token, left, right, *, owners, share):
    params, span = out.shape
    depth = got.shape[0] // owners
    kept[...] = held[...]
    token[...] = jnp.zeros_like(token)
    high_total = span // WIDE
    high_ids = lax.broadcasted_iota(jnp.int32, (high_total, LANES), 0).astype(BF16)
    low_ids = lax.broadcasted_iota(jnp.int32, (WIDE, LANES), 0).astype(BF16)
    one, zero = jnp.ones((), BF16), jnp.zeros((), BF16)
    half = params * high_total
    group = right.shape[1] // LANES
    places = [o * depth + h for o in range(owners) for h in range(share)]
    total = jnp.zeros((2 * half, WIDE), F32)
    for g in range(0, len(places), group):
        for t, place in enumerate(places[g : g + group]):
            at = slice(t * LANES, (t + 1) * LANES)
            rows = [got[place + k * share : place + k * share + 1, :] for k in range(params + 1)]
            local = rows[params].astype(jnp.int32) - me[0] * span
            high = lax.shift_right_arithmetic(local, 8)
            high = jnp.where((high >= 0) & (high < high_total), high, high_total).astype(F32)
            low = lax.bitwise_and(local, WIDE - 1).astype(F32)
            low = jnp.broadcast_to(low, (WIDE, LANES)).astype(BF16)
            right[:, at] = jnp.where(low_ids == low, one, zero)
            hit = high_ids == jnp.broadcast_to(high, (high_total, LANES)).astype(BF16)
            for k in range(params):
                for p, piece in enumerate(halves(jnp.broadcast_to(rows[k], (high_total, LANES)))):
                    row = p * half + k * high_total
                    left[row : row + high_total, at] = jnp.where(hit, piece, zero)
        total = total + lax.dot_general(left[...], right[...], NT, preferred_element_type=F32)
    for k in range(params):
        for h in range(high_total):
            row = k * high_total + h
            out[k : k + 1, h * WIDE : (h + 1) * WIDE] = total[row : row + 1, :] + total[half + row : half + row + 1, :]


def finish_kernel(*refs, seg_rows, folds):
    *parts, _, normal, curvature = refs
    total = parts[0][...]
    for part in parts[1:]:
        total = total + part[...]
    for c in range(folds):
        normal[:, c * LANES : (c + 1) * LANES] = total[c * seg_rows : (c + 1) * seg_rows]
    curvature[0, 0] = total[folds * seg_rows, 0]


def cost(microseconds):
    return pl.CostEstimate(flops=int(microseconds * 1e9), bytes_accessed=1, transcendentals=0)


def swapped(x, axis, size, offset):
    return lax.ppermute(x, axis, [(i, i ^ offset) for i in range(size)])


def per_device(tiles, tile_seg, tile_count, src_index, src_coef, obs_weight, att_dir, src_dir, *, sky, tm):
    tile_total, row_count, cols = tiles.shape
    params, span = src_dir.shape
    seg_rows = att_dir.shape[0]
    folds = cols // LANES
    across = range(2, tm, 2)
    me = lax.axis_index("tm").astype(jnp.int32).reshape(1)

    directions, index, coef, weight = pl.pallas_call(
        pack_kernel,
        out_shape=(
            jax.ShapeDtypeStruct((params * (span // LANES) + folds * seg_rows, LANES), F32),
            jax.ShapeDtypeStruct(src_index.shape, src_index.dtype),
            jax.ShapeDtypeStruct(src_coef.shape, F32),
            jax.ShapeDtypeStruct(obs_weight.shape, F32),
        ),
        in_specs=[HBM] * 5,
        out_specs=(VMEM,) * 4,
        scratch_shapes=[pltpu.VMEM((params, span), F32), pltpu.SemaphoreType.DMA((5 + folds,))],
        compiler_params=PARAMS,
        name="pack",
    )(*map(in_hbm, (src_dir, att_dir, src_index, src_coef, obs_weight)))

    far = list(across[1:])
    tables = {0: directions}
    for offset in across:
        tables[offset] = swapped(directions, "tm", tm, offset)
    tables[1] = swapped(directions, "tm", tm, 1)

    picked_shape = jax.ShapeDtypeStruct((params * tile_total, row_count), F32)

    def pick(offsets, before):
        return pl.pallas_call(
            functools.partial(pick_kernel, params=params, offsets=offsets, first=False),
            out_shape=picked_shape,
            in_specs=[SMEM] + [VMEM] * (len(offsets) + 2),
            out_specs=VMEM,
            compiler_params=PARAMS,
            cost_estimate=cost(0.4 * len(offsets)),
            name="pick",
        )(me, index, *[tables[o] for o in offsets], before)

    early = [0]
    picked, tiles_held = pl.pallas_call(
        functools.partial(pick_kernel, params=params, offsets=early, first=True),
        out_shape=(picked_shape, jax.ShapeDtypeStruct(tiles.shape, F32)),
        in_specs=[SMEM] + [VMEM] * (len(early) + 1) + [HBM],
        out_specs=(VMEM, VMEM),
        scratch_shapes=[pltpu.SemaphoreType.DMA],
        compiler_params=PARAMS,
        cost_estimate=cost(1.6),
        name="pick",
    )(me, index, *[tables[o] for o in early], in_hbm(tiles))

    def passed(offsets, after):
        return pl.pallas_call(
            functools.partial(pass_kernel, count=len(offsets)),
            out_shape=jax.ShapeDtypeStruct((len(offsets), *directions.shape), F32),
            in_specs=[VMEM] * (len(offsets) + 1),
            out_specs=VMEM,
            compiler_params=PARAMS,
            name="pass",
        )(*[tables[o] for o in offsets], after)

    first_pair = swapped(passed([2], picked), "tm", tm, 1)
    tables[3] = first_pair[0]
    picked = pick([1, 2], picked)
    slots = 2 * tile_total
    places = jax.ShapeDtypeStruct((slots, LANES), jnp.int32)
    tile_at, lane_at, coef_at, source_at = pl.pallas_call(
        functools.partial(order_kernel, owners=tm, span=span, cap=slots * LANES // tm),
        out_shape=(
            places,
            places,
            jax.ShapeDtypeStruct((params, slots, LANES), F32),
            jax.ShapeDtypeStruct((slots, LANES), F32),
        ),
        in_specs=[VMEM] * 3,
        out_specs=(VMEM,) * 4,
        scratch_shapes=[
            pltpu.VMEM((2 * slots, tile_total * LANES), BF16),
            pltpu.VMEM((LANES, tile_total * LANES), BF16),
        ],
        compiler_params=PARAMS,
        cost_estimate=cost(1.5),
        name="order",
    )(index, coef, picked)
    others = swapped(passed(far, tile_at), "tm", tm, 1)
    for q, offset in enumerate(far):
        tables[offset + 1] = others[q]
    picked = pick([3, *far], picked)
    late = [o + 1 for o in across[1:]]
    offsets = sorted(tables)
    share = slots // tm
    grads_from = up8((params + 1) * share)
    depth = up8(grads_from + (folds + 1) * CAP_TILES + 1)
    projected, sent = pl.pallas_call(
        functools.partial(project_kernel, seg_rows=seg_rows, offsets=offsets, late=late),
        out_shape=(
            jax.ShapeDtypeStruct((tile_total, row_count), F32),
            jax.ShapeDtypeStruct((tm * depth, LANES), F32),
        ),
        in_specs=[SMEM] + [HBM] * 2 + [VMEM] * (9 + tm),
        out_specs=(VMEM, VMEM),
        scratch_shapes=[
            pltpu.SMEM(tile_seg.shape, jnp.int32),
            pltpu.SMEM(tile_count.shape, jnp.int32),
            pltpu.SMEM((tm,), jnp.int32),
            pltpu.VMEM((tm, folds * seg_rows, LANES), F32),
            pltpu.SemaphoreType.DMA((2,)),
        ],
        compiler_params=PARAMS,
        name="project",
    )(
        me,
        *map(in_hbm, (tile_seg, tile_count)),
        tiles_held,
        picked,
        index,
        coef,
        weight,
        tile_at,
        lane_at,
        coef_at,
        source_at,
        *[tables[o] for o in offsets],
    )

    got = lax.all_to_all(sent.reshape(tm, depth, LANES), "tm", 0, 0).reshape(tm * depth, LANES)
    part_shape = jax.ShapeDtypeStruct((folds * seg_rows + 8, LANES), F32)
    part = pl.pallas_call(
        functools.partial(attitude_kernel, owners=tm, grads_from=grads_from, seg_rows=seg_rows, folds=folds),
        out_shape=part_shape,
        in_specs=[SMEM, VMEM],
        out_specs=VMEM,
        compiler_params=PARAMS,
        name="attitude",
    )(me, got)
    half = params * (span // WIDE)
    src_normal, projected, token = pl.pallas_call(
        functools.partial(source_kernel, owners=tm, share=share),
        out_shape=(
            jax.ShapeDtypeStruct((params, span), F32),
            jax.ShapeDtypeStruct((tile_total, row_count), F32),
            jax.ShapeDtypeStruct((8, LANES), F32),
        ),
        in_specs=[SMEM] + [VMEM] * 2,
        out_specs=(VMEM,) * 3,
        scratch_shapes=[
            pltpu.VMEM((2 * half, tile_total * LANES), BF16),
            pltpu.VMEM((WIDE, tile_total * LANES), BF16),
        ],
        compiler_params=PARAMS,
        cost_estimate=cost(2.0),
        name="source",
    )(me, got, projected)
    step = 1
    while step < sky:
        moved = swapped(part, "sky", sky, step)
        step *= 2
        if step < sky:
            part = pl.pallas_call(
                join_kernel,
                out_shape=part_shape,
                in_specs=[VMEM] * 3,
                out_specs=VMEM,
                compiler_params=PARAMS,
                name="join",
            )(part, moved, token)
    att_normal, curvature = pl.pallas_call(
        functools.partial(finish_kernel, seg_rows=seg_rows, folds=folds),
        out_shape=(
            jax.ShapeDtypeStruct((seg_rows, cols), F32),
            jax.ShapeDtypeStruct((1, 1), F32),
        ),
        in_specs=[VMEM] * 3,
        out_specs=(VMEM, SMEM),
        compiler_params=PARAMS,
        name="finish",
    )(part, moved, token)
    return projected, att_normal, src_normal, curvature.reshape(())


def solution(mesh):
    placed = (
        P(("sky", "tm"), None, None),
        P(("sky", "tm")),
        P(("sky", "tm")),
        P(("sky", "tm"), None),
        P(None, ("sky", "tm"), None),
        P(("sky", "tm"), None),
        P("tm", None),
        P(None, ("sky", "tm")),
    )
    return jax.shard_map(
        functools.partial(per_device, sky=mesh.shape["sky"], tm=mesh.shape["tm"]),
        mesh=mesh,
        in_specs=placed,
        out_specs=(P(("sky", "tm"), None), P("tm", None), P(None, ("sky", "tm")), P()),
        check_vma=False,
    )
```

```python
import functools

import jax
import jax.numpy as jnp
from jax import lax
from jax.experimental import pallas as pl
from jax.experimental.pallas import tpu as pltpu
from jax.sharding import PartitionSpec as P

LANES = 128
CAP_TILES = 4
WIDE = 256
NT = (((1,), (1,)), ((), ()))
F32 = jnp.float32
BF16 = jnp.bfloat16
VMEM = pl.BlockSpec(memory_space=pltpu.VMEM)
HBM = pl.BlockSpec(memory_space=pltpu.HBM)
SMEM = pl.BlockSpec(memory_space=pltpu.SMEM)
PARAMS = pltpu.CompilerParams(vmem_limit_bytes=16 * 1024 * 1024)


def up8(rows):
    return (rows + 7) // 8 * 8


def in_hbm(x):
    return pltpu.with_memory_space_constraint(x, pltpu.HBM)


def halves(x):
    high = x.astype(BF16)
    return high, (x - high.astype(F32)).astype(BF16)


def rows_of(values, shape):
    ids = lax.broadcasted_iota(jnp.int32, shape, 0)
    out = jnp.zeros(shape, jnp.int32)
    for t, value in enumerate(values):
        out = jnp.where(ids == t, value, out)
    return out


def pack_kernel(source, attitude, index, coef, weight, directions, index_out, coef_out, weight_out, held, sems):
    params, span = source.shape
    seg_rows, cols = attitude.shape
    copies = [
        pltpu.make_async_copy(source, held, sems.at[0]),
        pltpu.make_async_copy(index, index_out, sems.at[2]),
        pltpu.make_async_copy(coef, coef_out, sems.at[3]),
        pltpu.make_async_copy(weight, weight_out, sems.at[4]),
    ]
    base = params * (span // LANES)
    for c in range(cols // LANES):
        copies.append(
            pltpu.make_async_copy(
                attitude.at[:, pl.ds(c * LANES, LANES)],
                directions.at[pl.ds(base + c * seg_rows, seg_rows), :],
                sems.at[5 + c],
            )
        )
    for copy in copies:
        copy.start()
    copies[0].wait()
    for b in range(span // LANES):
        directions[b * params : (b + 1) * params, :] = held[:, b * LANES : (b + 1) * LANES]
    for copy in copies[1:]:
        copy.wait()


def gather(owner, table, ids, picked, params):
    blocks = (table.shape[0] // (params * 8)) * 8
    lane = lax.rem(ids, LANES)
    block = lax.div(ids, LANES) - owner * blocks

    picked = list(picked)
    for b in range(blocks):
        hit = block == b
        for k in range(params):
            row = table[b * params + k : b * params + k + 1, :]
            found = jnp.take_along_axis(jnp.broadcast_to(row, ids.shape), lane, axis=1)
            picked[k] = jnp.where(hit, found, picked[k])
    return picked


def pass_kernel(*refs, count):
    for q in range(count):
        refs[-1][q] = refs[q][...]


def pick_kernel(*refs, params, offsets, first):
    me, index, *refs = refs
    ids = index[...]
    rows = ids.shape[0]
    tables, refs = refs[: len(offsets)], refs[len(offsets) :]
    if first:
        tiles_in, out, tiles, sem = refs
        copy = pltpu.make_async_copy(tiles_in, tiles, sem)
        copy.start()
        picked = [jnp.zeros(ids.shape, F32) for _ in range(params)]
    else:
        before, out = refs
        picked = [before[k * rows : (k + 1) * rows, :] for k in range(params)]
    for offset, table in zip(offsets, tables):
        picked = gather(lax.bitwise_xor(me[0], offset), table, ids, picked, params)
    for k in range(params):
        out[k * rows : (k + 1) * rows, :] = picked[k]
    if first:
        copy.wait()


def order_kernel(index, coef, _, tile_at, lane_at, coef_out, source_out, left, right, *, owners, span, cap):
    params, tile_total, _ = coef.shape
    slots = tile_at.shape[0]
    ids = index[...]
    owner = lax.div(ids, span)
    mask = jnp.concatenate([jnp.where(owner == o, 1.0, 0.0) for o in range(owners)], axis=0)
    rows = mask.shape[0]
    half = mask.astype(BF16)
    row_ids = lax.broadcasted_iota(jnp.int32, (LANES, LANES), 0)
    col_ids = lax.broadcasted_iota(jnp.int32, (LANES, LANES), 1)
    upper = jnp.where(row_ids < col_ids, 1.0, 0.0).astype(BF16)
    inside = jnp.dot(half, upper, preferred_element_type=F32)
    counts = jnp.dot(half, jnp.ones((LANES, LANES), BF16), preferred_element_type=F32)
    one = lax.broadcasted_iota(jnp.int32, (rows, rows), 0)
    two = lax.broadcasted_iota(jnp.int32, (rows, rows), 1)
    earlier = (lax.div(one, tile_total) == lax.div(two, tile_total)) & (two < one)
    earlier = jnp.where(earlier, 1.0, 0.0).astype(BF16)
    rank = inside + jnp.dot(earlier, counts.astype(BF16), preferred_element_type=F32)
    rank = mask * rank
    total = rank[:tile_total]
    for o in range(1, owners):
        total = total + rank[o * tile_total : (o + 1) * tile_total]
    slot = owner * cap + total.astype(jnp.int32)
    high = lax.div(slot, LANES).astype(F32)
    low = lax.rem(slot, LANES).astype(F32)
    high_ids = lax.broadcasted_iota(jnp.int32, (slots, LANES), 0).astype(BF16)
    low_ids = lax.broadcasted_iota(jnp.int32, (LANES, LANES), 0).astype(BF16)
    lanes = lax.broadcasted_iota(jnp.int32, (slots, LANES), 1).astype(BF16)
    unit, zero = jnp.ones((), BF16), jnp.zeros((), BF16)
    for t in range(tile_total):
        at = slice(t * LANES, (t + 1) * LANES)
        hit = high_ids == jnp.broadcast_to(high[t : t + 1], (slots, LANES)).astype(BF16)
        left[:slots, at] = jnp.where(hit, jnp.full((), t + 1, BF16), zero)
        left[slots:, at] = jnp.where(hit, lanes, zero)
        right[:, at] = jnp.where(
            low_ids == jnp.broadcast_to(low[t : t + 1], (LANES, LANES)).astype(BF16), unit, zero
        )
    place = lax.dot_general(left[...], right[...], NT, preferred_element_type=F32).astype(jnp.int32)
    tile, lane = place[:slots] - 1, place[slots:]
    tile_at[...] = tile
    lane_at[...] = lane
    ordered = [jnp.zeros((slots, LANES), F32) for _ in range(params)] + [jnp.full((slots, LANES), -1.0, F32)]
    for t in range(tile_total):
        hit = tile == t
        for k in range(params + 1):
            row = coef[k, t : t + 1, :] if k < params else ids[t : t + 1].astype(F32)
            found = jnp.take_along_axis(jnp.broadcast_to(row, (slots, LANES)), lane, axis=1)
            ordered[k] = jnp.where(hit, found, ordered[k])
    for k in range(params):
        coef_out[k] = ordered[k]
    source_out[...] = ordered[params]


def project_kernel(*refs, seg_rows, offsets, late):
    me, seg_in, count_in, tiles, before, index, coef, weight, tile_at, lane_at, coef_at, source_at, *refs = refs
    tables, refs = refs[: len(offsets)], refs[len(offsets) :]
    projected, sent, seg, count, used, lines, sems = refs
    params, tile_total, width = coef.shape
    folds = tiles.shape[2] // LANES
    base = tables[0].shape[0] - folds * seg_rows
    copies = [
        pltpu.make_async_copy(seg_in, seg, sems.at[0]),
        pltpu.make_async_copy(count_in, count, sems.at[1]),
    ]
    for copy in copies:
        copy.start()
    ids = index[...]
    picked = [before[k * tile_total : (k + 1) * tile_total, :] for k in range(params)]
    for offset, table in zip(offsets, tables):
        lines[offset] = table[base:, :]
        if offset in late:
            picked = gather(lax.bitwise_xor(me[0], offset), table, ids, picked, params)
    for copy in copies:
        copy.wait()
    row_ids = lax.broadcasted_iota(jnp.int32, ids.shape, 0)
    total = jnp.zeros(ids.shape, F32)
    for t in range(tile_total):
        s = seg[t]
        place, local = lax.bitwise_xor(lax.div(s, seg_rows), me[0]), lax.rem(s, seg_rows)
        folded = None
        for c in range(folds):
            direction = lines[place, pl.ds(c * seg_rows + local, 1), :]
            product = tiles[t, :, c * LANES : (c + 1) * LANES] * direction
            folded = product if folded is None else folded + product
        total = jnp.where(row_ids == t, jnp.sum(folded.T, axis=0, keepdims=True), total)
    for k in range(params):
        total = total + coef[k] * picked[k]
    live = lax.broadcasted_iota(jnp.int32, ids.shape, 1) < rows_of(
        [count[t] for t in range(tile_total)], ids.shape
    )
    value = jnp.where(live, total, 0.0)
    weighted = weight[...] * value
    projected[...] = value
    owners = len(offsets)
    slots = tile_at.shape[0]
    depth = sent.shape[0] // owners
    share = slots // owners
    tile, lane = tile_at[...], lane_at[...]
    ordered = jnp.zeros(tile.shape, F32)
    for t in range(tile_total):
        row = jnp.broadcast_to(weighted[t : t + 1], tile.shape)
        ordered = jnp.where(tile == t, jnp.take_along_axis(row, lane, axis=1), ordered)
    grads_from = up8((params + 1) * share)
    names_from = grads_from + folds * CAP_TILES
    curve = jnp.sum(value * weighted, axis=0, keepdims=True)
    for o in range(owners):
        used[o] = 0
        sent[pl.ds(o * depth + grads_from, folds * CAP_TILES), :] = jnp.zeros((folds * CAP_TILES, LANES), F32)
        sent[pl.ds(o * depth + names_from, CAP_TILES), :] = jnp.full((CAP_TILES, LANES), -1.0, F32)
        sent[pl.ds(o * depth + names_from + CAP_TILES, 1), :] = curve
    for k in range(params + 1):
        values = coef_at[k] * ordered if k < params else source_at[...]
        for o in range(owners):
            sent[pl.ds(o * depth + k * share, share), :] = values[o * share : (o + 1) * share]
    pieces = jnp.concatenate(halves(weighted), axis=0).astype(F32)
    whose = lax.rem(lax.broadcasted_iota(jnp.int32, pieces.shape, 0), tile_total)
    grads = jnp.zeros((2 * tile_total, tiles.shape[2]), F32)
    rest = jnp.zeros((tile_total, tiles.shape[2]), F32)
    for t in range(tile_total):
        first, second = halves(tiles[t])
        left = jnp.where(whose == t, pieces, 0.0).astype(BF16)
        grads = grads + jnp.dot(left, first, preferred_element_type=F32)
        rest = rest + jnp.dot(left[:tile_total], second, preferred_element_type=F32)
    grads = grads[:tile_total] + grads[tile_total:] + rest
    for t in range(tile_total):
        s = seg[t]
        owner = lax.div(s, seg_rows)
        place = used[owner]
        used[owner] = place + 1
        start = owner * depth + place
        grad = grads[t : t + 1]
        for c in range(folds):
            sent[pl.ds(start + grads_from + c * CAP_TILES, 1), :] = grad[:, c * LANES : (c + 1) * LANES]
        sent[pl.ds(start + names_from, 1), :] = jnp.full((1, LANES), s, jnp.int32).astype(F32)


def attitude_kernel(me, got, part, *, owners, grads_from, seg_rows, folds):
    depth = got.shape[0] // owners
    names_from = grads_from + folds * CAP_TILES
    lane = lax.broadcasted_iota(jnp.int32, (owners, LANES), 1)
    first = me[0] * seg_rows
    hits, grads = [], [[] for _ in range(folds)]
    for r in range(CAP_TILES):
        name = got[pl.ds(names_from + r, owners, stride=depth), :].astype(jnp.int32)
        hits.append(jnp.where(name - first == lane, 1.0, 0.0))
        for c in range(folds):
            grads[c].append(got[pl.ds(grads_from + c * CAP_TILES + r, owners, stride=depth), :])
    pick = jnp.concatenate(hits, axis=0).T[:seg_rows].astype(BF16)
    for c in range(folds):
        total = jnp.zeros((seg_rows, LANES), F32)
        for piece in halves(jnp.concatenate(grads[c], axis=0)):
            total = total + jnp.dot(pick, piece, preferred_element_type=F32)
        part[pl.ds(c * seg_rows, seg_rows), :] = total
    curve = got[pl.ds(names_from + CAP_TILES, owners, stride=depth), :]
    whole = jnp.sum(jnp.sum(curve, axis=0, keepdims=True), axis=1, keepdims=True)
    part[pl.ds(folds * seg_rows, 8), :] = jnp.broadcast_to(whole, (8, LANES))


def source_kernel(me, got, held, out, kept, token, left, right, *, owners, share):
    params, span = out.shape
    depth = got.shape[0] // owners
    kept[...] = held[...]
    token[...] = jnp.zeros_like(token)
    high_total = span // WIDE
    high_ids = lax.broadcasted_iota(jnp.int32, (high_total, LANES), 0).astype(BF16)
    low_ids = lax.broadcasted_iota(jnp.int32, (WIDE, LANES), 0).astype(BF16)
    one, zero = jnp.ones((), BF16), jnp.zeros((), BF16)
    half = params * high_total
    group = right.shape[1] // LANES
    places = [o * depth + h for o in range(owners) for h in range(share)]
    total = jnp.zeros((2 * half, WIDE), F32)
    for g in range(0, len(places), group):
        for t, place in enumerate(places[g : g + group]):
            at = slice(t * LANES, (t + 1) * LANES)
            rows = [got[place + k * share : place + k * share + 1, :] for k in range(params + 1)]
            local = rows[params].astype(jnp.int32) - me[0] * span
            high = lax.shift_right_arithmetic(local, 8)
            high = jnp.where((high >= 0) & (high < high_total), high, high_total).astype(F32)
            low = lax.bitwise_and(local, WIDE - 1).astype(F32)
            low = jnp.broadcast_to(low, (WIDE, LANES)).astype(BF16)
            right[:, at] = jnp.where(low_ids == low, one, zero)
            hit = high_ids == jnp.broadcast_to(high, (high_total, LANES)).astype(BF16)
            for k in range(params):
                for p, piece in enumerate(halves(jnp.broadcast_to(rows[k], (high_total, LANES)))):
                    row = p * half + k * high_total
                    left[row : row + high_total, at] = jnp.where(hit, piece, zero)
        total = total + lax.dot_general(left[...], right[...], NT, preferred_element_type=F32)
    for k in range(params):
        for h in range(high_total):
            row = k * high_total + h
            out[k : k + 1, h * WIDE : (h + 1) * WIDE] = total[row : row + 1, :] + total[half + row : half + row + 1, :]


def finish_kernel(*refs, seg_rows, folds):
    *parts, _, normal, curvature = refs
    total = parts[0][...]
    for part in parts[1:]:
        total = total + part[...]
    for c in range(folds):
        normal[:, c * LANES : (c + 1) * LANES] = total[c * seg_rows : (c + 1) * seg_rows]
    curvature[0, 0] = total[folds * seg_rows, 0]


def cost(microseconds):
    return pl.CostEstimate(flops=int(microseconds * 1e9), bytes_accessed=1, transcendentals=0)


def swapped(x, axis, size, offset):
    return lax.ppermute(x, axis, [(i, i ^ offset) for i in range(size)])


def per_device(tiles, tile_seg, tile_count, src_index, src_coef, obs_weight, att_dir, src_dir, *, sky, tm):
    tile_total, row_count, cols = tiles.shape
    params, span = src_dir.shape
    seg_rows = att_dir.shape[0]
    folds = cols // LANES
    across = range(2, tm, 2)
    me = lax.axis_index("tm").astype(jnp.int32).reshape(1)

    directions, index, coef, weight = pl.pallas_call(
        pack_kernel,
        out_shape=(
            jax.ShapeDtypeStruct((params * (span // LANES) + folds * seg_rows, LANES), F32),
            jax.ShapeDtypeStruct(src_index.shape, src_index.dtype),
            jax.ShapeDtypeStruct(src_coef.shape, F32),
            jax.ShapeDtypeStruct(obs_weight.shape, F32),
        ),
        in_specs=[HBM] * 5,
        out_specs=(VMEM,) * 4,
        scratch_shapes=[pltpu.VMEM((params, span), F32), pltpu.SemaphoreType.DMA((5 + folds,))],
        compiler_params=PARAMS,
        name="pack",
    )(*map(in_hbm, (src_dir, att_dir, src_index, src_coef, obs_weight)))

    far = list(across[1:])
    tables = {0: directions}
    for offset in across:
        tables[offset] = swapped(directions, "tm", tm, offset)
    tables[1] = swapped(directions, "tm", tm, 1)

    picked_shape = jax.ShapeDtypeStruct((params * tile_total, row_count), F32)

    def pick(offsets, before):
        return pl.pallas_call(
            functools.partial(pick_kernel, params=params, offsets=offsets, first=False),
            out_shape=picked_shape,
            in_specs=[SMEM] + [VMEM] * (len(offsets) + 2),
            out_specs=VMEM,
            compiler_params=PARAMS,
            cost_estimate=cost(0.4 * len(offsets)),
            name="pick",
        )(me, index, *[tables[o] for o in offsets], before)

    early = [0]
    picked, tiles_held = pl.pallas_call(
        functools.partial(pick_kernel, params=params, offsets=early, first=True),
        out_shape=(picked_shape, jax.ShapeDtypeStruct(tiles.shape, F32)),
        in_specs=[SMEM] + [VMEM] * (len(early) + 1) + [HBM],
        out_specs=(VMEM, VMEM),
        scratch_shapes=[pltpu.SemaphoreType.DMA],
        compiler_params=PARAMS,
        cost_estimate=cost(1.6),
        name="pick",
    )(me, index, *[tables[o] for o in early], in_hbm(tiles))

    def passed(offsets, after):
        return pl.pallas_call(
            functools.partial(pass_kernel, count=len(offsets)),
            out_shape=jax.ShapeDtypeStruct((len(offsets), *directions.shape), F32),
            in_specs=[VMEM] * (len(offsets) + 1),
            out_specs=VMEM,
            compiler_params=PARAMS,
            name="pass",
        )(*[tables[o] for o in offsets], after)

    first_pair = swapped(passed([2], picked), "tm", tm, 1)
    tables[3] = first_pair[0]
    picked = pick([1, 2], picked)
    slots = 2 * tile_total
    places = jax.ShapeDtypeStruct((slots, LANES), jnp.int32)
    tile_at, lane_at, coef_at, source_at = pl.pallas_call(
        functools.partial(order_kernel, owners=tm, span=span, cap=slots * LANES // tm),
        out_shape=(
            places,
            places,
            jax.ShapeDtypeStruct((params, slots, LANES), F32),
            jax.ShapeDtypeStruct((slots, LANES), F32),
        ),
        in_specs=[VMEM] * 3,
        out_specs=(VMEM,) * 4,
        scratch_shapes=[
            pltpu.VMEM((2 * slots, tile_total * LANES), BF16),
            pltpu.VMEM((LANES, tile_total * LANES), BF16),
        ],
        compiler_params=PARAMS,
        cost_estimate=cost(1.5),
        name="order",
    )(index, coef, picked)
    others = swapped(passed(far, tile_at), "tm", tm, 1)
    for q, offset in enumerate(far):
        tables[offset + 1] = others[q]
    picked = pick([3, *far], picked)
    late = [o + 1 for o in across[1:]]
    offsets = sorted(tables)
    share = slots // tm
    grads_from = up8((params + 1) * share)
    depth = up8(grads_from + (folds + 1) * CAP_TILES + 1)
    projected, sent = pl.pallas_call(
        functools.partial(project_kernel, seg_rows=seg_rows, offsets=offsets, late=late),
        out_shape=(
            jax.ShapeDtypeStruct((tile_total, row_count), F32),
            jax.ShapeDtypeStruct((tm * depth, LANES), F32),
        ),
        in_specs=[SMEM] + [HBM] * 2 + [VMEM] * (9 + tm),
        out_specs=(VMEM, VMEM),
        scratch_shapes=[
            pltpu.SMEM(tile_seg.shape, jnp.int32),
            pltpu.SMEM(tile_count.shape, jnp.int32),
            pltpu.SMEM((tm,), jnp.int32),
            pltpu.VMEM((tm, folds * seg_rows, LANES), F32),
            pltpu.SemaphoreType.DMA((2,)),
        ],
        compiler_params=PARAMS,
        name="project",
    )(
        me,
        *map(in_hbm, (tile_seg, tile_count)),
        tiles_held,
        picked,
        index,
        coef,
        weight,
        tile_at,
        lane_at,
        coef_at,
        source_at,
        *[tables[o] for o in offsets],
    )

    got = lax.all_to_all(sent.reshape(tm, depth, LANES), "tm", 0, 0).reshape(tm * depth, LANES)
    part_shape = jax.ShapeDtypeStruct((folds * seg_rows + 8, LANES), F32)
    part = pl.pallas_call(
        functools.partial(attitude_kernel, owners=tm, grads_from=grads_from, seg_rows=seg_rows, folds=folds),
        out_shape=part_shape,
        in_specs=[SMEM, VMEM],
        out_specs=VMEM,
        compiler_params=PARAMS,
        name="attitude",
    )(me, got)
    half = params * (span // WIDE)
    src_normal, projected, token = pl.pallas_call(
        functools.partial(source_kernel, owners=tm, share=share),
        out_shape=(
            jax.ShapeDtypeStruct((params, span), F32),
            jax.ShapeDtypeStruct((tile_total, row_count), F32),
            jax.ShapeDtypeStruct((8, LANES), F32),
        ),
        in_specs=[SMEM] + [VMEM] * 2,
        out_specs=(VMEM,) * 3,
        scratch_shapes=[
            pltpu.VMEM((2 * half, tile_total * LANES), BF16),
            pltpu.VMEM((WIDE, tile_total * LANES), BF16),
        ],
        compiler_params=PARAMS,
        cost_estimate=cost(2.0),
        name="source",
    )(me, got, projected)
    order = [*range(sky // 2, sky), *range(1, sky // 2)]
    others = [swapped(part, "sky", sky, offset) for offset in order]
    att_normal, curvature = pl.pallas_call(
        functools.partial(finish_kernel, seg_rows=seg_rows, folds=folds),
        out_shape=(
            jax.ShapeDtypeStruct((seg_rows, cols), F32),
            jax.ShapeDtypeStruct((1, 1), F32),
        ),
        in_specs=[VMEM] * (sky + 1),
        out_specs=(VMEM, SMEM),
        compiler_params=PARAMS,
        name="finish",
    )(part, *others, token)
    return projected, att_normal, src_normal, curvature.reshape(())


def solution(mesh):
    placed = (
        P(("sky", "tm"), None, None),
        P(("sky", "tm")),
        P(("sky", "tm")),
        P(("sky", "tm"), None),
        P(None, ("sky", "tm"), None),
        P(("sky", "tm"), None),
        P("tm", None),
        P(None, ("sky", "tm")),
    )
    return jax.shard_map(
        functools.partial(per_device, sky=mesh.shape["sky"], tm=mesh.shape["tm"]),
        mesh=mesh,
        in_specs=placed,
        out_specs=(P(("sky", "tm"), None), P("tm", None), P(None, ("sky", "tm")), P()),
        check_vma=False,
    )
```

```python
import functools

import jax
import jax.numpy as jnp
from jax import lax
from jax.experimental import pallas as pl
from jax.experimental.pallas import tpu as pltpu
from jax.sharding import PartitionSpec as P

LANES = 128
CAP_TILES = 4
WIDE = 256
NT = (((1,), (1,)), ((), ()))
F32 = jnp.float32
BF16 = jnp.bfloat16
VMEM = pl.BlockSpec(memory_space=pltpu.VMEM)
HBM = pl.BlockSpec(memory_space=pltpu.HBM)
SMEM = pl.BlockSpec(memory_space=pltpu.SMEM)
PARAMS = pltpu.CompilerParams(vmem_limit_bytes=16 * 1024 * 1024)


def up8(rows):
    return (rows + 7) // 8 * 8


def in_hbm(x):
    return pltpu.with_memory_space_constraint(x, pltpu.HBM)


def halves(x):
    high = x.astype(BF16)
    return high, (x - high.astype(F32)).astype(BF16)


def thirds(x):
    high = x.astype(BF16)
    return (high, *halves(x - high.astype(F32)))


def pack_kernel(source, attitude, *refs):
    small, (directions, *outs), (held, sems) = refs[:5], refs[5:11], refs[11:]
    params, span = source.shape
    seg_rows, cols = attitude.shape
    copies = [
        pltpu.make_async_copy(source, held, sems.at[0]),
        *[pltpu.make_async_copy(x, out, sems.at[1 + q]) for q, (x, out) in enumerate(zip(small, outs))],
    ]
    base = params * (span // LANES)
    for c in range(cols // LANES):
        copies.append(
            pltpu.make_async_copy(
                attitude.at[:, pl.ds(c * LANES, LANES)],
                directions.at[pl.ds(base + c * seg_rows, seg_rows), :],
                sems.at[6 + c],
            )
        )
    for copy in copies:
        copy.start()
    copies[0].wait()
    for b in range(span // LANES):
        directions[b * params : (b + 1) * params, :] = held[:, b * LANES : (b + 1) * LANES]
    for copy in copies[1:]:
        copy.wait()


def serve(owner, table, block, column, coef, total, share):
    params = coef.shape[0]
    blocks = (table.shape[0] // (params * 8)) * 8
    parts = 8 // share
    rows = pl.ds(pl.multiple_of(owner * 8, 8), 8)
    here, lane = block[rows, :], column[rows, :]
    part = lax.div(lax.broadcasted_iota(jnp.int32, here.shape, 0), share)
    picked = [jnp.zeros(here.shape, F32) for _ in range(params)]
    for b in range(blocks // parts):
        hit = here == b
        for k in range(params):
            line = None
            for p in range(parts):
                at = (p * (blocks // parts) + b) * params + k
                row = jnp.broadcast_to(table[at : at + 1, :], here.shape)
                line = row if line is None else jnp.where(part == p, row, line)
            picked[k] = jnp.where(hit, jnp.take_along_axis(line, lane, axis=1), picked[k])
    terms = jnp.zeros(here.shape, F32)
    for k in range(params):
        terms = terms + coef[k, rows, :] * picked[k]
    total[rows, :] = terms


def own_kernel(me, table, block, column, coef, tiles_in, total, tiles, sem, *, share):
    copy = pltpu.make_async_copy(tiles_in, tiles, sem)
    copy.start()
    total[...] = jnp.zeros_like(total)
    serve(me[0], table, block, column, coef, total, share)
    copy.wait()


def pick_kernel(*refs, offsets, share):
    me, *tables, block, column, coef, before, total = refs
    total[...] = before[...]
    for offset, table in zip(offsets, tables):
        serve(lax.bitwise_xor(me[0], offset), table, block, column, coef, total, share)


def pass_kernel(*refs, count):
    for q in range(count):
        refs[-1][q] = refs[q][...]


def order_kernel(me, seg, count, index, coef, *refs, owners, span, cap, seg_rows):
    tile_at, lane_at, coef_out, source_out, block, column, coef_by, row_at, rank_at, live, aim, fill, names, left, right = refs
    params, tile_total, _ = coef.shape
    slots = tile_at.shape[0]
    ids = index[...]
    owner = lax.div(ids, span)
    mask = jnp.concatenate([jnp.where(owner == o, 1.0, 0.0) for o in range(owners)], axis=0)
    rows = mask.shape[0]
    half = mask.astype(BF16)
    row_ids = lax.broadcasted_iota(jnp.int32, (LANES, LANES), 0)
    col_ids = lax.broadcasted_iota(jnp.int32, (LANES, LANES), 1)
    upper = jnp.where(row_ids < col_ids, 1.0, 0.0).astype(BF16)
    inside = jnp.dot(half, upper, preferred_element_type=F32)
    counts = jnp.dot(half, jnp.ones((LANES, LANES), BF16), preferred_element_type=F32)
    one = lax.broadcasted_iota(jnp.int32, (rows, rows), 0)
    two = lax.broadcasted_iota(jnp.int32, (rows, rows), 1)
    earlier = (lax.div(one, tile_total) == lax.div(two, tile_total)) & (two < one)
    earlier = jnp.where(earlier, 1.0, 0.0).astype(BF16)
    rank = inside + jnp.dot(earlier, counts.astype(BF16), preferred_element_type=F32)
    rank = mask * rank
    total = rank[:tile_total]
    for o in range(1, owners):
        total = total + rank[o * tile_total : (o + 1) * tile_total]
    place = total.astype(jnp.int32)
    row_at[...] = owner * 8 + lax.div(place, LANES)
    rank_at[...] = lax.rem(place, LANES)
    slot = owner * cap + place
    high = lax.div(slot, LANES).astype(F32)
    low = lax.rem(slot, LANES).astype(F32)
    high_ids = lax.broadcasted_iota(jnp.int32, (slots, LANES), 0).astype(BF16)
    low_ids = lax.broadcasted_iota(jnp.int32, (LANES, LANES), 0).astype(BF16)
    lanes = lax.broadcasted_iota(jnp.int32, (slots, LANES), 1).astype(BF16)
    unit, zero = jnp.ones((), BF16), jnp.zeros((), BF16)
    for t in range(tile_total):
        at = slice(t * LANES, (t + 1) * LANES)
        hit = high_ids == jnp.broadcast_to(high[t : t + 1], (slots, LANES)).astype(BF16)
        left[:slots, at] = jnp.where(hit, jnp.full((), t + 1, BF16), zero)
        left[slots:, at] = jnp.where(hit, lanes, zero)
        right[:, at] = jnp.where(
            low_ids == jnp.broadcast_to(low[t : t + 1], (LANES, LANES)).astype(BF16), unit, zero
        )
    place = lax.dot_general(left[...], right[...], NT, preferred_element_type=F32).astype(jnp.int32)
    tile, lane = place[:slots] - 1, place[slots:]
    tile_at[...] = tile
    lane_at[...] = lane
    ordered = [jnp.zeros((slots, LANES), F32) for _ in range(params)] + [jnp.full((slots, LANES), -1.0, F32)]
    for t in range(tile_total):
        hit = tile == t
        for k in range(params + 1):
            row = coef[k, t : t + 1, :] if k < params else ids[t : t + 1].astype(F32)
            found = jnp.take_along_axis(jnp.broadcast_to(row, (slots, LANES)), lane, axis=1)
            ordered[k] = jnp.where(hit, found, ordered[k])
    for k in range(params):
        coef_out[k] = ordered[k]
    source_out[...] = ordered[params]
    source = ordered[params].astype(jnp.int32)
    blocks, share = span // LANES, slots // owners
    parts = 8 // share
    within = jnp.where(source < 0, -blocks, lax.div(lax.rem(source, span), LANES))
    across = jnp.where(source < 0, 0, lax.rem(source, LANES))
    for o in range(owners):
        rows, mine = slice(o * 8, (o + 1) * 8), slice(o * share, (o + 1) * share)
        block[rows, :] = jnp.concatenate([within[mine] - p * (blocks // parts) for p in range(parts)], axis=0)
        column[rows, :] = jnp.concatenate([across[mine]] * parts, axis=0)
        for k in range(params):
            coef_by[k, rows, :] = jnp.concatenate([ordered[k][mine]] * parts, axis=0)
    square = (tile_total, tile_total)
    one = lax.broadcasted_iota(jnp.int32, square, 0)
    two = lax.broadcasted_iota(jnp.int32, square, 1)

    def down_of(row):
        return jnp.sum(jnp.where(one == two, jnp.broadcast_to(row, square), 0), axis=1, keepdims=True)

    along, down = seg[...], down_of(seg[...])
    owner_along, owner_down = lax.div(along, seg_rows), lax.div(down, seg_rows)
    live[...] = jnp.where(
        lax.broadcasted_iota(jnp.int32, ids.shape, 1) < jnp.broadcast_to(down_of(count[...]), ids.shape), 1.0, 0.0
    )
    line = lax.bitwise_xor(owner_down, me[0]) * seg_rows + lax.rem(down, seg_rows)
    aim[...] = jnp.where(
        lax.broadcasted_iota(jnp.int32, aim.shape, 1) == jnp.broadcast_to(line, aim.shape), 1.0, 0.0
    )
    same = jnp.broadcast_to(owner_down, square) == jnp.broadcast_to(owner_along, square)
    ranks = jnp.sum(jnp.where(same & (one < two), 1, 0), axis=0, keepdims=True)
    place = jnp.broadcast_to(owner_along * CAP_TILES + ranks, fill.shape)
    filled = lax.broadcasted_iota(jnp.int32, fill.shape, 0) == place
    fill[...] = jnp.where(filled, 1.0, 0.0)
    named = jnp.sum(jnp.where(filled, jnp.broadcast_to(along + 1, fill.shape), 0), axis=1, keepdims=True) - 1
    names[...] = jnp.broadcast_to(named, names.shape).astype(F32)


def project_kernel(*refs, seg_rows, offsets, late):
    me, tiles, before, weight, tile_at, lane_at, coef_at, source_at, *refs = refs
    block, column, coef_by, row_at, rank_at, live, aim, fill, names, *refs = refs
    tables, refs = refs[: len(offsets)], refs[len(offsets) :]
    projected, sent, lines, served = refs
    params, tile_total, width = coef_at.shape[0], *weight.shape
    share = tile_at.shape[0] // len(offsets)
    folds = tiles.shape[2] // LANES
    base = tables[0].shape[0] - folds * seg_rows
    served[...] = before[...]
    for offset, table in zip(offsets, tables):
        for c in range(folds):
            lines[offset * seg_rows : (offset + 1) * seg_rows, c * LANES : (c + 1) * LANES] = table[
                base + c * seg_rows : base + (c + 1) * seg_rows, :
            ]
        if offset in late:
            serve(lax.bitwise_xor(me[0], offset), table, block, column, coef_by, served, share)
    shape = weight.shape
    row, rank = row_at[...], rank_at[...]
    total = jnp.zeros(shape, F32)
    for o in range(len(offsets)):
        for h in range(share):
            line = served[o * 8 + h : o * 8 + h + 1, :]
            for p in range(1, 8 // share):
                at = o * 8 + p * share + h
                line = line + served[at : at + 1, :]
            found = jnp.take_along_axis(jnp.broadcast_to(line, shape), rank, axis=1)
            total = jnp.where(row == o * 8 + h, found, total)
    hit = aim[...].astype(BF16)
    directions = jnp.zeros((tile_total, folds * LANES), F32)
    for piece in thirds(lines[...]):
        directions = directions + jnp.dot(hit, piece, preferred_element_type=F32)
    row_ids = lax.broadcasted_iota(jnp.int32, shape, 0)
    tile_part = jnp.zeros(shape, F32)
    for t in range(tile_total):
        folded = None
        for c in range(folds):
            part = slice(c * LANES, (c + 1) * LANES)
            product = tiles[t, :, part] * directions[t : t + 1, part]
            folded = product if folded is None else folded + product
        tile_part = jnp.where(row_ids == t, jnp.sum(folded.T, axis=0, keepdims=True), tile_part)
    total = total + tile_part
    value = jnp.where(live[...] > 0.5, total, 0.0)
    weighted = weight[...] * value
    projected[...] = value
    owners = len(offsets)
    slots = tile_at.shape[0]
    depth = sent.shape[0] // owners
    tile, lane = tile_at[...], lane_at[...]
    ordered = jnp.zeros(tile.shape, F32)
    for t in range(tile_total):
        row = jnp.broadcast_to(weighted[t : t + 1], tile.shape)
        ordered = jnp.where(tile == t, jnp.take_along_axis(row, lane, axis=1), ordered)
    grads_from = up8((params + 1) * share)
    names_from = grads_from + folds * CAP_TILES
    curve = jnp.sum(value * weighted, axis=0, keepdims=True)
    for k in range(params + 1):
        values = coef_at[k] * ordered if k < params else source_at[...]
        for o in range(owners):
            sent[pl.ds(o * depth + k * share, share), :] = values[o * share : (o + 1) * share]
    pieces = jnp.concatenate(halves(weighted), axis=0).astype(F32)
    whose = lax.rem(lax.broadcasted_iota(jnp.int32, pieces.shape, 0), tile_total)
    grads = jnp.zeros((2 * tile_total, tiles.shape[2]), F32)
    rest = jnp.zeros((tile_total, tiles.shape[2]), F32)
    for t in range(tile_total):
        first, second = halves(tiles[t])
        left = jnp.where(whose == t, pieces, 0.0).astype(BF16)
        grads = grads + jnp.dot(left, first, preferred_element_type=F32)
        rest = rest + jnp.dot(left[:tile_total], second, preferred_element_type=F32)
    grads = grads[:tile_total] + grads[tile_total:] + rest
    place = fill[...].astype(BF16)
    placed = jnp.zeros((fill.shape[0], folds * LANES), F32)
    for piece in halves(grads):
        placed = placed + jnp.dot(place, piece, preferred_element_type=F32)
    for o in range(owners):
        rows = slice(o * CAP_TILES, (o + 1) * CAP_TILES)
        for c in range(folds):
            sent[pl.ds(o * depth + grads_from + c * CAP_TILES, CAP_TILES), :] = placed[rows, c * LANES : (c + 1) * LANES]
        sent[pl.ds(o * depth + names_from, CAP_TILES), :] = names[rows, :]
        sent[pl.ds(o * depth + names_from + CAP_TILES, 1), :] = curve


def attitude_kernel(me, got, part, *, owners, grads_from, seg_rows, folds):
    depth = got.shape[0] // owners
    names_from = grads_from + folds * CAP_TILES
    lane = lax.broadcasted_iota(jnp.int32, (owners, LANES), 1)
    first = me[0] * seg_rows
    hits, grads = [], [[] for _ in range(folds)]
    for r in range(CAP_TILES):
        name = got[pl.ds(names_from + r, owners, stride=depth), :].astype(jnp.int32)
        hits.append(jnp.where(name - first == lane, 1.0, 0.0))
        for c in range(folds):
            grads[c].append(got[pl.ds(grads_from + c * CAP_TILES + r, owners, stride=depth), :])
    pick = jnp.concatenate(hits, axis=0).T[:seg_rows].astype(BF16)
    for c in range(folds):
        total = jnp.zeros((seg_rows, LANES), F32)
        for piece in halves(jnp.concatenate(grads[c], axis=0)):
            total = total + jnp.dot(pick, piece, preferred_element_type=F32)
        part[pl.ds(c * seg_rows, seg_rows), :] = total
    curve = got[pl.ds(names_from + CAP_TILES, owners, stride=depth), :]
    whole = jnp.sum(jnp.sum(curve, axis=0, keepdims=True), axis=1, keepdims=True)
    part[pl.ds(folds * seg_rows, 8), :] = jnp.broadcast_to(whole, (8, LANES))


def source_kernel(me, got, held, out, kept, token, left, right, *, owners, share):
    params, span = out.shape
    depth = got.shape[0] // owners
    kept[...] = held[...]
    token[...] = jnp.zeros_like(token)
    high_total = span // WIDE
    high_ids = lax.broadcasted_iota(jnp.int32, (high_total, LANES), 0).astype(BF16)
    low_ids = lax.broadcasted_iota(jnp.int32, (WIDE, LANES), 0).astype(BF16)
    one, zero = jnp.ones((), BF16), jnp.zeros((), BF16)
    half = params * high_total
    group = right.shape[1] // LANES
    places = [o * depth + h for o in range(owners) for h in range(share)]
    total = jnp.zeros((2 * half, WIDE), F32)
    for g in range(0, len(places), group):
        for t, place in enumerate(places[g : g + group]):
            at = slice(t * LANES, (t + 1) * LANES)
            rows = [got[place + k * share : place + k * share + 1, :] for k in range(params + 1)]
            local = rows[params].astype(jnp.int32) - me[0] * span
            high = lax.shift_right_arithmetic(local, 8)
            high = jnp.where((high >= 0) & (high < high_total), high, high_total).astype(F32)
            low = lax.bitwise_and(local, WIDE - 1).astype(F32)
            low = jnp.broadcast_to(low, (WIDE, LANES)).astype(BF16)
            right[:, at] = jnp.where(low_ids == low, one, zero)
            hit = high_ids == jnp.broadcast_to(high, (high_total, LANES)).astype(BF16)
            for k in range(params):
                for p, piece in enumerate(halves(jnp.broadcast_to(rows[k], (high_total, LANES)))):
                    row = p * half + k * high_total
                    left[row : row + high_total, at] = jnp.where(hit, piece, zero)
        total = total + lax.dot_general(left[...], right[...], NT, preferred_element_type=F32)
    for k in range(params):
        for h in range(high_total):
            row = k * high_total + h
            out[k : k + 1, h * WIDE : (h + 1) * WIDE] = total[row : row + 1, :] + total[half + row : half + row + 1, :]


def finish_kernel(*refs, seg_rows, folds):
    *parts, _, normal, curvature = refs
    total = parts[0][...]
    for part in parts[1:]:
        total = total + part[...]
    for c in range(folds):
        normal[:, c * LANES : (c + 1) * LANES] = total[c * seg_rows : (c + 1) * seg_rows]
    curvature[0, 0] = total[folds * seg_rows, 0]


def cost(microseconds):
    return pl.CostEstimate(flops=int(microseconds * 1e9), bytes_accessed=1, transcendentals=0)


def swapped(x, axis, size, offset):
    return lax.ppermute(x, axis, [(i, i ^ offset) for i in range(size)])


def per_device(tiles, tile_seg, tile_count, src_index, src_coef, obs_weight, att_dir, src_dir, *, sky, tm):
    tile_total, row_count, cols = tiles.shape
    params, span = src_dir.shape
    seg_rows = att_dir.shape[0]
    folds = cols // LANES
    across = range(3, tm, 2)
    me = lax.axis_index("tm").astype(jnp.int32).reshape(1)

    directions, index, coef, weight, seg, count = pl.pallas_call(
        pack_kernel,
        out_shape=(
            jax.ShapeDtypeStruct((params * (span // LANES) + folds * seg_rows, LANES), F32),
            jax.ShapeDtypeStruct(src_index.shape, src_index.dtype),
            jax.ShapeDtypeStruct(src_coef.shape, F32),
            jax.ShapeDtypeStruct(obs_weight.shape, F32),
            jax.ShapeDtypeStruct((1, tile_total), jnp.int32),
            jax.ShapeDtypeStruct((1, tile_total), jnp.int32),
        ),
        in_specs=[HBM] * 7,
        out_specs=(VMEM,) * 6,
        scratch_shapes=[pltpu.VMEM((params, span), F32), pltpu.SemaphoreType.DMA((6 + folds,))],
        compiler_params=PARAMS,
        name="pack",
    )(*map(in_hbm, (src_dir, att_dir, src_index, src_coef, obs_weight, *(x.reshape(1, -1) for x in (tile_seg, tile_count)))))

    far = list(across[1:])
    tables = {0: directions}
    for offset in across:
        tables[offset] = swapped(directions, "tm", tm, offset)
    tables[1] = swapped(directions, "tm", tm, 1)

    def passed(offsets, after):
        return pl.pallas_call(
            functools.partial(pass_kernel, count=len(offsets)),
            out_shape=jax.ShapeDtypeStruct((len(offsets), *directions.shape), F32),
            in_specs=[VMEM] * (len(offsets) + 1),
            out_specs=VMEM,
            compiler_params=PARAMS,
            name="pass",
        )(*[tables[o] for o in offsets], after)

    slots = 2 * tile_total
    share = slots // tm
    places = jax.ShapeDtypeStruct((slots, LANES), jnp.int32)
    by_owner = jax.ShapeDtypeStruct((tm * 8, LANES), jnp.int32)
    by_tile = jax.ShapeDtypeStruct(src_index.shape, jnp.int32)
    tile_at, lane_at, coef_at, source_at, block, column, coef_by, row_at, rank_at, *extra = pl.pallas_call(
        functools.partial(order_kernel, owners=tm, span=span, cap=share * LANES, seg_rows=seg_rows),
        out_shape=(
            places,
            places,
            jax.ShapeDtypeStruct((params, slots, LANES), F32),
            jax.ShapeDtypeStruct((slots, LANES), F32),
            by_owner,
            by_owner,
            jax.ShapeDtypeStruct((params, tm * 8, LANES), F32),
            by_tile,
            by_tile,
            jax.ShapeDtypeStruct(src_index.shape, F32),
            jax.ShapeDtypeStruct((tile_total, tm * seg_rows), F32),
            jax.ShapeDtypeStruct((tm * CAP_TILES, tile_total), F32),
            jax.ShapeDtypeStruct((tm * CAP_TILES, LANES), F32),
        ),
        in_specs=[SMEM] + [VMEM] * 4,
        out_specs=(VMEM,) * 13,
        scratch_shapes=[
            pltpu.VMEM((2 * slots, tile_total * LANES), BF16),
            pltpu.VMEM((LANES, tile_total * LANES), BF16),
        ],
        compiler_params=PARAMS,
        cost_estimate=cost(1.5),
        name="order",
    )(me, seg, count, index, coef)
    picked_shape = jax.ShapeDtypeStruct((tm * 8, LANES), F32)
    picked, tiles_held = pl.pallas_call(
        functools.partial(own_kernel, share=share),
        out_shape=(picked_shape, jax.ShapeDtypeStruct(tiles.shape, F32)),
        in_specs=[SMEM] + [VMEM] * 4 + [HBM],
        out_specs=(VMEM, VMEM),
        scratch_shapes=[pltpu.SemaphoreType.DMA],
        compiler_params=PARAMS,
        cost_estimate=cost(1.6),
        name="own",
    )(me, directions, block, column, coef_by, in_hbm(tiles))

    def pick(offsets, before):
        return pl.pallas_call(
            functools.partial(pick_kernel, offsets=offsets, share=share),
            out_shape=picked_shape,
            in_specs=[SMEM] + [VMEM] * (len(offsets) + 4),
            out_specs=VMEM,
            compiler_params=PARAMS,
            cost_estimate=cost(0.4 * len(offsets)),
            name="pick",
        )(me, *[tables[o] for o in offsets], block, column, coef_by, before)

    first_pair = swapped(passed([3], picked), "tm", tm, 1)
    tables[2] = first_pair[0]
    picked = pick([1, 3], picked)
    others = swapped(passed(far, picked), "tm", tm, 1)
    for q, offset in enumerate(far):
        tables[offset - 1] = others[q]
    picked = pick([2, *far], picked)
    late = [o - 1 for o in across[1:]]
    offsets = sorted(tables)
    grads_from = up8((params + 1) * share)
    depth = up8(grads_from + (folds + 1) * CAP_TILES + 1)
    projected, sent = pl.pallas_call(
        functools.partial(project_kernel, seg_rows=seg_rows, offsets=offsets, late=late),
        out_shape=(
            jax.ShapeDtypeStruct((tile_total, row_count), F32),
            jax.ShapeDtypeStruct((tm * depth, LANES), F32),
        ),
        in_specs=[SMEM] + [VMEM] * (16 + tm),
        out_specs=(VMEM, VMEM),
        scratch_shapes=[
            pltpu.VMEM((tm * seg_rows, folds * LANES), F32),
            pltpu.VMEM((tm * 8, LANES), F32),
        ],
        compiler_params=PARAMS,
        name="project",
    )(
        me,
        tiles_held,
        picked,
        weight,
        tile_at,
        lane_at,
        coef_at,
        source_at,
        block,
        column,
        coef_by,
        row_at,
        rank_at,
        *extra,
        *[tables[o] for o in offsets],
    )

    got = lax.all_to_all(sent.reshape(tm, depth, LANES), "tm", 0, 0).reshape(tm * depth, LANES)
    part_shape = jax.ShapeDtypeStruct((folds * seg_rows + 8, LANES), F32)
    part = pl.pallas_call(
        functools.partial(attitude_kernel, owners=tm, grads_from=grads_from, seg_rows=seg_rows, folds=folds),
        out_shape=part_shape,
        in_specs=[SMEM, VMEM],
        out_specs=VMEM,
        compiler_params=PARAMS,
        name="attitude",
    )(me, got)
    half = params * (span // WIDE)
    src_normal, projected, token = pl.pallas_call(
        functools.partial(source_kernel, owners=tm, share=share),
        out_shape=(
            jax.ShapeDtypeStruct((params, span), F32),
            jax.ShapeDtypeStruct((tile_total, row_count), F32),
            jax.ShapeDtypeStruct((8, LANES), F32),
        ),
        in_specs=[SMEM] + [VMEM] * 2,
        out_specs=(VMEM,) * 3,
        scratch_shapes=[
            pltpu.VMEM((2 * half, tile_total * LANES), BF16),
            pltpu.VMEM((WIDE, tile_total * LANES), BF16),
        ],
        compiler_params=PARAMS,
        cost_estimate=cost(2.0),
        name="source",
    )(me, got, projected)
    order = [*range(sky // 2, sky), *range(1, sky // 2)]
    others = [swapped(part, "sky", sky, offset) for offset in order]
    att_normal, curvature = pl.pallas_call(
        functools.partial(finish_kernel, seg_rows=seg_rows, folds=folds),
        out_shape=(
            jax.ShapeDtypeStruct((seg_rows, cols), F32),
            jax.ShapeDtypeStruct((1, 1), F32),
        ),
        in_specs=[VMEM] * (sky + 1),
        out_specs=(VMEM, SMEM),
        compiler_params=PARAMS,
        name="finish",
    )(part, *others, token)
    return projected, att_normal, src_normal, curvature.reshape(())


def solution(mesh):
    placed = (
        P(("sky", "tm"), None, None),
        P(("sky", "tm")),
        P(("sky", "tm")),
        P(("sky", "tm"), None),
        P(None, ("sky", "tm"), None),
        P(("sky", "tm"), None),
        P("tm", None),
        P(None, ("sky", "tm")),
    )
    return jax.shard_map(
        functools.partial(per_device, sky=mesh.shape["sky"], tm=mesh.shape["tm"]),
        mesh=mesh,
        in_specs=placed,
        out_specs=(P(("sky", "tm"), None), P("tm", None), P(None, ("sky", "tm")), P()),
        check_vma=False,
    )
```

```python
import functools

import jax
import jax.numpy as jnp
from jax import lax
from jax.experimental import pallas as pl
from jax.experimental.pallas import tpu as pltpu
from jax.sharding import PartitionSpec as P

LANES = 128
CAP_TILES = 4
WIDE = 256
NT = (((1,), (1,)), ((), ()))
F32 = jnp.float32
BF16 = jnp.bfloat16
VMEM = pl.BlockSpec(memory_space=pltpu.VMEM)
HBM = pl.BlockSpec(memory_space=pltpu.HBM)
SMEM = pl.BlockSpec(memory_space=pltpu.SMEM)
PARAMS = pltpu.CompilerParams(vmem_limit_bytes=16 * 1024 * 1024)


def up8(rows):
    return (rows + 7) // 8 * 8


def in_hbm(x):
    return pltpu.with_memory_space_constraint(x, pltpu.HBM)


def halves(x):
    high = x.astype(BF16)
    return high, (x - high.astype(F32)).astype(BF16)


def pack_kernel(source, attitude, *refs):
    small, (directions, *outs), (held, sems) = refs[:5], refs[5:11], refs[11:]
    params, span = source.shape
    seg_rows, cols = attitude.shape
    copies = [
        pltpu.make_async_copy(source, held, sems.at[0]),
        *[pltpu.make_async_copy(x, out, sems.at[1 + q]) for q, (x, out) in enumerate(zip(small, outs))],
    ]
    base = params * (span // LANES)
    for c in range(cols // LANES):
        copies.append(
            pltpu.make_async_copy(
                attitude.at[:, pl.ds(c * LANES, LANES)],
                directions.at[pl.ds(base + c * seg_rows, seg_rows), :],
                sems.at[6 + c],
            )
        )
    for copy in copies:
        copy.start()
    copies[0].wait()
    for b in range(span // LANES):
        directions[b * params : (b + 1) * params, :] = held[:, b * LANES : (b + 1) * LANES]
    for copy in copies[1:]:
        copy.wait()


def serve(owner, table, block, column, coef, total, share):
    params = coef.shape[0]
    blocks = (table.shape[0] // (params * 8)) * 8
    parts = 8 // share
    rows = pl.ds(pl.multiple_of(owner * 8, 8), 8)
    here, lane = block[rows, :], column[rows, :]
    part = lax.div(lax.broadcasted_iota(jnp.int32, here.shape, 0), share)
    picked = [jnp.zeros(here.shape, F32) for _ in range(params)]
    for b in range(blocks // parts):
        hit = here == b
        for k in range(params):
            line = None
            for p in range(parts):
                at = (p * (blocks // parts) + b) * params + k
                row = jnp.broadcast_to(table[at : at + 1, :], here.shape)
                line = row if line is None else jnp.where(part == p, row, line)
            picked[k] = jnp.where(hit, jnp.take_along_axis(line, lane, axis=1), picked[k])
    terms = jnp.zeros(here.shape, F32)
    for k in range(params):
        terms = terms + coef[k, rows, :] * picked[k]
    total[rows, :] = terms


def own_kernel(me, table, block, column, coef, tiles_in, total, tiles, pieces, sems, *, share):
    chunks = sems.shape[0]
    each = tiles.shape[0] // chunks
    copies = []
    for q in range(chunks):
        part = pl.ds(q * each, each)
        copies.append(pltpu.make_async_copy(tiles_in.at[part], tiles.at[part], sems.at[q]))
        copies[q].start()
    total[...] = jnp.zeros_like(total)
    serve(me[0], table, block, column, coef, total, share)
    for q in range(chunks):
        copies[q].wait()
        for t in range(q * each, (q + 1) * each):
            depth = tiles.shape[1]
            pieces[t, :depth, :], pieces[t, depth:, :] = halves(tiles[t])


def pick_kernel(*refs, offsets, share):
    me, *tables, block, column, coef, before, total = refs
    total[...] = before[...]
    for offset, table in zip(offsets, tables):
        serve(lax.bitwise_xor(me[0], offset), table, block, column, coef, total, share)


def pass_kernel(*refs, count):
    for q in range(count):
        refs[-1][q] = refs[q][...]


def order_kernel(me, seg, count, index, coef, *refs, owners, span, cap, seg_rows):
    tile_at, lane_at, coef_out, source_out, block, column, coef_by, row_at, rank_at, live, aim, fill, names, left, right = refs
    params, tile_total, _ = coef.shape
    slots = tile_at.shape[0]
    ids = index[...]
    owner = lax.div(ids, span)
    mask = jnp.concatenate([jnp.where(owner == o, 1.0, 0.0) for o in range(owners)], axis=0)
    rows = mask.shape[0]
    half = mask.astype(BF16)
    row_ids = lax.broadcasted_iota(jnp.int32, (LANES, LANES), 0)
    col_ids = lax.broadcasted_iota(jnp.int32, (LANES, LANES), 1)
    upper = jnp.where(row_ids < col_ids, 1.0, 0.0).astype(BF16)
    inside = jnp.dot(half, upper, preferred_element_type=F32)
    counts = jnp.dot(half, jnp.ones((LANES, LANES), BF16), preferred_element_type=F32)
    one = lax.broadcasted_iota(jnp.int32, (rows, rows), 0)
    two = lax.broadcasted_iota(jnp.int32, (rows, rows), 1)
    earlier = (lax.div(one, tile_total) == lax.div(two, tile_total)) & (two < one)
    earlier = jnp.where(earlier, 1.0, 0.0).astype(BF16)
    rank = inside + jnp.dot(earlier, counts.astype(BF16), preferred_element_type=F32)
    rank = mask * rank
    total = rank[:tile_total]
    for o in range(1, owners):
        total = total + rank[o * tile_total : (o + 1) * tile_total]
    place = total.astype(jnp.int32)
    row_at[...] = owner * 8 + lax.div(place, LANES)
    rank_at[...] = lax.rem(place, LANES)
    slot = owner * cap + place
    high = lax.div(slot, LANES).astype(F32)
    low = lax.rem(slot, LANES).astype(F32)
    high_ids = lax.broadcasted_iota(jnp.int32, (slots, LANES), 0).astype(BF16)
    low_ids = lax.broadcasted_iota(jnp.int32, (LANES, LANES), 0).astype(BF16)
    lanes = lax.broadcasted_iota(jnp.int32, (slots, LANES), 1).astype(BF16)
    unit, zero = jnp.ones((), BF16), jnp.zeros((), BF16)
    for t in range(tile_total):
        at = slice(t * LANES, (t + 1) * LANES)
        hit = high_ids == jnp.broadcast_to(high[t : t + 1], (slots, LANES)).astype(BF16)
        left[:slots, at] = jnp.where(hit, jnp.full((), t + 1, BF16), zero)
        left[slots:, at] = jnp.where(hit, lanes, zero)
        right[:, at] = jnp.where(
            low_ids == jnp.broadcast_to(low[t : t + 1], (LANES, LANES)).astype(BF16), unit, zero
        )
    place = lax.dot_general(left[...], right[...], NT, preferred_element_type=F32).astype(jnp.int32)
    tile, lane = place[:slots] - 1, place[slots:]
    tile_at[...] = tile
    lane_at[...] = lane
    ordered = [jnp.zeros((slots, LANES), F32) for _ in range(params)] + [jnp.full((slots, LANES), -1.0, F32)]
    for t in range(tile_total):
        hit = tile == t
        for k in range(params + 1):
            row = coef[k, t : t + 1, :] if k < params else ids[t : t + 1].astype(F32)
            found = jnp.take_along_axis(jnp.broadcast_to(row, (slots, LANES)), lane, axis=1)
            ordered[k] = jnp.where(hit, found, ordered[k])
    for k in range(params):
        coef_out[k] = ordered[k]
    source_out[...] = ordered[params]
    source = ordered[params].astype(jnp.int32)
    blocks, share = span // LANES, slots // owners
    parts = 8 // share
    within = jnp.where(source < 0, -blocks, lax.div(lax.rem(source, span), LANES))
    across = jnp.where(source < 0, 0, lax.rem(source, LANES))
    for o in range(owners):
        rows, mine = slice(o * 8, (o + 1) * 8), slice(o * share, (o + 1) * share)
        block[rows, :] = jnp.concatenate([within[mine] - p * (blocks // parts) for p in range(parts)], axis=0)
        column[rows, :] = jnp.concatenate([across[mine]] * parts, axis=0)
        for k in range(params):
            coef_by[k, rows, :] = jnp.concatenate([ordered[k][mine]] * parts, axis=0)
    square = (tile_total, tile_total)
    one = lax.broadcasted_iota(jnp.int32, square, 0)
    two = lax.broadcasted_iota(jnp.int32, square, 1)

    def down_of(row):
        return jnp.sum(jnp.where(one == two, jnp.broadcast_to(row, square), 0), axis=1, keepdims=True)

    along, down = seg[...], down_of(seg[...])
    owner_along, owner_down = lax.div(along, seg_rows), lax.div(down, seg_rows)
    live[...] = jnp.where(
        lax.broadcasted_iota(jnp.int32, ids.shape, 1) < jnp.broadcast_to(down_of(count[...]), ids.shape), 1.0, 0.0
    )
    line = lax.bitwise_xor(owner_down, me[0]) * seg_rows + lax.rem(down, seg_rows)
    aim[...] = jnp.where(
        lax.broadcasted_iota(jnp.int32, aim.shape, 1) == jnp.broadcast_to(line, aim.shape), 1.0, 0.0
    )
    same = jnp.broadcast_to(owner_down, square) == jnp.broadcast_to(owner_along, square)
    ranks = jnp.sum(jnp.where(same & (one < two), 1, 0), axis=0, keepdims=True)
    wide = (names.shape[0], tile_total)
    place = jnp.broadcast_to(owner_along * CAP_TILES + ranks, wide)
    filled = lax.broadcasted_iota(jnp.int32, wide, 0) == place
    ones = jnp.where(filled, 1.0, 0.0)
    for t in range(tile_total):
        fill[t] = jnp.broadcast_to(ones[:, t : t + 1], names.shape)
    named = jnp.sum(jnp.where(filled, jnp.broadcast_to(along + 1, wide), 0), axis=1, keepdims=True) - 1
    names[...] = jnp.broadcast_to(named, names.shape).astype(F32)


def project_kernel(*refs, seg_rows, offsets, late):
    me, tiles, pieces, before, weight, tile_at, lane_at, coef_at, source_at, *refs = refs
    block, column, coef_by, row_at, rank_at, live, aim, fill, names, *refs = refs
    tables, refs = refs[: len(offsets)], refs[len(offsets) :]
    projected, sent, lines, served = refs
    params, tile_total, width = coef_at.shape[0], *weight.shape
    share = tile_at.shape[0] // len(offsets)
    folds = tiles.shape[2] // LANES
    base = tables[0].shape[0] - folds * seg_rows
    served[...] = before[...]
    for offset, table in zip(offsets, tables):
        for c in range(folds):
            lines[offset * seg_rows : (offset + 1) * seg_rows, c * LANES : (c + 1) * LANES] = table[
                base + c * seg_rows : base + (c + 1) * seg_rows, :
            ]
        if offset in late:
            serve(lax.bitwise_xor(me[0], offset), table, block, column, coef_by, served, share)
    shape = weight.shape
    row, rank = row_at[...], rank_at[...]
    total = jnp.zeros(shape, F32)
    for o in range(len(offsets)):
        for h in range(share):
            line = served[o * 8 + h : o * 8 + h + 1, :]
            for p in range(1, 8 // share):
                at = o * 8 + p * share + h
                line = line + served[at : at + 1, :]
            found = jnp.take_along_axis(jnp.broadcast_to(line, shape), rank, axis=1)
            total = jnp.where(row == o * 8 + h, found, total)
    hit = aim[...].astype(BF16)
    directions = jnp.zeros((tile_total, folds * LANES), F32)
    for piece in halves(lines[...]):
        directions = directions + jnp.dot(hit, piece, preferred_element_type=F32)
    row_ids = lax.broadcasted_iota(jnp.int32, shape, 0)
    tile_part = jnp.zeros(shape, F32)
    for t in range(tile_total):
        folded = None
        for c in range(folds):
            part = slice(c * LANES, (c + 1) * LANES)
            product = tiles[t, :, part] * directions[t : t + 1, part]
            folded = product if folded is None else folded + product
        tile_part = jnp.where(row_ids == t, jnp.sum(folded.T, axis=0, keepdims=True), tile_part)
    total = total + tile_part
    value = jnp.where(live[...] > 0.5, total, 0.0)
    weighted = weight[...] * value
    projected[...] = value
    owners = len(offsets)
    slots = tile_at.shape[0]
    depth = sent.shape[0] // owners
    tile, lane = tile_at[...], lane_at[...]
    ordered = jnp.zeros(tile.shape, F32)
    for t in range(tile_total):
        row = jnp.broadcast_to(weighted[t : t + 1], tile.shape)
        ordered = jnp.where(tile == t, jnp.take_along_axis(row, lane, axis=1), ordered)
    grads_from = up8((params + 1) * share)
    names_from = grads_from + folds * CAP_TILES
    curve = jnp.sum(value * weighted, axis=0, keepdims=True)
    for k in range(params + 1):
        values = coef_at[k] * ordered if k < params else source_at[...]
        for o in range(owners):
            sent[pl.ds(o * depth + k * share, share), :] = values[o * share : (o + 1) * share]
    high, low = (x.astype(F32) for x in halves(weighted))
    places = fill.shape[1]
    nothing = jnp.zeros((places, LANES), BF16)
    sums = jnp.zeros((2 * places, folds * LANES), F32)
    for t in range(tile_total):
        mask = fill[t]
        one = (mask * high[t : t + 1]).astype(BF16)
        two = (mask * low[t : t + 1]).astype(BF16)
        left = jnp.concatenate(
            [jnp.concatenate([one, one], axis=1), jnp.concatenate([two, nothing], axis=1)], axis=0
        )
        sums = sums + jnp.dot(left, pieces[t], preferred_element_type=F32)
    placed = sums[:places] + sums[places:]
    for o in range(owners):
        rows = slice(o * CAP_TILES, (o + 1) * CAP_TILES)
        for c in range(folds):
            sent[pl.ds(o * depth + grads_from + c * CAP_TILES, CAP_TILES), :] = placed[rows, c * LANES : (c + 1) * LANES]
        sent[pl.ds(o * depth + names_from, CAP_TILES), :] = names[rows, :]
        sent[pl.ds(o * depth + names_from + CAP_TILES, 1), :] = curve


def attitude_kernel(me, got, part, *, owners, grads_from, seg_rows, folds):
    depth = got.shape[0] // owners
    names_from = grads_from + folds * CAP_TILES
    lane = lax.broadcasted_iota(jnp.int32, (owners, LANES), 1)
    first = me[0] * seg_rows
    hits, grads = [], [[] for _ in range(folds)]
    for r in range(CAP_TILES):
        name = got[pl.ds(names_from + r, owners, stride=depth), :].astype(jnp.int32)
        hits.append(jnp.where(name - first == lane, 1.0, 0.0))
        for c in range(folds):
            grads[c].append(got[pl.ds(grads_from + c * CAP_TILES + r, owners, stride=depth), :])
    pick = jnp.concatenate(hits, axis=0).T[:seg_rows].astype(BF16)
    for c in range(folds):
        total = jnp.zeros((seg_rows, LANES), F32)
        for piece in halves(jnp.concatenate(grads[c], axis=0)):
            total = total + jnp.dot(pick, piece, preferred_element_type=F32)
        part[pl.ds(c * seg_rows, seg_rows), :] = total
    curve = got[pl.ds(names_from + CAP_TILES, owners, stride=depth), :]
    whole = jnp.sum(jnp.sum(curve, axis=0, keepdims=True), axis=1, keepdims=True)
    part[pl.ds(folds * seg_rows, 8), :] = jnp.broadcast_to(whole, (8, LANES))


def source_kernel(me, got, held, out, kept, token, left, right, *, owners, share):
    params, span = out.shape
    depth = got.shape[0] // owners
    kept[...] = held[...]
    token[...] = jnp.zeros_like(token)
    high_total = span // WIDE
    high_ids = lax.broadcasted_iota(jnp.int32, (high_total, LANES), 0).astype(BF16)
    low_ids = lax.broadcasted_iota(jnp.int32, (WIDE, LANES), 0).astype(BF16)
    one, zero = jnp.ones((), BF16), jnp.zeros((), BF16)
    half = params * high_total
    group = right.shape[1] // LANES
    places = [o * depth + h for o in range(owners) for h in range(share)]
    total = jnp.zeros((2 * half, WIDE), F32)
    for g in range(0, len(places), group):
        for t, place in enumerate(places[g : g + group]):
            at = slice(t * LANES, (t + 1) * LANES)
            rows = [got[place + k * share : place + k * share + 1, :] for k in range(params + 1)]
            local = rows[params].astype(jnp.int32) - me[0] * span
            high = lax.shift_right_arithmetic(local, 8)
            high = jnp.where((high >= 0) & (high < high_total), high, high_total).astype(F32)
            low = lax.bitwise_and(local, WIDE - 1).astype(F32)
            low = jnp.broadcast_to(low, (WIDE, LANES)).astype(BF16)
            right[:, at] = jnp.where(low_ids == low, one, zero)
            hit = high_ids == jnp.broadcast_to(high, (high_total, LANES)).astype(BF16)
            for k in range(params):
                for p, piece in enumerate(halves(jnp.broadcast_to(rows[k], (high_total, LANES)))):
                    row = p * half + k * high_total
                    left[row : row + high_total, at] = jnp.where(hit, piece, zero)
        total = total + lax.dot_general(left[...], right[...], NT, preferred_element_type=F32)
    for k in range(params):
        for h in range(high_total):
            row = k * high_total + h
            out[k : k + 1, h * WIDE : (h + 1) * WIDE] = total[row : row + 1, :] + total[half + row : half + row + 1, :]


def finish_kernel(*refs, seg_rows, folds):
    *parts, _, normal, curvature = refs
    total = parts[0][...]
    for part in parts[1:]:
        total = total + part[...]
    for c in range(folds):
        normal[:, c * LANES : (c + 1) * LANES] = total[c * seg_rows : (c + 1) * seg_rows]
    curvature[0, 0] = total[folds * seg_rows, 0]


def cost(microseconds):
    return pl.CostEstimate(flops=int(microseconds * 1e9), bytes_accessed=1, transcendentals=0)


def swapped(x, axis, size, offset):
    return lax.ppermute(x, axis, [(i, i ^ offset) for i in range(size)])


def per_device(tiles, tile_seg, tile_count, src_index, src_coef, obs_weight, att_dir, src_dir, *, sky, tm):
    tile_total, row_count, cols = tiles.shape
    params, span = src_dir.shape
    seg_rows = att_dir.shape[0]
    folds = cols // LANES
    across = [*range(tm - 1, 2, -2)]
    me = lax.axis_index("tm").astype(jnp.int32).reshape(1)

    directions, index, coef, weight, seg, count = pl.pallas_call(
        pack_kernel,
        out_shape=(
            jax.ShapeDtypeStruct((params * (span // LANES) + folds * seg_rows, LANES), F32),
            jax.ShapeDtypeStruct(src_index.shape, src_index.dtype),
            jax.ShapeDtypeStruct(src_coef.shape, F32),
            jax.ShapeDtypeStruct(obs_weight.shape, F32),
            jax.ShapeDtypeStruct((1, tile_total), jnp.int32),
            jax.ShapeDtypeStruct((1, tile_total), jnp.int32),
        ),
        in_specs=[HBM] * 7,
        out_specs=(VMEM,) * 6,
        scratch_shapes=[pltpu.VMEM((params, span), F32), pltpu.SemaphoreType.DMA((6 + folds,))],
        compiler_params=PARAMS,
        name="pack",
    )(*map(in_hbm, (src_dir, att_dir, src_index, src_coef, obs_weight, *(x.reshape(1, -1) for x in (tile_seg, tile_count)))))

    far = list(across[1:])
    tables = {0: directions}
    for offset in across:
        tables[offset] = swapped(directions, "tm", tm, offset)
    tables[1] = swapped(directions, "tm", tm, 1)

    def passed(offsets, after):
        return pl.pallas_call(
            functools.partial(pass_kernel, count=len(offsets)),
            out_shape=jax.ShapeDtypeStruct((len(offsets), *directions.shape), F32),
            in_specs=[VMEM] * (len(offsets) + 1),
            out_specs=VMEM,
            compiler_params=PARAMS,
            name="pass",
        )(*[tables[o] for o in offsets], after)

    slots = 2 * tile_total
    share = slots // tm
    places = jax.ShapeDtypeStruct((slots, LANES), jnp.int32)
    by_owner = jax.ShapeDtypeStruct((tm * 8, LANES), jnp.int32)
    by_tile = jax.ShapeDtypeStruct(src_index.shape, jnp.int32)
    tile_at, lane_at, coef_at, source_at, block, column, coef_by, row_at, rank_at, *extra = pl.pallas_call(
        functools.partial(order_kernel, owners=tm, span=span, cap=share * LANES, seg_rows=seg_rows),
        out_shape=(
            places,
            places,
            jax.ShapeDtypeStruct((params, slots, LANES), F32),
            jax.ShapeDtypeStruct((slots, LANES), F32),
            by_owner,
            by_owner,
            jax.ShapeDtypeStruct((params, tm * 8, LANES), F32),
            by_tile,
            by_tile,
            jax.ShapeDtypeStruct(src_index.shape, F32),
            jax.ShapeDtypeStruct((tile_total, tm * seg_rows), F32),
            jax.ShapeDtypeStruct((tile_total, tm * CAP_TILES, LANES), F32),
            jax.ShapeDtypeStruct((tm * CAP_TILES, LANES), F32),
        ),
        in_specs=[SMEM] + [VMEM] * 4,
        out_specs=(VMEM,) * 13,
        scratch_shapes=[
            pltpu.VMEM((2 * slots, tile_total * LANES), BF16),
            pltpu.VMEM((LANES, tile_total * LANES), BF16),
        ],
        compiler_params=PARAMS,
        cost_estimate=cost(1.5),
        name="order",
    )(me, seg, count, index, coef)
    picked_shape = jax.ShapeDtypeStruct((tm * 8, LANES), F32)
    picked, tiles_held, pieces = pl.pallas_call(
        functools.partial(own_kernel, share=share),
        out_shape=(picked_shape, jax.ShapeDtypeStruct(tiles.shape, F32), jax.ShapeDtypeStruct((tile_total, 2 * row_count, cols), BF16)),
        in_specs=[SMEM] + [VMEM] * 4 + [HBM],
        out_specs=(VMEM,) * 3,
        scratch_shapes=[pltpu.SemaphoreType.DMA((4,))],
        compiler_params=PARAMS,
        cost_estimate=cost(1.6),
        name="own",
    )(me, directions, block, column, coef_by, in_hbm(tiles))

    def pick(offsets, before):
        return pl.pallas_call(
            functools.partial(pick_kernel, offsets=offsets, share=share),
            out_shape=picked_shape,
            in_specs=[SMEM] + [VMEM] * (len(offsets) + 4),
            out_specs=VMEM,
            compiler_params=PARAMS,
            cost_estimate=cost(0.4 * len(offsets)),
            name="pick",
        )(me, *[tables[o] for o in offsets], block, column, coef_by, before)

    first_pair = swapped(passed(across[:1], picked), "tm", tm, 1)
    tables[across[0] - 1] = first_pair[0]
    picked = pick([1, across[0]], picked)
    others = swapped(passed(far, picked), "tm", tm, 1)
    for q, offset in enumerate(far):
        tables[offset - 1] = others[q]
    picked = pick([across[0] - 1, *far], picked)
    late = [o - 1 for o in across[1:]]
    offsets = sorted(tables)
    grads_from = up8((params + 1) * share)
    depth = up8(grads_from + (folds + 1) * CAP_TILES + 1)
    projected, sent = pl.pallas_call(
        functools.partial(project_kernel, seg_rows=seg_rows, offsets=offsets, late=late),
        out_shape=(
            jax.ShapeDtypeStruct((tile_total, row_count), F32),
            jax.ShapeDtypeStruct((tm * depth, LANES), F32),
        ),
        in_specs=[SMEM] + [VMEM] * (17 + tm),
        out_specs=(VMEM, VMEM),
        scratch_shapes=[
            pltpu.VMEM((tm * seg_rows, folds * LANES), F32),
            pltpu.VMEM((tm * 8, LANES), F32),
        ],
        compiler_params=PARAMS,
        name="project",
    )(
        me,
        tiles_held,
        pieces,
        picked,
        weight,
        tile_at,
        lane_at,
        coef_at,
        source_at,
        block,
        column,
        coef_by,
        row_at,
        rank_at,
        *extra,
        *[tables[o] for o in offsets],
    )

    got = lax.all_to_all(sent.reshape(tm, depth, LANES), "tm", 0, 0).reshape(tm * depth, LANES)
    part_shape = jax.ShapeDtypeStruct((folds * seg_rows + 8, LANES), F32)
    part = pl.pallas_call(
        functools.partial(attitude_kernel, owners=tm, grads_from=grads_from, seg_rows=seg_rows, folds=folds),
        out_shape=part_shape,
        in_specs=[SMEM, VMEM],
        out_specs=VMEM,
        compiler_params=PARAMS,
        name="attitude",
    )(me, got)
    half = params * (span // WIDE)
    src_normal, projected, token = pl.pallas_call(
        functools.partial(source_kernel, owners=tm, share=share),
        out_shape=(
            jax.ShapeDtypeStruct((params, span), F32),
            jax.ShapeDtypeStruct((tile_total, row_count), F32),
            jax.ShapeDtypeStruct((8, LANES), F32),
        ),
        in_specs=[SMEM] + [VMEM] * 2,
        out_specs=(VMEM,) * 3,
        scratch_shapes=[
            pltpu.VMEM((2 * half, tile_total * LANES), BF16),
            pltpu.VMEM((WIDE, tile_total * LANES), BF16),
        ],
        compiler_params=PARAMS,
        cost_estimate=cost(2.0),
        name="source",
    )(me, got, projected)
    order = [*range(sky // 2, sky), *range(1, sky // 2)]
    others = [swapped(part, "sky", sky, offset) for offset in order]
    att_normal, curvature = pl.pallas_call(
        functools.partial(finish_kernel, seg_rows=seg_rows, folds=folds),
        out_shape=(
            jax.ShapeDtypeStruct((seg_rows, cols), F32),
            jax.ShapeDtypeStruct((1, 1), F32),
        ),
        in_specs=[VMEM] * (sky + 1),
        out_specs=(VMEM, SMEM),
        compiler_params=PARAMS,
        name="finish",
    )(part, *others, token)
    return projected, att_normal, src_normal, curvature.reshape(())


def solution(mesh):
    placed = (
        P(("sky", "tm"), None, None),
        P(("sky", "tm")),
        P(("sky", "tm")),
        P(("sky", "tm"), None),
        P(None, ("sky", "tm"), None),
        P(("sky", "tm"), None),
        P("tm", None),
        P(None, ("sky", "tm")),
    )
    return jax.shard_map(
        functools.partial(per_device, sky=mesh.shape["sky"], tm=mesh.shape["tm"]),
        mesh=mesh,
        in_specs=placed,
        out_specs=(P(("sky", "tm"), None), P("tm", None), P(None, ("sky", "tm")), P()),
        check_vma=False,
    )
```

```python
import functools

import jax
import jax.numpy as jnp
from jax import lax
from jax.experimental import pallas as pl
from jax.experimental.pallas import tpu as pltpu
from jax.sharding import PartitionSpec as P

LANES = 128
CAP_TILES = 4
WIDE = 256
NT = (((1,), (1,)), ((), ()))
F32 = jnp.float32
BF16 = jnp.bfloat16
VMEM = pl.BlockSpec(memory_space=pltpu.VMEM)
HBM = pl.BlockSpec(memory_space=pltpu.HBM)
SMEM = pl.BlockSpec(memory_space=pltpu.SMEM)
PARAMS = pltpu.CompilerParams(vmem_limit_bytes=16 * 1024 * 1024)


def up8(rows):
    return (rows + 7) // 8 * 8


def in_hbm(x):
    return pltpu.with_memory_space_constraint(x, pltpu.HBM)


def halves(x):
    high = x.astype(BF16)
    return high, (x - high.astype(F32)).astype(BF16)


def pack_kernel(source, attitude, *refs):
    small, (directions, *outs), (held, sems) = refs[:5], refs[5:11], refs[11:]
    params, span = source.shape
    seg_rows, cols = attitude.shape
    copies = [
        pltpu.make_async_copy(source, held, sems.at[0]),
        *[pltpu.make_async_copy(x, out, sems.at[1 + q]) for q, (x, out) in enumerate(zip(small, outs))],
    ]
    base = params * (span // LANES)
    for c in range(cols // LANES):
        copies.append(
            pltpu.make_async_copy(
                attitude.at[:, pl.ds(c * LANES, LANES)],
                directions.at[pl.ds(base + c * seg_rows, seg_rows), :],
                sems.at[6 + c],
            )
        )
    for copy in copies:
        copy.start()
    copies[0].wait()
    for b in range(span // LANES):
        directions[b * params : (b + 1) * params, :] = held[:, b * LANES : (b + 1) * LANES]
    for copy in copies[1:]:
        copy.wait()


def serve(owner, table, block, column, coef, total, share):
    params = coef.shape[0]
    blocks = (table.shape[0] // (params * 8)) * 8
    parts = 8 // share
    rows = pl.ds(pl.multiple_of(owner * 8, 8), 8)
    here, lane = block[rows, :], column[rows, :]
    part = lax.div(lax.broadcasted_iota(jnp.int32, here.shape, 0), share)
    picked = [jnp.zeros(here.shape, F32) for _ in range(params)]
    for b in range(blocks // parts):
        hit = here == b
        for k in range(params):
            line = None
            for p in range(parts):
                at = (p * (blocks // parts) + b) * params + k
                row = jnp.broadcast_to(table[at : at + 1, :], here.shape)
                line = row if line is None else jnp.where(part == p, row, line)
            picked[k] = jnp.where(hit, jnp.take_along_axis(line, lane, axis=1), picked[k])
    terms = jnp.zeros(here.shape, F32)
    for k in range(params):
        terms = terms + coef[k, rows, :] * picked[k]
    total[rows, :] = terms


def own_kernel(me, table, block, column, coef, tiles_in, total, tiles, pieces, sems, *, share):
    chunks = sems.shape[0]
    each = tiles.shape[0] // chunks
    copies = []
    for q in range(chunks):
        part = pl.ds(q * each, each)
        copies.append(pltpu.make_async_copy(tiles_in.at[part], tiles.at[part], sems.at[q]))
        copies[q].start()
    total[...] = jnp.zeros_like(total)
    serve(me[0], table, block, column, coef, total, share)
    for q in range(chunks):
        copies[q].wait()
        for t in range(q * each, (q + 1) * each):
            depth = tiles.shape[1]
            pieces[t, :depth, :], pieces[t, depth:, :] = halves(tiles[t])


def pick_kernel(*refs, offsets, share):
    me, *tables, block, column, coef, before, total = refs
    total[...] = before[...]
    for offset, table in zip(offsets, tables):
        serve(lax.bitwise_xor(me[0], offset), table, block, column, coef, total, share)


def pass_kernel(*refs, count):
    for q in range(count):
        refs[-1][q] = refs[q][...]


def order_kernel(me, seg, count, index, coef, *refs, owners, span, cap, seg_rows):
    tile_at, lane_at, coef_out, source_out, block, column, coef_by, row_at, rank_at, live, aim, fill, names, left, right = refs
    params, tile_total, _ = coef.shape
    slots = tile_at.shape[0]
    ids = index[...]
    owner = lax.div(ids, span)
    mask = jnp.concatenate([jnp.where(owner == o, 1.0, 0.0) for o in range(owners)], axis=0)
    rows = mask.shape[0]
    half = mask.astype(BF16)
    row_ids = lax.broadcasted_iota(jnp.int32, (LANES, LANES), 0)
    col_ids = lax.broadcasted_iota(jnp.int32, (LANES, LANES), 1)
    upper = jnp.where(row_ids < col_ids, 1.0, 0.0).astype(BF16)
    inside = jnp.dot(half, upper, preferred_element_type=F32)
    counts = jnp.dot(half, jnp.ones((LANES, LANES), BF16), preferred_element_type=F32)
    one = lax.broadcasted_iota(jnp.int32, (rows, rows), 0)
    two = lax.broadcasted_iota(jnp.int32, (rows, rows), 1)
    earlier = (lax.div(one, tile_total) == lax.div(two, tile_total)) & (two < one)
    earlier = jnp.where(earlier, 1.0, 0.0).astype(BF16)
    rank = inside + jnp.dot(earlier, counts.astype(BF16), preferred_element_type=F32)
    rank = mask * rank
    total = rank[:tile_total]
    for o in range(1, owners):
        total = total + rank[o * tile_total : (o + 1) * tile_total]
    place = total.astype(jnp.int32)
    row_at[...] = owner * 8 + lax.div(place, LANES)
    rank_at[...] = lax.rem(place, LANES)
    slot = owner * cap + place
    high = lax.div(slot, LANES).astype(F32)
    low = lax.rem(slot, LANES).astype(F32)
    high_ids = lax.broadcasted_iota(jnp.int32, (slots, LANES), 0).astype(BF16)
    low_ids = lax.broadcasted_iota(jnp.int32, (LANES, LANES), 0).astype(BF16)
    lanes = lax.broadcasted_iota(jnp.int32, (slots, LANES), 1).astype(BF16)
    unit, zero = jnp.ones((), BF16), jnp.zeros((), BF16)
    for t in range(tile_total):
        at = slice(t * LANES, (t + 1) * LANES)
        hit = high_ids == jnp.broadcast_to(high[t : t + 1], (slots, LANES)).astype(BF16)
        left[:slots, at] = jnp.where(hit, jnp.full((), t + 1, BF16), zero)
        left[slots:, at] = jnp.where(hit, lanes, zero)
        right[:, at] = jnp.where(
            low_ids == jnp.broadcast_to(low[t : t + 1], (LANES, LANES)).astype(BF16), unit, zero
        )
    place = lax.dot_general(left[...], right[...], NT, preferred_element_type=F32).astype(jnp.int32)
    tile, lane = place[:slots] - 1, place[slots:]
    tile_at[...] = tile
    lane_at[...] = lane
    ordered = [jnp.zeros((slots, LANES), F32) for _ in range(params)] + [jnp.full((slots, LANES), -1.0, F32)]
    for t in range(tile_total):
        hit = tile == t
        for k in range(params + 1):
            row = coef[k, t : t + 1, :] if k < params else ids[t : t + 1].astype(F32)
            found = jnp.take_along_axis(jnp.broadcast_to(row, (slots, LANES)), lane, axis=1)
            ordered[k] = jnp.where(hit, found, ordered[k])
    for k in range(params):
        coef_out[k] = ordered[k]
    source_out[...] = ordered[params]
    source = ordered[params].astype(jnp.int32)
    blocks, share = span // LANES, slots // owners
    parts = 8 // share
    within = jnp.where(source < 0, -blocks, lax.div(lax.rem(source, span), LANES))
    across = jnp.where(source < 0, 0, lax.rem(source, LANES))
    for o in range(owners):
        rows, mine = slice(o * 8, (o + 1) * 8), slice(o * share, (o + 1) * share)
        block[rows, :] = jnp.concatenate([within[mine] - p * (blocks // parts) for p in range(parts)], axis=0)
        column[rows, :] = jnp.concatenate([across[mine]] * parts, axis=0)
        for k in range(params):
            coef_by[k, rows, :] = jnp.concatenate([ordered[k][mine]] * parts, axis=0)
    square = (tile_total, tile_total)
    one = lax.broadcasted_iota(jnp.int32, square, 0)
    two = lax.broadcasted_iota(jnp.int32, square, 1)

    def down_of(row):
        return jnp.sum(jnp.where(one == two, jnp.broadcast_to(row, square), 0), axis=1, keepdims=True)

    along, down = seg[...], down_of(seg[...])
    owner_along, owner_down = lax.div(along, seg_rows), lax.div(down, seg_rows)
    live[...] = jnp.where(
        lax.broadcasted_iota(jnp.int32, ids.shape, 1) < jnp.broadcast_to(down_of(count[...]), ids.shape), 1.0, 0.0
    )
    line = lax.bitwise_xor(owner_down, me[0]) * seg_rows + lax.rem(down, seg_rows)
    aim[...] = jnp.where(
        lax.broadcasted_iota(jnp.int32, aim.shape, 1) == jnp.broadcast_to(line, aim.shape), 1.0, 0.0
    )
    same = jnp.broadcast_to(owner_down, square) == jnp.broadcast_to(owner_along, square)
    ranks = jnp.sum(jnp.where(same & (one < two), 1, 0), axis=0, keepdims=True)
    wide = (names.shape[0], tile_total)
    place = jnp.broadcast_to(owner_along * CAP_TILES + ranks, wide)
    filled = lax.broadcasted_iota(jnp.int32, wide, 0) == place
    ones = jnp.where(filled, 1.0, 0.0)
    for t in range(tile_total):
        fill[t] = jnp.broadcast_to(ones[:, t : t + 1], names.shape)
    named = jnp.sum(jnp.where(filled, jnp.broadcast_to(along + 1, wide), 0), axis=1, keepdims=True) - 1
    names[...] = jnp.broadcast_to(named, names.shape).astype(F32)


def project_kernel(*refs, seg_rows, offsets, late):
    me, tiles, pieces, before, weight, tile_at, lane_at, coef_at, source_at, *refs = refs
    block, column, coef_by, row_at, rank_at, live, aim, fill, names, *refs = refs
    tables, refs = refs[: len(offsets)], refs[len(offsets) :]
    projected, sent, lines, served = refs
    params, tile_total, width = coef_at.shape[0], *weight.shape
    share = tile_at.shape[0] // len(offsets)
    folds = tiles.shape[2] // LANES
    base = tables[0].shape[0] - folds * seg_rows
    served[...] = before[...]
    for offset, table in zip(offsets, tables):
        for c in range(folds):
            lines[offset * seg_rows : (offset + 1) * seg_rows, c * LANES : (c + 1) * LANES] = table[
                base + c * seg_rows : base + (c + 1) * seg_rows, :
            ]
        if offset in late:
            serve(lax.bitwise_xor(me[0], offset), table, block, column, coef_by, served, share)
    shape = weight.shape
    row, rank = row_at[...], rank_at[...]
    total = jnp.zeros(shape, F32)
    for o in range(len(offsets)):
        for h in range(share):
            line = served[o * 8 + h : o * 8 + h + 1, :]
            for p in range(1, 8 // share):
                at = o * 8 + p * share + h
                line = line + served[at : at + 1, :]
            found = jnp.take_along_axis(jnp.broadcast_to(line, shape), rank, axis=1)
            total = jnp.where(row == o * 8 + h, found, total)
    hit = aim[...].astype(BF16)
    directions = jnp.zeros((tile_total, folds * LANES), F32)
    for piece in halves(lines[...]):
        directions = directions + jnp.dot(hit, piece, preferred_element_type=F32)
    row_ids = lax.broadcasted_iota(jnp.int32, shape, 0)
    tile_part = jnp.zeros(shape, F32)
    for t in range(tile_total):
        folded = None
        for c in range(folds):
            part = slice(c * LANES, (c + 1) * LANES)
            product = tiles[t, :, part] * directions[t : t + 1, part]
            folded = product if folded is None else folded + product
        tile_part = jnp.where(row_ids == t, jnp.sum(folded.T, axis=0, keepdims=True), tile_part)
    total = total + tile_part
    value = jnp.where(live[...] > 0.5, total, 0.0)
    weighted = weight[...] * value
    projected[...] = value
    owners = len(offsets)
    slots = tile_at.shape[0]
    depth = sent.shape[0] // owners
    tile, lane = tile_at[...], lane_at[...]
    ordered = jnp.zeros(tile.shape, F32)
    for t in range(tile_total):
        row = jnp.broadcast_to(weighted[t : t + 1], tile.shape)
        ordered = jnp.where(tile == t, jnp.take_along_axis(row, lane, axis=1), ordered)
    grads_from = up8((params + 1) * share)
    names_from = grads_from + folds * CAP_TILES
    curve = jnp.sum(value * weighted, axis=0, keepdims=True)
    for k in range(params + 1):
        values = coef_at[k] * ordered if k < params else source_at[...]
        for o in range(owners):
            sent[pl.ds(o * depth + k * share, share), :] = values[o * share : (o + 1) * share]
    high, low = (x.astype(F32) for x in halves(weighted))
    places = fill.shape[1]
    nothing = jnp.zeros((places, LANES), BF16)
    sums = jnp.zeros((2 * places, folds * LANES), F32)
    for t in range(tile_total):
        mask = fill[t]
        one = (mask * high[t : t + 1]).astype(BF16)
        two = (mask * low[t : t + 1]).astype(BF16)
        left = jnp.concatenate(
            [jnp.concatenate([one, one], axis=1), jnp.concatenate([two, nothing], axis=1)], axis=0
        )
        sums = sums + jnp.dot(left, pieces[t], preferred_element_type=F32)
    placed = sums[:places] + sums[places:]
    for o in range(owners):
        rows = slice(o * CAP_TILES, (o + 1) * CAP_TILES)
        for c in range(folds):
            sent[pl.ds(o * depth + grads_from + c * CAP_TILES, CAP_TILES), :] = placed[rows, c * LANES : (c + 1) * LANES]
        sent[pl.ds(o * depth + names_from, CAP_TILES), :] = names[rows, :]
        sent[pl.ds(o * depth + names_from + CAP_TILES, 1), :] = curve


def attitude_kernel(me, got, part, *, owners, grads_from, seg_rows, folds):
    depth = got.shape[0] // owners
    names_from = grads_from + folds * CAP_TILES
    lane = lax.broadcasted_iota(jnp.int32, (owners, LANES), 1)
    first = me[0] * seg_rows
    hits, grads = [], [[] for _ in range(folds)]
    for r in range(CAP_TILES):
        name = got[pl.ds(names_from + r, owners, stride=depth), :].astype(jnp.int32)
        hits.append(jnp.where(name - first == lane, 1.0, 0.0))
        for c in range(folds):
            grads[c].append(got[pl.ds(grads_from + c * CAP_TILES + r, owners, stride=depth), :])
    pick = jnp.concatenate(hits, axis=0).T[:seg_rows].astype(BF16)
    for c in range(folds):
        total = jnp.zeros((seg_rows, LANES), F32)
        for piece in halves(jnp.concatenate(grads[c], axis=0)):
            total = total + jnp.dot(pick, piece, preferred_element_type=F32)
        part[pl.ds(c * seg_rows, seg_rows), :] = total
    curve = got[pl.ds(names_from + CAP_TILES, owners, stride=depth), :]
    whole = jnp.sum(jnp.sum(curve, axis=0, keepdims=True), axis=1, keepdims=True)
    part[pl.ds(folds * seg_rows, 8), :] = jnp.broadcast_to(whole, (8, LANES))


def source_kernel(me, got, held, out, kept, token, left, right, *, owners, share):
    params, span = out.shape
    depth = got.shape[0] // owners
    kept[...] = held[...]
    token[...] = jnp.zeros_like(token)
    high_total = span // WIDE
    high_ids = lax.broadcasted_iota(jnp.int32, (high_total, LANES), 0).astype(BF16)
    low_ids = lax.broadcasted_iota(jnp.int32, (WIDE, LANES), 0).astype(BF16)
    one, zero = jnp.ones((), BF16), jnp.zeros((), BF16)
    half = params * high_total
    group = right.shape[1] // LANES
    places = [o * depth + h for o in range(owners) for h in range(share)]
    total = jnp.zeros((2 * half, WIDE), F32)
    for g in range(0, len(places), group):
        for t, place in enumerate(places[g : g + group]):
            at = slice(t * LANES, (t + 1) * LANES)
            rows = [got[place + k * share : place + k * share + 1, :] for k in range(params + 1)]
            local = rows[params].astype(jnp.int32) - me[0] * span
            high = lax.shift_right_arithmetic(local, 8)
            high = jnp.where((high >= 0) & (high < high_total), high, high_total).astype(F32)
            low = lax.bitwise_and(local, WIDE - 1).astype(F32)
            low = jnp.broadcast_to(low, (WIDE, LANES)).astype(BF16)
            right[:, at] = jnp.where(low_ids == low, one, zero)
            hit = high_ids == jnp.broadcast_to(high, (high_total, LANES)).astype(BF16)
            for k in range(params):
                for p, piece in enumerate(halves(jnp.broadcast_to(rows[k], (high_total, LANES)))):
                    row = p * half + k * high_total
                    left[row : row + high_total, at] = jnp.where(hit, piece, zero)
        total = total + lax.dot_general(left[...], right[...], NT, preferred_element_type=F32)
    for k in range(params):
        for h in range(high_total):
            row = k * high_total + h
            out[k : k + 1, h * WIDE : (h + 1) * WIDE] = total[row : row + 1, :] + total[half + row : half + row + 1, :]


def finish_kernel(*refs, seg_rows, folds):
    *parts, _, normal, curvature = refs
    total = parts[0][...]
    for part in parts[1:]:
        total = total + part[...]
    for c in range(folds):
        normal[:, c * LANES : (c + 1) * LANES] = total[c * seg_rows : (c + 1) * seg_rows]
    curvature[0, 0] = total[folds * seg_rows, 0]


def cost(microseconds):
    return pl.CostEstimate(flops=int(microseconds * 1e9), bytes_accessed=1, transcendentals=0)


def swapped(x, axis, size, offset):
    return lax.ppermute(x, axis, [(i, i ^ offset) for i in range(size)])


def per_device(tiles, tile_seg, tile_count, src_index, src_coef, obs_weight, att_dir, src_dir, *, sky, tm):
    tile_total, row_count, cols = tiles.shape
    params, span = src_dir.shape
    seg_rows = att_dir.shape[0]
    folds = cols // LANES
    across = [*range(tm - 1, 2, -2)]
    me = lax.axis_index("tm").astype(jnp.int32).reshape(1)

    directions, index, coef, weight, seg, count = pl.pallas_call(
        pack_kernel,
        out_shape=(
            jax.ShapeDtypeStruct((params * (span // LANES) + folds * seg_rows, LANES), F32),
            jax.ShapeDtypeStruct(src_index.shape, src_index.dtype),
            jax.ShapeDtypeStruct(src_coef.shape, F32),
            jax.ShapeDtypeStruct(obs_weight.shape, F32),
            jax.ShapeDtypeStruct((1, tile_total), jnp.int32),
            jax.ShapeDtypeStruct((1, tile_total), jnp.int32),
        ),
        in_specs=[HBM] * 7,
        out_specs=(VMEM,) * 6,
        scratch_shapes=[pltpu.VMEM((params, span), F32), pltpu.SemaphoreType.DMA((6 + folds,))],
        compiler_params=PARAMS,
        name="pack",
    )(*map(in_hbm, (src_dir, att_dir, src_index, src_coef, obs_weight, *(x.reshape(1, -1) for x in (tile_seg, tile_count)))))

    far = list(across[1:])
    tables = {0: directions}
    for offset in across:
        tables[offset] = swapped(directions, "tm", tm, offset)
    tables[1] = swapped(directions, "tm", tm, 1)

    def passed(offsets, after):
        return pl.pallas_call(
            functools.partial(pass_kernel, count=len(offsets)),
            out_shape=jax.ShapeDtypeStruct((len(offsets), *directions.shape), F32),
            in_specs=[VMEM] * (len(offsets) + 1),
            out_specs=VMEM,
            compiler_params=PARAMS,
            name="pass",
        )(*[tables[o] for o in offsets], after)

    slots = 2 * tile_total
    share = slots // tm
    places = jax.ShapeDtypeStruct((slots, LANES), jnp.int32)
    by_owner = jax.ShapeDtypeStruct((tm * 8, LANES), jnp.int32)
    by_tile = jax.ShapeDtypeStruct(src_index.shape, jnp.int32)
    tile_at, lane_at, coef_at, source_at, block, column, coef_by, row_at, rank_at, *extra = pl.pallas_call(
        functools.partial(order_kernel, owners=tm, span=span, cap=share * LANES, seg_rows=seg_rows),
        out_shape=(
            places,
            places,
            jax.ShapeDtypeStruct((params, slots, LANES), F32),
            jax.ShapeDtypeStruct((slots, LANES), F32),
            by_owner,
            by_owner,
            jax.ShapeDtypeStruct((params, tm * 8, LANES), F32),
            by_tile,
            by_tile,
            jax.ShapeDtypeStruct(src_index.shape, F32),
            jax.ShapeDtypeStruct((tile_total, tm * seg_rows), F32),
            jax.ShapeDtypeStruct((tile_total, tm * CAP_TILES, LANES), F32),
            jax.ShapeDtypeStruct((tm * CAP_TILES, LANES), F32),
        ),
        in_specs=[SMEM] + [VMEM] * 4,
        out_specs=(VMEM,) * 13,
        scratch_shapes=[
            pltpu.VMEM((2 * slots, tile_total * LANES), BF16),
            pltpu.VMEM((LANES, tile_total * LANES), BF16),
        ],
        compiler_params=PARAMS,
        cost_estimate=cost(1.5),
        name="order",
    )(me, seg, count, index, coef)
    picked_shape = jax.ShapeDtypeStruct((tm * 8, LANES), F32)
    picked, tiles_held, pieces = pl.pallas_call(
        functools.partial(own_kernel, share=share),
        out_shape=(picked_shape, jax.ShapeDtypeStruct(tiles.shape, F32), jax.ShapeDtypeStruct((tile_total, 2 * row_count, cols), BF16)),
        in_specs=[SMEM] + [VMEM] * 4 + [HBM],
        out_specs=(VMEM,) * 3,
        scratch_shapes=[pltpu.SemaphoreType.DMA((4,))],
        compiler_params=PARAMS,
        cost_estimate=cost(1.6),
        name="own",
    )(me, directions, block, column, coef_by, in_hbm(tiles))

    def pick(offsets, before):
        return pl.pallas_call(
            functools.partial(pick_kernel, offsets=offsets, share=share),
            out_shape=picked_shape,
            in_specs=[SMEM] + [VMEM] * (len(offsets) + 4),
            out_specs=VMEM,
            compiler_params=PARAMS,
            cost_estimate=cost(0.4 * len(offsets)),
            name="pick",
        )(me, *[tables[o] for o in offsets], block, column, coef_by, before)

    first_pair = swapped(passed(across[:1], picked), "tm", tm, 1)
    tables[across[0] - 1] = first_pair[0]
    picked = pick(across[:1], picked)
    others = swapped(passed(far, picked), "tm", tm, 1)
    for q, offset in enumerate(far):
        tables[offset - 1] = others[q]
    picked = pick([1, across[0] - 1, *far], picked)
    late = [o - 1 for o in across[1:]]
    offsets = sorted(tables)
    grads_from = up8((params + 1) * share)
    depth = up8(grads_from + (folds + 1) * CAP_TILES + 1)
    projected, sent = pl.pallas_call(
        functools.partial(project_kernel, seg_rows=seg_rows, offsets=offsets, late=late),
        out_shape=(
            jax.ShapeDtypeStruct((tile_total, row_count), F32),
            jax.ShapeDtypeStruct((tm * depth, LANES), F32),
        ),
        in_specs=[SMEM] + [VMEM] * (17 + tm),
        out_specs=(VMEM, VMEM),
        scratch_shapes=[
            pltpu.VMEM((tm * seg_rows, folds * LANES), F32),
            pltpu.VMEM((tm * 8, LANES), F32),
        ],
        compiler_params=PARAMS,
        name="project",
    )(
        me,
        tiles_held,
        pieces,
        picked,
        weight,
        tile_at,
        lane_at,
        coef_at,
        source_at,
        block,
        column,
        coef_by,
        row_at,
        rank_at,
        *extra,
        *[tables[o] for o in offsets],
    )

    got = lax.all_to_all(sent.reshape(tm, depth, LANES), "tm", 0, 0).reshape(tm * depth, LANES)
    part_shape = jax.ShapeDtypeStruct((folds * seg_rows + 8, LANES), F32)
    part = pl.pallas_call(
        functools.partial(attitude_kernel, owners=tm, grads_from=grads_from, seg_rows=seg_rows, folds=folds),
        out_shape=part_shape,
        in_specs=[SMEM, VMEM],
        out_specs=VMEM,
        compiler_params=PARAMS,
        name="attitude",
    )(me, got)
    half = params * (span // WIDE)
    src_normal, projected, token = pl.pallas_call(
        functools.partial(source_kernel, owners=tm, share=share),
        out_shape=(
            jax.ShapeDtypeStruct((params, span), F32),
            jax.ShapeDtypeStruct((tile_total, row_count), F32),
            jax.ShapeDtypeStruct((8, LANES), F32),
        ),
        in_specs=[SMEM] + [VMEM] * 2,
        out_specs=(VMEM,) * 3,
        scratch_shapes=[
            pltpu.VMEM((2 * half, tile_total * LANES), BF16),
            pltpu.VMEM((WIDE, tile_total * LANES), BF16),
        ],
        compiler_params=PARAMS,
        cost_estimate=cost(2.0),
        name="source",
    )(me, got, projected)
    order = [*range(sky // 2, sky), *range(1, sky // 2)]
    others = [swapped(part, "sky", sky, offset) for offset in order]
    att_normal, curvature = pl.pallas_call(
        functools.partial(finish_kernel, seg_rows=seg_rows, folds=folds),
        out_shape=(
            jax.ShapeDtypeStruct((seg_rows, cols), F32),
            jax.ShapeDtypeStruct((1, 1), F32),
        ),
        in_specs=[VMEM] * (sky + 1),
        out_specs=(VMEM, SMEM),
        compiler_params=PARAMS,
        name="finish",
    )(part, *others, token)
    return projected, att_normal, src_normal, curvature.reshape(())


def solution(mesh):
    placed = (
        P(("sky", "tm"), None, None),
        P(("sky", "tm")),
        P(("sky", "tm")),
        P(("sky", "tm"), None),
        P(None, ("sky", "tm"), None),
        P(("sky", "tm"), None),
        P("tm", None),
        P(None, ("sky", "tm")),
    )
    return jax.shard_map(
        functools.partial(per_device, sky=mesh.shape["sky"], tm=mesh.shape["tm"]),
        mesh=mesh,
        in_specs=placed,
        out_specs=(P(("sky", "tm"), None), P("tm", None), P(None, ("sky", "tm")), P()),
        check_vma=False,
    )
```

```python
import functools

import jax
import jax.numpy as jnp
from jax import lax
from jax.experimental import pallas as pl
from jax.experimental.pallas import tpu as pltpu
from jax.sharding import PartitionSpec as P

LANES = 128
CAP_TILES = 4
WIDE = 256
NT = (((1,), (1,)), ((), ()))
F32 = jnp.float32
BF16 = jnp.bfloat16
VMEM = pl.BlockSpec(memory_space=pltpu.VMEM)
HBM = pl.BlockSpec(memory_space=pltpu.HBM)
SMEM = pl.BlockSpec(memory_space=pltpu.SMEM)
PARAMS = pltpu.CompilerParams(vmem_limit_bytes=16 * 1024 * 1024)


def up8(rows):
    return (rows + 7) // 8 * 8


def in_hbm(x):
    return pltpu.with_memory_space_constraint(x, pltpu.HBM)


def halves(x):
    high = x.astype(BF16)
    return high, (x - high.astype(F32)).astype(BF16)


def pack_kernel(source, attitude, *refs):
    small, (directions, *outs), (held, sems) = refs[:5], refs[5:11], refs[11:]
    params, span = source.shape
    seg_rows, cols = attitude.shape
    copies = [
        pltpu.make_async_copy(source, held, sems.at[0]),
        *[pltpu.make_async_copy(x, out, sems.at[1 + q]) for q, (x, out) in enumerate(zip(small, outs))],
    ]
    base = params * (span // LANES)
    for c in range(cols // LANES):
        copies.append(
            pltpu.make_async_copy(
                attitude.at[:, pl.ds(c * LANES, LANES)],
                directions.at[pl.ds(base + c * seg_rows, seg_rows), :],
                sems.at[6 + c],
            )
        )
    for copy in copies:
        copy.start()
    copies[0].wait()
    for b in range(span // LANES):
        directions[b * params : (b + 1) * params, :] = held[:, b * LANES : (b + 1) * LANES]
    for copy in copies[1:]:
        copy.wait()


def serve(owner, table, block, column, coef, total, share):
    params = coef.shape[0]
    blocks = (table.shape[0] // (params * 8)) * 8
    parts = 8 // share
    rows = pl.ds(pl.multiple_of(owner * 8, 8), 8)
    here, lane = block[rows, :], column[rows, :]
    part = lax.div(lax.broadcasted_iota(jnp.int32, here.shape, 0), share)
    picked = [jnp.zeros(here.shape, F32) for _ in range(params)]
    for b in range(blocks // parts):
        hit = here == b
        for k in range(params):
            line = None
            for p in range(parts):
                at = (p * (blocks // parts) + b) * params + k
                row = jnp.broadcast_to(table[at : at + 1, :], here.shape)
                line = row if line is None else jnp.where(part == p, row, line)
            picked[k] = jnp.where(hit, jnp.take_along_axis(line, lane, axis=1), picked[k])
    terms = jnp.zeros(here.shape, F32)
    for k in range(params):
        terms = terms + coef[k, rows, :] * picked[k]
    total[rows, :] = terms


def own_kernel(me, table, block, column, coef, tiles_in, total, tiles, pieces, sems, *, share):
    chunks = sems.shape[0]
    each = tiles.shape[0] // chunks
    copies = []
    for q in range(chunks):
        part = pl.ds(q * each, each)
        copies.append(pltpu.make_async_copy(tiles_in.at[part], tiles.at[part], sems.at[q]))
        copies[q].start()
    total[...] = jnp.zeros_like(total)
    serve(me[0], table, block, column, coef, total, share)
    for q in range(chunks):
        copies[q].wait()
        for t in range(q * each, (q + 1) * each):
            depth = tiles.shape[1]
            pieces[t, :depth, :], pieces[t, depth:, :] = halves(tiles[t])


def pick_kernel(*refs, offsets, share):
    me, *tables, block, column, coef, before, total = refs
    total[...] = before[...]
    for offset, table in zip(offsets, tables):
        serve(lax.bitwise_xor(me[0], offset), table, block, column, coef, total, share)


def pass_kernel(*refs, count):
    for q in range(count):
        refs[-1][q] = refs[q][...]


def order_kernel(me, seg, count, index, coef, *refs, owners, span, cap, seg_rows):
    tile_at, lane_at, coef_out, source_out, block, column, coef_by, row_at, rank_at, live, aim, fill, names, left, right = refs
    params, tile_total, _ = coef.shape
    slots = tile_at.shape[0]
    ids = index[...]
    owner = lax.div(ids, span)
    mask = jnp.concatenate([jnp.where(owner == o, 1.0, 0.0) for o in range(owners)], axis=0)
    rows = mask.shape[0]
    half = mask.astype(BF16)
    row_ids = lax.broadcasted_iota(jnp.int32, (LANES, LANES), 0)
    col_ids = lax.broadcasted_iota(jnp.int32, (LANES, LANES), 1)
    upper = jnp.where(row_ids < col_ids, 1.0, 0.0).astype(BF16)
    inside = jnp.dot(half, upper, preferred_element_type=F32)
    counts = jnp.dot(half, jnp.ones((LANES, LANES), BF16), preferred_element_type=F32)
    one = lax.broadcasted_iota(jnp.int32, (rows, rows), 0)
    two = lax.broadcasted_iota(jnp.int32, (rows, rows), 1)
    earlier = (lax.div(one, tile_total) == lax.div(two, tile_total)) & (two < one)
    earlier = jnp.where(earlier, 1.0, 0.0).astype(BF16)
    rank = inside + jnp.dot(earlier, counts.astype(BF16), preferred_element_type=F32)
    rank = mask * rank
    total = rank[:tile_total]
    for o in range(1, owners):
        total = total + rank[o * tile_total : (o + 1) * tile_total]
    place = total.astype(jnp.int32)
    row_at[...] = owner * 8 + lax.div(place, LANES)
    rank_at[...] = lax.rem(place, LANES)
    slot = owner * cap + place
    high = lax.div(slot, LANES).astype(F32)
    low = lax.rem(slot, LANES).astype(F32)
    high_ids = lax.broadcasted_iota(jnp.int32, (slots, LANES), 0).astype(BF16)
    low_ids = lax.broadcasted_iota(jnp.int32, (LANES, LANES), 0).astype(BF16)
    lanes = lax.broadcasted_iota(jnp.int32, (slots, LANES), 1).astype(BF16)
    unit, zero = jnp.ones((), BF16), jnp.zeros((), BF16)
    for t in range(tile_total):
        at = slice(t * LANES, (t + 1) * LANES)
        hit = high_ids == jnp.broadcast_to(high[t : t + 1], (slots, LANES)).astype(BF16)
        left[:slots, at] = jnp.where(hit, jnp.full((), t + 1, BF16), zero)
        left[slots:, at] = jnp.where(hit, lanes, zero)
        right[:, at] = jnp.where(
            low_ids == jnp.broadcast_to(low[t : t + 1], (LANES, LANES)).astype(BF16), unit, zero
        )
    place = lax.dot_general(left[...], right[...], NT, preferred_element_type=F32).astype(jnp.int32)
    tile, lane = place[:slots] - 1, place[slots:]
    tile_at[...] = tile
    lane_at[...] = lane
    ordered = [jnp.zeros((slots, LANES), F32) for _ in range(params)] + [jnp.full((slots, LANES), -1.0, F32)]
    for t in range(tile_total):
        hit = tile == t
        for k in range(params + 1):
            row = coef[k, t : t + 1, :] if k < params else ids[t : t + 1].astype(F32)
            found = jnp.take_along_axis(jnp.broadcast_to(row, (slots, LANES)), lane, axis=1)
            ordered[k] = jnp.where(hit, found, ordered[k])
    for k in range(params):
        coef_out[k] = ordered[k]
    source_out[...] = ordered[params]
    source = ordered[params].astype(jnp.int32)
    blocks, share = span // LANES, slots // owners
    parts = 8 // share
    within = jnp.where(source < 0, -blocks, lax.div(lax.rem(source, span), LANES))
    across = jnp.where(source < 0, 0, lax.rem(source, LANES))
    for o in range(owners):
        rows, mine = slice(o * 8, (o + 1) * 8), slice(o * share, (o + 1) * share)
        block[rows, :] = jnp.concatenate([within[mine] - p * (blocks // parts) for p in range(parts)], axis=0)
        column[rows, :] = jnp.concatenate([across[mine]] * parts, axis=0)
        for k in range(params):
            coef_by[k, rows, :] = jnp.concatenate([ordered[k][mine]] * parts, axis=0)
    square = (tile_total, tile_total)
    one = lax.broadcasted_iota(jnp.int32, square, 0)
    two = lax.broadcasted_iota(jnp.int32, square, 1)

    def down_of(row):
        return jnp.sum(jnp.where(one == two, jnp.broadcast_to(row, square), 0), axis=1, keepdims=True)

    along, down = seg[...], down_of(seg[...])
    owner_along, owner_down = lax.div(along, seg_rows), lax.div(down, seg_rows)
    live[...] = jnp.where(
        lax.broadcasted_iota(jnp.int32, ids.shape, 1) < jnp.broadcast_to(down_of(count[...]), ids.shape), 1.0, 0.0
    )
    line = lax.bitwise_xor(owner_down, me[0]) * seg_rows + lax.rem(down, seg_rows)
    aim[...] = jnp.where(
        lax.broadcasted_iota(jnp.int32, aim.shape, 1) == jnp.broadcast_to(line, aim.shape), 1.0, 0.0
    )
    same = jnp.broadcast_to(owner_down, square) == jnp.broadcast_to(owner_along, square)
    ranks = jnp.sum(jnp.where(same & (one < two), 1, 0), axis=0, keepdims=True)
    wide = (names.shape[0], tile_total)
    place = jnp.broadcast_to(owner_along * CAP_TILES + ranks, wide)
    filled = lax.broadcasted_iota(jnp.int32, wide, 0) == place
    ones = jnp.where(filled, 1.0, 0.0)
    for t in range(tile_total):
        fill[t] = jnp.broadcast_to(ones[:, t : t + 1], names.shape)
    named = jnp.sum(jnp.where(filled, jnp.broadcast_to(along + 1, wide), 0), axis=1, keepdims=True) - 1
    names[...] = jnp.broadcast_to(named, names.shape).astype(F32)


def project_kernel(*refs, seg_rows, offsets, late):
    me, tiles, pieces, before, weight, tile_at, lane_at, coef_at, source_at, *refs = refs
    block, column, coef_by, row_at, rank_at, live, aim, fill, names, *refs = refs
    tables, refs = refs[: len(offsets)], refs[len(offsets) :]
    projected, sent, lines, served = refs
    params, tile_total, width = coef_at.shape[0], *weight.shape
    share = tile_at.shape[0] // len(offsets)
    folds = tiles.shape[2] // LANES
    base = tables[0].shape[0] - folds * seg_rows
    served[...] = before[...]
    for offset, table in zip(offsets, tables):
        for c in range(folds):
            lines[offset * seg_rows : (offset + 1) * seg_rows, c * LANES : (c + 1) * LANES] = table[
                base + c * seg_rows : base + (c + 1) * seg_rows, :
            ]
        if offset in late:
            serve(lax.bitwise_xor(me[0], offset), table, block, column, coef_by, served, share)
    shape = weight.shape
    row, rank = row_at[...], rank_at[...]
    total = jnp.zeros(shape, F32)
    for o in range(len(offsets)):
        for h in range(share):
            line = served[o * 8 + h : o * 8 + h + 1, :]
            for p in range(1, 8 // share):
                at = o * 8 + p * share + h
                line = line + served[at : at + 1, :]
            found = jnp.take_along_axis(jnp.broadcast_to(line, shape), rank, axis=1)
            total = jnp.where(row == o * 8 + h, found, total)
    hit = aim[...].astype(BF16)
    directions = jnp.zeros((tile_total, folds * LANES), F32)
    for piece in halves(lines[...]):
        directions = directions + jnp.dot(hit, piece, preferred_element_type=F32)
    row_ids = lax.broadcasted_iota(jnp.int32, shape, 0)
    tile_part = jnp.zeros(shape, F32)
    for t in range(tile_total):
        folded = None
        for c in range(folds):
            part = slice(c * LANES, (c + 1) * LANES)
            product = tiles[t, :, part] * directions[t : t + 1, part]
            folded = product if folded is None else folded + product
        tile_part = jnp.where(row_ids == t, jnp.sum(folded.T, axis=0, keepdims=True), tile_part)
    total = total + tile_part
    value = jnp.where(live[...] > 0.5, total, 0.0)
    weighted = weight[...] * value
    projected[...] = value
    owners = len(offsets)
    slots = tile_at.shape[0]
    depth = sent.shape[0] // owners
    tile, lane = tile_at[...], lane_at[...]
    ordered = jnp.zeros(tile.shape, F32)
    for t in range(tile_total):
        row = jnp.broadcast_to(weighted[t : t + 1], tile.shape)
        ordered = jnp.where(tile == t, jnp.take_along_axis(row, lane, axis=1), ordered)
    grads_from = up8((params + 1) * share)
    names_from = grads_from + folds * CAP_TILES
    curve = jnp.sum(value * weighted, axis=0, keepdims=True)
    for k in range(params + 1):
        values = coef_at[k] * ordered if k < params else source_at[...]
        for o in range(owners):
            sent[pl.ds(o * depth + k * share, share), :] = values[o * share : (o + 1) * share]
    high, low = (x.astype(F32) for x in halves(weighted))
    places = fill.shape[1]
    nothing = jnp.zeros((places, LANES), BF16)
    sums = jnp.zeros((2 * places, folds * LANES), F32)
    for t in range(tile_total):
        mask = fill[t]
        one = (mask * high[t : t + 1]).astype(BF16)
        two = (mask * low[t : t + 1]).astype(BF16)
        left = jnp.concatenate(
            [jnp.concatenate([one, one], axis=1), jnp.concatenate([two, nothing], axis=1)], axis=0
        )
        sums = sums + jnp.dot(left, pieces[t], preferred_element_type=F32)
    placed = sums[:places] + sums[places:]
    for o in range(owners):
        rows = slice(o * CAP_TILES, (o + 1) * CAP_TILES)
        for c in range(folds):
            sent[pl.ds(o * depth + grads_from + c * CAP_TILES, CAP_TILES), :] = placed[rows, c * LANES : (c + 1) * LANES]
        sent[pl.ds(o * depth + names_from, CAP_TILES), :] = names[rows, :]
        sent[pl.ds(o * depth + names_from + CAP_TILES, 1), :] = curve


def attitude_kernel(me, got, part, *, owners, grads_from, seg_rows, folds):
    depth = got.shape[0] // owners
    names_from = grads_from + folds * CAP_TILES
    lane = lax.broadcasted_iota(jnp.int32, (owners, LANES), 1)
    first = me[0] * seg_rows
    hits, grads = [], [[] for _ in range(folds)]
    for r in range(CAP_TILES):
        name = got[pl.ds(names_from + r, owners, stride=depth), :].astype(jnp.int32)
        hits.append(jnp.where(name - first == lane, 1.0, 0.0))
        for c in range(folds):
            grads[c].append(got[pl.ds(grads_from + c * CAP_TILES + r, owners, stride=depth), :])
    pick = jnp.concatenate(hits, axis=0).T[:seg_rows].astype(BF16)
    for c in range(folds):
        total = jnp.zeros((seg_rows, LANES), F32)
        for piece in halves(jnp.concatenate(grads[c], axis=0)):
            total = total + jnp.dot(pick, piece, preferred_element_type=F32)
        part[pl.ds(c * seg_rows, seg_rows), :] = total
    curve = got[pl.ds(names_from + CAP_TILES, owners, stride=depth), :]
    whole = jnp.sum(jnp.sum(curve, axis=0, keepdims=True), axis=1, keepdims=True)
    part[pl.ds(folds * seg_rows, 8), :] = jnp.broadcast_to(whole, (8, LANES))


def source_kernel(me, got, held, out, kept, token, left, right, *, owners, share):
    params, span = out.shape
    depth = got.shape[0] // owners
    kept[...] = held[...]
    token[...] = jnp.zeros_like(token)
    high_total = span // WIDE
    high_ids = lax.broadcasted_iota(jnp.int32, (high_total, LANES), 0).astype(BF16)
    low_ids = lax.broadcasted_iota(jnp.int32, (WIDE, LANES), 0).astype(BF16)
    one, zero = jnp.ones((), BF16), jnp.zeros((), BF16)
    half = params * high_total
    group = right.shape[1] // LANES
    places = [o * depth + h for o in range(owners) for h in range(share)]
    total = jnp.zeros((2 * half, WIDE), F32)
    for g in range(0, len(places), group):
        for t, place in enumerate(places[g : g + group]):
            at = slice(t * LANES, (t + 1) * LANES)
            rows = [got[place + k * share : place + k * share + 1, :] for k in range(params + 1)]
            local = rows[params].astype(jnp.int32) - me[0] * span
            high = lax.shift_right_arithmetic(local, 8)
            high = jnp.where((high >= 0) & (high < high_total), high, high_total).astype(F32)
            low = lax.bitwise_and(local, WIDE - 1).astype(F32)
            low = jnp.broadcast_to(low, (WIDE, LANES)).astype(BF16)
            right[:, at] = jnp.where(low_ids == low, one, zero)
            hit = high_ids == jnp.broadcast_to(high, (high_total, LANES)).astype(BF16)
            for k in range(params):
                for p, piece in enumerate(halves(jnp.broadcast_to(rows[k], (high_total, LANES)))):
                    row = p * half + k * high_total
                    left[row : row + high_total, at] = jnp.where(hit, piece, zero)
        total = total + lax.dot_general(left[...], right[...], NT, preferred_element_type=F32)
    for k in range(params):
        for h in range(high_total):
            row = k * high_total + h
            out[k : k + 1, h * WIDE : (h + 1) * WIDE] = total[row : row + 1, :] + total[half + row : half + row + 1, :]


def finish_kernel(*refs, seg_rows, folds):
    *parts, _, normal, curvature = refs
    total = parts[0][...]
    for part in parts[1:]:
        total = total + part[...]
    for c in range(folds):
        normal[:, c * LANES : (c + 1) * LANES] = total[c * seg_rows : (c + 1) * seg_rows]
    curvature[0, 0] = total[folds * seg_rows, 0]


def cost(microseconds):
    return pl.CostEstimate(flops=int(microseconds * 1e9), bytes_accessed=1, transcendentals=0)


def swapped(x, axis, size, offset):
    return lax.ppermute(x, axis, [(i, i ^ offset) for i in range(size)])


def per_device(tiles, tile_seg, tile_count, src_index, src_coef, obs_weight, att_dir, src_dir, *, sky, tm):
    tile_total, row_count, cols = tiles.shape
    params, span = src_dir.shape
    seg_rows = att_dir.shape[0]
    folds = cols // LANES
    across = [*range(tm - 1, 2, -2)]
    me = lax.axis_index("tm").astype(jnp.int32).reshape(1)

    directions, index, coef, weight, seg, count = pl.pallas_call(
        pack_kernel,
        out_shape=(
            jax.ShapeDtypeStruct((params * (span // LANES) + folds * seg_rows, LANES), F32),
            jax.ShapeDtypeStruct(src_index.shape, src_index.dtype),
            jax.ShapeDtypeStruct(src_coef.shape, F32),
            jax.ShapeDtypeStruct(obs_weight.shape, F32),
            jax.ShapeDtypeStruct((1, tile_total), jnp.int32),
            jax.ShapeDtypeStruct((1, tile_total), jnp.int32),
        ),
        in_specs=[HBM] * 7,
        out_specs=(VMEM,) * 6,
        scratch_shapes=[pltpu.VMEM((params, span), F32), pltpu.SemaphoreType.DMA((6 + folds,))],
        compiler_params=PARAMS,
        name="pack",
    )(*map(in_hbm, (src_dir, att_dir, src_index, src_coef, obs_weight, *(x.reshape(1, -1) for x in (tile_seg, tile_count)))))

    far = list(across[1:])
    tables = {0: directions}
    for offset in across:
        tables[offset] = swapped(directions, "tm", tm, offset)
    tables[1] = swapped(directions, "tm", tm, 1)

    def passed(offsets, after):
        return pl.pallas_call(
            functools.partial(pass_kernel, count=len(offsets)),
            out_shape=jax.ShapeDtypeStruct((len(offsets), *directions.shape), F32),
            in_specs=[VMEM] * (len(offsets) + 1),
            out_specs=VMEM,
            compiler_params=PARAMS,
            name="pass",
        )(*[tables[o] for o in offsets], after)

    slots = 2 * tile_total
    share = slots // tm
    places = jax.ShapeDtypeStruct((slots, LANES), jnp.int32)
    by_owner = jax.ShapeDtypeStruct((tm * 8, LANES), jnp.int32)
    by_tile = jax.ShapeDtypeStruct(src_index.shape, jnp.int32)
    tile_at, lane_at, coef_at, source_at, block, column, coef_by, row_at, rank_at, *extra = pl.pallas_call(
        functools.partial(order_kernel, owners=tm, span=span, cap=share * LANES, seg_rows=seg_rows),
        out_shape=(
            places,
            places,
            jax.ShapeDtypeStruct((params, slots, LANES), F32),
            jax.ShapeDtypeStruct((slots, LANES), F32),
            by_owner,
            by_owner,
            jax.ShapeDtypeStruct((params, tm * 8, LANES), F32),
            by_tile,
            by_tile,
            jax.ShapeDtypeStruct(src_index.shape, F32),
            jax.ShapeDtypeStruct((tile_total, tm * seg_rows), F32),
            jax.ShapeDtypeStruct((tile_total, tm * CAP_TILES, LANES), F32),
            jax.ShapeDtypeStruct((tm * CAP_TILES, LANES), F32),
        ),
        in_specs=[SMEM] + [VMEM] * 4,
        out_specs=(VMEM,) * 13,
        scratch_shapes=[
            pltpu.VMEM((2 * slots, tile_total * LANES), BF16),
            pltpu.VMEM((LANES, tile_total * LANES), BF16),
        ],
        compiler_params=PARAMS,
        cost_estimate=cost(1.5),
        name="order",
    )(me, seg, count, index, coef)
    picked_shape = jax.ShapeDtypeStruct((tm * 8, LANES), F32)
    picked, tiles_held, pieces = pl.pallas_call(
        functools.partial(own_kernel, share=share),
        out_shape=(picked_shape, jax.ShapeDtypeStruct(tiles.shape, F32), jax.ShapeDtypeStruct((tile_total, 2 * row_count, cols), BF16)),
        in_specs=[SMEM] + [VMEM] * 4 + [HBM],
        out_specs=(VMEM,) * 3,
        scratch_shapes=[pltpu.SemaphoreType.DMA((8,))],
        compiler_params=PARAMS,
        cost_estimate=cost(1.6),
        name="own",
    )(me, directions, block, column, coef_by, in_hbm(tiles))

    def pick(offsets, before):
        return pl.pallas_call(
            functools.partial(pick_kernel, offsets=offsets, share=share),
            out_shape=picked_shape,
            in_specs=[SMEM] + [VMEM] * (len(offsets) + 4),
            out_specs=VMEM,
            compiler_params=PARAMS,
            cost_estimate=cost(0.4 * len(offsets)),
            name="pick",
        )(me, *[tables[o] for o in offsets], block, column, coef_by, before)

    first_pair = swapped(passed(across[:1], picked), "tm", tm, 1)
    tables[across[0] - 1] = first_pair[0]
    picked = pick(across[:1], picked)
    others = swapped(passed(far, picked), "tm", tm, 1)
    for q, offset in enumerate(far):
        tables[offset - 1] = others[q]
    picked = pick([1, across[0] - 1, *far], picked)
    late = [o - 1 for o in across[1:]]
    offsets = sorted(tables)
    grads_from = up8((params + 1) * share)
    depth = up8(grads_from + (folds + 1) * CAP_TILES + 1)
    projected, sent = pl.pallas_call(
        functools.partial(project_kernel, seg_rows=seg_rows, offsets=offsets, late=late),
        out_shape=(
            jax.ShapeDtypeStruct((tile_total, row_count), F32),
            jax.ShapeDtypeStruct((tm * depth, LANES), F32),
        ),
        in_specs=[SMEM] + [VMEM] * (17 + tm),
        out_specs=(VMEM, VMEM),
        scratch_shapes=[
            pltpu.VMEM((tm * seg_rows, folds * LANES), F32),
            pltpu.VMEM((tm * 8, LANES), F32),
        ],
        compiler_params=PARAMS,
        name="project",
    )(
        me,
        tiles_held,
        pieces,
        picked,
        weight,
        tile_at,
        lane_at,
        coef_at,
        source_at,
        block,
        column,
        coef_by,
        row_at,
        rank_at,
        *extra,
        *[tables[o] for o in offsets],
    )

    got = lax.all_to_all(sent.reshape(tm, depth, LANES), "tm", 0, 0).reshape(tm * depth, LANES)
    part_shape = jax.ShapeDtypeStruct((folds * seg_rows + 8, LANES), F32)
    part = pl.pallas_call(
        functools.partial(attitude_kernel, owners=tm, grads_from=grads_from, seg_rows=seg_rows, folds=folds),
        out_shape=part_shape,
        in_specs=[SMEM, VMEM],
        out_specs=VMEM,
        compiler_params=PARAMS,
        name="attitude",
    )(me, got)
    half = params * (span // WIDE)
    src_normal, projected, token = pl.pallas_call(
        functools.partial(source_kernel, owners=tm, share=share),
        out_shape=(
            jax.ShapeDtypeStruct((params, span), F32),
            jax.ShapeDtypeStruct((tile_total, row_count), F32),
            jax.ShapeDtypeStruct((8, LANES), F32),
        ),
        in_specs=[SMEM] + [VMEM] * 2,
        out_specs=(VMEM,) * 3,
        scratch_shapes=[
            pltpu.VMEM((2 * half, tile_total * LANES), BF16),
            pltpu.VMEM((WIDE, tile_total * LANES), BF16),
        ],
        compiler_params=PARAMS,
        cost_estimate=cost(2.0),
        name="source",
    )(me, got, projected)
    order = [*range(sky // 2, sky), *range(1, sky // 2)]
    others = [swapped(part, "sky", sky, offset) for offset in order]
    att_normal, curvature = pl.pallas_call(
        functools.partial(finish_kernel, seg_rows=seg_rows, folds=folds),
        out_shape=(
            jax.ShapeDtypeStruct((seg_rows, cols), F32),
            jax.ShapeDtypeStruct((1, 1), F32),
        ),
        in_specs=[VMEM] * (sky + 1),
        out_specs=(VMEM, SMEM),
        compiler_params=PARAMS,
        name="finish",
    )(part, *others, token)
    return projected, att_normal, src_normal, curvature.reshape(())


def solution(mesh):
    placed = (
        P(("sky", "tm"), None, None),
        P(("sky", "tm")),
        P(("sky", "tm")),
        P(("sky", "tm"), None),
        P(None, ("sky", "tm"), None),
        P(("sky", "tm"), None),
        P("tm", None),
        P(None, ("sky", "tm")),
    )
    return jax.shard_map(
        functools.partial(per_device, sky=mesh.shape["sky"], tm=mesh.shape["tm"]),
        mesh=mesh,
        in_specs=placed,
        out_specs=(P(("sky", "tm"), None), P("tm", None), P(None, ("sky", "tm")), P()),
        check_vma=False,
    )
```
